32 devices in a mesh: dp: 8 (over z, core), tensor: 4 (over y, x).
Axes of the slice: x: 2, y: 2, z: 4, core: 2. Of those that a mesh axis runs over, the one named last changes fastest.
Arguments:
- layer_input: bfloat16 [16, 1024, 2048], P('dp', 'tensor'), may hold values from -6 to 6
- segments: int32 [16, 1024], P('dp'), may hold values from 0 to 4, as said below
- query_key_value_weight: bfloat16 [3, 2048, 2048], P(None, 'dp', 'tensor'), may hold values from -0.125 to 0.125
- output_weight: bfloat16 [2048, 2048], P('tensor', 'dp'), may hold values from -0.5 to 0.5
- norm1_gain: bfloat16 [2048], P('dp'), may hold values from 0.25 to 1.75
- gate_up_weight: bfloat16 [2, 2048, 8192], P(None, 'dp', 'tensor'), may hold values from -0.125 to 0.125
- down_weight: bfloat16 [8192, 2048], P('tensor', 'dp'), may hold values from -0.125 to 0.125
- norm2_gain: bfloat16 [2048], P('dp'), may hold values from 0.25 to 1.75
- grad_out: bfloat16 [16, 1024, 2048], P('dp', 'tensor'), may hold values from -6 to 6
Outputs:
- layer_out: bfloat16 [16, 1024, 2048], P('dp', 'tensor')
- grad_input: bfloat16 [16, 1024, 2048], P('dp', 'tensor')
- grad_qkv: float32 [3, 2048, 2048], P(None, 'dp', 'tensor')
- grad_wout: float32 [2048, 2048], P('tensor', 'dp')
- grad_gain1: float32 [2048], P('dp')
- grad_gateup: float32 [2, 2048, 8192], P(None, 'dp', 'tensor')
- grad_wdown: float32 [8192, 2048], P('tensor', 'dp')
- grad_gain2: float32 [2048], P('dp')
The draws below stay inside these ranges and needn't reach their ends.
Inputs may be any that keep to these rules, and one draw needn't show every extreme that they name: `segments`: in every row the ids start at 0 and never fall; in every row one segment covers positions 64 to 959.
All inputs are finite; a program needn't handle non-finite values.
Results may differ from the reference program's by a relative error of at most 0.025.
Values may be sent and summed in bfloat16 or wider, within the bound.
A program may use at most 320 MiB of HBM per device.

```python
import jax
import jax.numpy as jnp
from jax import lax

D = 2048
HEADS = 32
HEAD_DIM = 64
FF = 8192
SEQ_LEN = 1024
SEQS_GRP = 2
NSEQ = 16


def draw_segments(key, part):
    key = jax.random.fold_in(key, 7)
    keys_four = jax.random.split(key, 4)
    edge_len = SEQ_LEN // 16
    shape_col = (NSEQ, 1)
    first_cut = jax.random.randint(keys_four[0], shape_col, 1, edge_len + 1)
    early_cut = jax.random.randint(keys_four[1], shape_col, 1, edge_len + 1)
    late_cut = jax.random.randint(keys_four[2], shape_col, SEQ_LEN - edge_len, SEQ_LEN)
    last_cut = jax.random.randint(keys_four[3], shape_col, SEQ_LEN - edge_len, SEQ_LEN)
    position_ids = jnp.arange(SEQ_LEN, dtype=jnp.int32)[None, :]
    seg_ids = (position_ids >= first_cut).astype(jnp.int32) + (position_ids >= early_cut).astype(jnp.int32)
    seg_ids = seg_ids + (position_ids >= late_cut).astype(jnp.int32) + (position_ids >= last_cut).astype(jnp.int32)
    return seg_ids.astype(jnp.int32)


def shard_levels(key, dims, cuts, smallest, top_value):
    def one(dim, shards_of):
        heights = jax.random.uniform(jax.random.fold_in(jax.random.fold_in(key, 6), dim), (shards_of,), jnp.float32, smallest / len(cuts), top_value / len(cuts))
        return jnp.repeat(jnp.exp(heights), dims[dim] // shards_of).reshape((-1,) + (1,) * (len(dims) - dim - 1))

    level = one(*cuts[0])
    for cut in cuts[1:]:
        level = level * one(*cut)
    return level


def noise(stream_key, extent, deviation, most, shards=(), kind=jnp.bfloat16):
    values = jax.random.normal(stream_key, extent, jnp.float32) * deviation
    if len(shards) > 0:
        values = shard_levels(stream_key, extent, shards, -0.22, 0.18) * values
    return jnp.clip(values, min=-most, max=most).astype(kind)


def setup_inputs(seed: int = 0) -> dict:
    streams_of = jax.random.split(jax.random.key(seed), 10)
    return {
        "layer_input": noise(streams_of[0], (NSEQ, SEQ_LEN, D), 1.0, 6.0, ((0, 8), (1, 4))),
        "segments": draw_segments(jax.random.fold_in(streams_of[9], 71), 0),
        "query_key_value_weight": noise(streams_of[2], (3, D, D), D ** -0.5, 0.125, ((1, 8), (2, 4))),
        "output_weight": noise(streams_of[3], (D, D), (D // 16) ** -0.5, 0.5, ((0, 4), (1, 8))),
        "norm1_gain": jnp.clip(1.0 + 0.15 * jax.random.normal(streams_of[4], (D,), jnp.float32), 0.25, 1.75).astype(jnp.bfloat16),
        "gate_up_weight": noise(streams_of[5], (2, D, FF), D ** -0.5, 0.125, ((1, 8), (2, 4))),
        "down_weight": noise(streams_of[6], (FF, D), (FF // 4) ** -0.5, 0.125, ((0, 4), (1, 8))),
        "norm2_gain": jnp.clip(1.0 + 0.15 * jax.random.normal(streams_of[7], (D,), jnp.float32), 0.25, 1.75).astype(jnp.bfloat16),
        "grad_out": noise(streams_of[8], (NSEQ, SEQ_LEN, D), 1.0, 6.0, ((0, 8), (1, 4))),
    }


NORM_EPS = 1e-05
ROPE_BASE = 130000.0
MASKED_SCORE = -1e+30

@jax.custom_vjp
def low(v):
    return lax.optimization_barrier(v.astype(jnp.bfloat16)).astype(jnp.float32)

@jax.custom_vjp
def lowered_backward(v):
    return v

def low_keep(v):
    return (low(v), None)

def low_pass(kept, grad):
    return (grad,)

def back_keep(v):
    return (v, None)

def back_low(kept, grad):
    return (low(grad),)
low.defvjp(low_keep, low_pass)
lowered_backward.defvjp(back_keep, back_low)

def positions(segments):
    row_len = segments.shape[-1]
    position_ids = jnp.arange(row_len, dtype=jnp.int32)
    change = jnp.concatenate([jnp.ones_like(segments[:, :1]), (segments[:, 1:] != segments[:, :-1]).astype(jnp.int32)], axis=1)
    doc_start = lax.cummax(jnp.where(change > 0, position_ids[None, :], 0), axis=1)
    return position_ids[None, :] - doc_start

def rotary(segments):
    doc_pos = positions(segments).astype(jnp.float32)
    half_dim = HEAD_DIM // 2
    inv_freq = ROPE_BASE ** (-jnp.arange(half_dim, dtype=jnp.float32) * 2.0 / HEAD_DIM)
    angles = doc_pos[..., None] * inv_freq
    cos_table = jnp.concatenate([jnp.cos(angles), jnp.cos(angles)], axis=-1)
    sin_table = jnp.concatenate([jnp.sin(angles), jnp.sin(angles)], axis=-1)
    return (cos_table[:, :, None, :], sin_table[:, :, None, :])

def rotate(vectors, cos_table, sin_table):
    half_dim = vectors.shape[-1] // 2
    turned = jnp.concatenate([-vectors[..., half_dim:], vectors[..., :half_dim]], axis=-1)
    return vectors * cos_table + turned * sin_table

def rms_norm(vectors, gain_vec):
    return vectors * lax.rsqrt(lax.optimization_barrier(jnp.mean(vectors * vectors, axis=-1, keepdims=True)) + NORM_EPS) * gain_vec

def block_mask(segments, seq_id, row_start, block_rows):
    all_seg = lax.dynamic_index_in_dim(segments, seq_id, 0, False)
    row_seg = lax.dynamic_slice_in_dim(all_seg, row_start, block_rows, 0)
    row_ids = row_start + jnp.arange(block_rows, dtype=jnp.int32)
    col_ids = jnp.arange(all_seg.shape[0], dtype=jnp.int32)
    return (row_seg[:, None] == all_seg[None, :]) & (row_ids[:, None] >= col_ids[None, :])

def attend(queries, key_rows, values, segments):
    seq_count = queries.shape[0]
    block_rows = min(512, SEQ_LEN)
    blocks = SEQ_LEN // block_rows
    score_scale = HEAD_DIM ** (-0.5)

    def one_block(block_index):
        seq_id = block_index // blocks
        row_start = block_index % blocks * block_rows
        query_block = lax.dynamic_slice_in_dim(lax.dynamic_index_in_dim(queries, seq_id, 0, False), row_start, block_rows, 0)
        key_seq = lax.dynamic_index_in_dim(key_rows, seq_id, 0, False)
        value_seq = lax.dynamic_index_in_dim(values, seq_id, 0, False)
        allowed = block_mask(segments, seq_id, row_start, block_rows)
        scores = lowered_backward(jnp.einsum('qhe,khe->hqk', query_block, key_seq, precision=lax.Precision.HIGHEST) * score_scale)
        scores = jnp.where(allowed[None], scores, MASKED_SCORE)
        attn_probs = jax.nn.softmax(scores, axis=-1)
        return jnp.einsum('hqk,khe->qhe', low(attn_probs), value_seq, precision=lax.Precision.HIGHEST)
    outcome = lax.map(jax.checkpoint(one_block), jnp.arange(seq_count * blocks, dtype=jnp.int32))
    return outcome.reshape(seq_count, SEQ_LEN, HEADS, HEAD_DIM)

def forward_group(input_tokens, segments, cos_table, sin_table, query_key_value_weight, output_weight, gain_one, gate_up_weight, down_weight, gain_two):
    seq_count = input_tokens.shape[0]
    first_normed = low(rms_norm(input_tokens, gain_one))
    projected_output = lowered_backward(jnp.einsum('bqi,oix->obqx', first_normed, query_key_value_weight, precision=lax.Precision.HIGHEST))
    split_heads = projected_output.reshape(3, seq_count, SEQ_LEN, HEADS, HEAD_DIM)
    queries = low(rotate(split_heads[0], cos_table, sin_table))
    key_rows = low(rotate(split_heads[1], cos_table, sin_table))
    values = low(split_heads[2])
    attended_context = low(lowered_backward(attend(queries, key_rows, values, segments))).reshape(seq_count, SEQ_LEN, D)
    middle_state = input_tokens + lowered_backward(jnp.einsum('tgy,yc->tgc', attended_context, output_weight, precision=lax.Precision.HIGHEST))
    second_normed = low(rms_norm(middle_state, gain_two))
    gate_up_output = lowered_backward(jnp.einsum('qjr,prt->pqjt', second_normed, gate_up_weight, precision=lax.Precision.HIGHEST))
    hidden_state = low(jax.nn.silu(gate_up_output[0]) * gate_up_output[1])
    return middle_state + jnp.einsum('muv,vw->muw', hidden_state, down_weight, precision=lax.Precision.HIGHEST)

def reference(layer_input, segments, query_key_value_weight, output_weight, norm1_gain, gate_up_weight, down_weight, norm2_gain, grad_out):
    params = tuple((weight.astype(jnp.float32) for weight in (query_key_value_weight, output_weight, norm1_gain, gate_up_weight, down_weight, norm2_gain)))
    groups = layer_input.shape[0] // SEQS_GRP
    input_tokens = layer_input.astype(jnp.float32).reshape(groups, SEQS_GRP, SEQ_LEN, D)
    upstream = grad_out.astype(jnp.float32).reshape(groups, SEQS_GRP, SEQ_LEN, D)
    seg_groups = segments.reshape(groups, SEQS_GRP, SEQ_LEN)

    def advance(totals, scan_item):
        input_block, grad_block, seg_block = scan_item
        cos_table, sin_table = rotary(seg_block)

        def one_layer(input_rows, weight_qkv, weight_out, gain_one, weight_gateup, weight_down, gain_two):
            return forward_group(input_rows, seg_block, cos_table, sin_table, weight_qkv, weight_out, gain_one, weight_gateup, weight_down, gain_two)
        result, pull_back = jax.vjp(one_layer, input_block, *params)
        grad_list = pull_back(grad_block)
        totals = tuple((running + update for running, update in zip(totals, grad_list[1:])))
        return (totals, (result, grad_list[0]))
    start_totals = tuple((jnp.zeros_like(weight) for weight in params))
    totals, (results, grad_inputs) = lax.scan(advance, start_totals, (input_tokens, upstream, seg_groups))
    shape_all = layer_input.shape
    return (results.reshape(shape_all).astype(jnp.bfloat16), grad_inputs.reshape(shape_all).astype(jnp.bfloat16), totals[0], totals[1], totals[2], totals[3], totals[4], totals[5])
```

```python
import functools

import jax
import jax.numpy as jnp
from jax import lax
from jax.experimental import pallas as pl
from jax.experimental.pallas import tpu as pltpu
from jax.sharding import PartitionSpec as P

HEAD_DIM = 64
HALF = HEAD_DIM // 2
PAIR = 2 * HEAD_DIM
NORM_EPS = 1e-05
ROPE_BASE = 130000.0
MASKED_SCORE = -1e30
BF = jnp.bfloat16
F32 = jnp.float32
VMEM_LIMIT = 60 * 1024 * 1024

NT = (((1,), (1,)), ((), ()))


def dot(a, b):
    return jnp.dot(a, b, preferred_element_type=F32)


def dot_nt(a, b):
    return lax.dot_general(a, b, NT, preferred_element_type=F32)


class Order:
    last = None


ANY = pl.BlockSpec(memory_space=pl.ANY)


def call(body, grid, in_specs, out_specs, out_shape, scratch=(), flops=0, nbytes=0, aliases=None, prefetch=0):
    first_extra = prefetch + len(in_specs)

    def run(*args):
        extra = [] if Order.last is None else [Order.last]

        def ordered_body(*refs):
            body(*refs[:first_extra], *refs[first_extra + len(extra) :])

        outs = pl.pallas_call(
            ordered_body,
            grid_spec=pltpu.PrefetchScalarGridSpec(
                num_scalar_prefetch=prefetch,
                grid=grid,
                in_specs=in_specs + [ANY] * len(extra),
                out_specs=out_specs,
                scratch_shapes=list(scratch),
            ),
            out_shape=out_shape,
            input_output_aliases=aliases or {},
            cost_estimate=pl.CostEstimate(flops=flops, bytes_accessed=nbytes, transcendentals=0),
            compiler_params=pltpu.CompilerParams(vmem_limit_bytes=VMEM_LIMIT),
        )(*args, *extra)
        Order.last = outs[-1] if isinstance(outs, (list, tuple)) else outs
        return outs

    return run


def whole_spec(shape, buffers=1):
    zeros = (0,) * len(shape)
    return pl.BlockSpec(shape, lambda *_: zeros, pipeline_mode=pl.Buffered(buffers))


def sds(shape, dtype):
    return jax.ShapeDtypeStruct(shape, dtype)


def swap_perm(count, bit):
    return [(i, i ^ bit) for i in range(count)]


def gather_pieces(block, nt):
    if nt != 4:
        full = lax.all_gather(block, "tensor", axis=0, tiled=False)
        return [(full[r],) for r in range(nt)]
    half = block.shape[1] // 2
    from_x = lax.ppermute(block, "tensor", swap_perm(4, 1))
    from_y = lax.ppermute(block, "tensor", swap_perm(4, 2))
    diag_x = lax.ppermute(from_y[:, :half], "tensor", swap_perm(4, 1))
    diag_y = lax.ppermute(from_x[:, half:], "tensor", swap_perm(4, 2))
    return [(block,), (from_x,), (from_y,), (diag_x, diag_y)]


def add_half_kernel(base_ref, part_ref, out_ref):
    out_ref[...] = (base_ref[...].astype(F32) + part_ref[...].astype(F32)).astype(BF)


def add_half(base, part, which):
    rows, width = base.shape
    half = width // 2
    tile = min(256, rows)
    return call(
        add_half_kernel,
        (rows // tile,),
        [
            pl.BlockSpec((tile, half), lambda i: (i, which)),
            pl.BlockSpec((tile, half), lambda i: (i, 0)),
        ],
        pl.BlockSpec((tile, half), lambda i: (i, which)),
        sds(base.shape, BF),
        nbytes=rows * half * 6,
        aliases={0: 0},
    )(base, part)


class Scatter:
    def __init__(self, parts, nt):
        self.nt = nt
        if nt != 4:
            full = jnp.stack([p[0] for p in parts])
            self.terms = [lax.psum_scatter(full, "tensor", scatter_dimension=0, tiled=False)]
            return
        (self.own,), (self.to_x,), (self.to_y,), (diag_x, diag_y) = parts
        self.for_y = lax.ppermute(diag_x, "tensor", swap_perm(4, 1))
        self.for_x = lax.ppermute(diag_y, "tensor", swap_perm(4, 2))

    def second(self):
        if self.nt != 4:
            return
        to_y = add_half(self.to_y, self.for_y, 0)
        to_x = add_half(self.to_x, self.for_x, 1)
        self.terms = [
            self.own,
            lax.ppermute(to_x, "tensor", swap_perm(4, 1)),
            lax.ppermute(to_y, "tensor", swap_perm(4, 2)),
        ]


def piece_shapes(nt, rows, width):
    if nt != 4:
        return [((rows, width),)] * nt
    return [((rows, width),)] * 3 + [((rows, width // 2),) * 2]


def flat(pieces):
    return [a for p in pieces for a in p]


def regroup(items, nt):
    if nt != 4:
        return [(a,) for a in items]
    return [(items[0],), (items[1],), (items[2],), (items[3], items[4])]


def fill_from_pieces(refs, full_ref, nt):
    for slot, part in enumerate(regroup(refs, nt)):
        if len(part) == 1:
            full_ref[slot] = part[0][...]
        else:
            half = part[0].shape[1]
            full_ref[slot, :, :half] = part[0][...]
            full_ref[slot, :, half:] = part[1][...]


def out_piece_specs(nt, rows, width, step):
    specs = []
    half_steps = width // step // 2
    for part in piece_shapes(nt, rows, width):
        if len(part) == 1:
            specs.append(pl.BlockSpec((rows, step), lambda j: (0, j)))
        else:
            specs.append(pl.BlockSpec((rows, step), lambda j: (0, jnp.minimum(j, half_steps - 1))))
            specs.append(pl.BlockSpec((rows, step), lambda j: (0, jnp.maximum(j - half_steps, 0))))
    return specs


def store_piece(outs, nt, slot, steps, value):
    part = regroup(outs, nt)[slot]
    if len(part) == 1:
        part[0][...] = value.astype(BF)
    else:
        j = pl.program_id(0)

        @pl.when(j < steps // 2)
        def _():
            part[0][...] = value.astype(BF)

        @pl.when(j >= steps // 2)
        def _():
            part[1][...] = value.astype(BF)


def turn(v):
    lane = lax.broadcasted_iota(jnp.int32, v.shape, 1)
    return jnp.where(lane % HEAD_DIM < HALF, pltpu.roll(v, PAIR - HALF, 1), pltpu.roll(v, HALF, 1))


def rotate(v, cos, sin):
    return v * cos + turn(v) * sin


def unrotate(u, cos, sin):
    return u * cos + turn(u * sin)


def assemble_kernel(nt, normed, *refs):
    pieces, full_ref = refs[: -1 - normed], refs[-1]
    fill_from_pieces(pieces, full_ref, nt)
    if normed:
        gain = refs[-2][...]
        for slot in range(nt):
            x = full_ref[slot].astype(F32)
            scale = lax.rsqrt(jnp.mean(x * x, axis=-1, keepdims=True) + NORM_EPS)
            full_ref[slot] = (x * scale * gain).astype(BF)


def assemble(pieces, nt, gain=None):
    rows, width = pieces[0][0].shape
    tile = min(64, rows)
    items = flat(pieces)
    extra = [] if gain is None else [gain]
    return call(
        functools.partial(assemble_kernel, nt, len(extra)),
        (rows // tile,),
        [pl.BlockSpec((tile, a.shape[1]), lambda i: (i, 0)) for a in items]
        + [whole_spec(a.shape) for a in extra],
        pl.BlockSpec((nt, tile, width), lambda i: (0, i, 0)),
        sds((nt, rows, width), BF),
        nbytes=4 * nt * rows * width,
    )(*items, *extra)


def qkv_kernel(nt, a1_ref, w_ref, cos_ref, sin_ref, out_ref):
    cols = out_ref.shape[3]
    weight = w_ref[:, 0].reshape(-1, cols)

    @pl.when(pl.program_id(0) < 2)
    def _():
        for slot in range(nt):
            raw = dot(a1_ref[slot], weight)
            cos, sin = cos_ref[slot], sin_ref[slot]
            for p in range(cols // PAIR):
                part = slice(p * PAIR, (p + 1) * PAIR)
                out_ref[0, slot, :, part] = rotate(raw[:, part], cos, sin).astype(BF)

    @pl.when(pl.program_id(0) == 2)
    def _():
        for slot in range(nt):
            out_ref[0, slot] = dot(a1_ref[slot], weight).astype(BF)


def project_qkv(a1, weight, cos, sin, nt):
    nd, _, ds, hc = weight.shape
    _, rows, width = a1.shape
    return call(
        functools.partial(qkv_kernel, nt),
        (3,),
        [
            whole_spec(a1.shape),
            pl.BlockSpec((nd, 1, ds, hc), lambda c: (0, c, 0, 0)),
            whole_spec(cos.shape),
            whole_spec(sin.shape),
        ],
        pl.BlockSpec((1, nt, rows, hc), lambda c: (c, 0, 0, 0)),
        sds((3, nt, rows, hc), BF),
        flops=2 * nt * rows * width * hc * 3,
        nbytes=2 * (nt * rows * width + 3 * width * hc + 3 * nt * rows * hc),
    )(a1, weight, cos, sin)


def allowed_block(start, key_block, query_block, size):
    key_id = lax.broadcasted_iota(jnp.int32, (size, size), 0) + key_block * size
    ok = key_id >= start
    if key_block == query_block:
        ok &= lax.broadcasted_iota(jnp.int32, (size, size), 1) + query_block * size >= key_id
    return ok


def attn_fwd_kernel(nt, slot_ref, q_ref, k_ref, v_ref, start_ref, ctx_ref, lse_ref, vt_ref):
    size = q_ref.shape[1]
    for b in range(nt):
        vt_ref[b] = v_ref[slot_ref[b]].T
    lane = lax.broadcasted_iota(jnp.int32, (size, PAIR), 1)
    for p in range(nt):
        slot = slot_ref[p]
        q = q_ref[slot] * BF(HEAD_DIM**-0.5)
        start = start_ref[0, pl.ds(slot, 1), :]
        outs = []
        for h in range(2):
            qh = jnp.where((lane >= HEAD_DIM) == (h == 1), q, BF(0))
            scores = []
            for b in range(p + 1):
                s = dot_nt(k_ref[slot_ref[b]], qh)
                scores.append(jnp.where(allowed_block(start, b, p, size), s, MASKED_SCORE))
            top = functools.reduce(
                jnp.maximum, [jnp.max(s, axis=0, keepdims=True) for s in scores]
            )
            total = jnp.zeros((1, size), F32)
            acc = jnp.zeros((HEAD_DIM, size), F32)
            for b, s in enumerate(scores):
                e = jnp.exp(s - top)
                total += jnp.sum(e, axis=0, keepdims=True)
                acc += dot(vt_ref[b, h * HEAD_DIM : (h + 1) * HEAD_DIM, :], e.astype(BF))
            outs.append(acc / total)
            lse_ref[0, 0, pl.ds(2 * p + h, 1), :] = top + jnp.log(total)
        ctx_ref[slot] = jnp.concatenate(outs, axis=0).T.astype(BF)


def qkv_specs(nt, size):
    def spec(c):
        return pl.BlockSpec((None, nt, size, PAIR), lambda s, g, _: (c, 0, s, g))

    return [spec(c) for c in range(3)]


def attention_forward(qkv, start, slot_of, nt):
    _, _, rows, hc = qkv.shape
    seqs = start.shape[0]
    size = rows // seqs
    pairs = hc // PAIR
    blk = pl.BlockSpec((nt, size, PAIR), lambda s, g, _: (0, s, g))
    return call(
        functools.partial(attn_fwd_kernel, nt),
        (seqs, pairs),
        qkv_specs(nt, size) + [pl.BlockSpec((1, nt, size), lambda s, g, _: (s, 0, 0))],
        [blk, pl.BlockSpec((1, 1, 2 * nt, size), lambda s, g, _: (s, g, 0, 0))],
        [sds((nt, rows, hc), BF), sds((seqs, pairs, 2 * nt, size), F32)],
        scratch=[pltpu.VMEM((nt, PAIR, size), BF)],
        flops=seqs * pairs * 2 * 4 * (nt * size) ** 2 * 128,
        nbytes=8 * nt * rows * hc,
        prefetch=1,
    )(slot_of, qkv, qkv, qkv, start)


def attn_bwd_kernel(
    nt, slot_ref, q_ref, k_ref, v_ref, go_ref, start_ref, lse_ref, cos_ref, sin_ref,
    gq_ref, gk_ref, gv_ref, kt_ref, dk_ref, dv_ref,
):
    size = q_ref.shape[1]
    scale = HEAD_DIM**-0.5
    for b in range(nt):
        kt_ref[b] = k_ref[slot_ref[b]].T
    dk_ref[...] = jnp.zeros_like(dk_ref)
    dv_ref[...] = jnp.zeros_like(dv_ref)
    lane = lax.broadcasted_iota(jnp.int32, (size, PAIR), 1)
    for p in range(nt):
        slot = slot_ref[p]
        q = q_ref[slot] * BF(scale)
        go = go_ref[slot]
        start = start_ref[0, pl.ds(slot, 1), :]
        outs = []
        for h in range(2):
            mine = (lane >= HEAD_DIM) == (h == 1)
            qh = jnp.where(mine, q, BF(0))
            goh = jnp.where(mine, go, BF(0))
            lse = lse_ref[0, 0, pl.ds(2 * p + h, 1), :]
            probs, grads = [], []
            inner = jnp.zeros((1, size), F32)
            for b in range(p + 1):
                key_slot = slot_ref[b]
                s = dot_nt(k_ref[key_slot], qh)
                s = jnp.where(allowed_block(start, b, p, size), s, MASKED_SCORE)
                e = jnp.exp(s - lse)
                g = dot_nt(v_ref[key_slot], goh)
                inner += jnp.sum(e * g, axis=0, keepdims=True)
                probs.append(e)
                grads.append(g)
            dqt = jnp.zeros((HEAD_DIM, size), F32)
            for b in range(p + 1):
                ds = (probs[b] * (grads[b] - inner)).astype(BF)
                dv_ref[b] += dot(probs[b].astype(BF), goh)
                dk_ref[b] += dot(ds, qh)
                dqt += dot(kt_ref[b, h * HEAD_DIM : (h + 1) * HEAD_DIM, :], ds)
            outs.append(dqt)
        dq = jnp.concatenate(outs, axis=0).T * scale
        gq_ref[slot] = unrotate(dq, cos_ref[slot], sin_ref[slot]).astype(BF)
    for b in range(nt):
        slot = slot_ref[b]
        gk_ref[slot] = unrotate(dk_ref[b], cos_ref[slot], sin_ref[slot]).astype(BF)
        gv_ref[slot] = dv_ref[b].astype(BF)


def attention_backward(qkv, go, start, lse, cos, sin, slot_of, nt):
    _, _, rows, hc = qkv.shape
    seqs = start.shape[0]
    size = rows // seqs
    pairs = hc // PAIR
    blk = pl.BlockSpec((nt, size, PAIR), lambda s, g, _: (0, s, g))
    table = pl.BlockSpec((nt, size, PAIR), lambda s, g, _: (0, s, 0))
    return call(
        functools.partial(attn_bwd_kernel, nt),
        (seqs, pairs),
        qkv_specs(nt, size)
        + [
            blk,
            pl.BlockSpec((1, nt, size), lambda s, g, _: (s, 0, 0)),
            pl.BlockSpec((1, 1, 2 * nt, size), lambda s, g, _: (s, g, 0, 0)),
            table, table,
        ],
        [blk, blk, blk],
        [sds((nt, rows, hc), BF)] * 3,
        scratch=[
            pltpu.VMEM((nt, PAIR, size), BF),
            pltpu.VMEM((nt, size, PAIR), F32),
            pltpu.VMEM((nt, size, PAIR), F32),
        ],
        flops=seqs * pairs * 2 * 10 * (nt * size) ** 2 * 128,
        nbytes=14 * nt * rows * hc,
        prefetch=1,
    )(slot_of, qkv, qkv, qkv, go, start, lse, cos, sin)


def shard_group(nd, count):
    while nd % count or nd // count % 2:
        count //= 2
    return max(count, 1)


def cols_out_kernel(nt, steps, lhs_ref, w_ref, *outs):
    for slot in range(nt):
        lhs = lhs_ref[slot]
        parts = [dot(lhs, w_ref[j]) for j in range(w_ref.shape[0])]
        store_piece(outs, nt, slot, steps, jnp.concatenate(parts, axis=1))


def mm_cols(lhs, weight, nt, group):
    nd, depth, ds = weight.shape
    group = shard_group(nd, group)
    rows = lhs.shape[1]
    width = nd * ds
    shapes = flat(piece_shapes(nt, rows, width))
    outs = call(
        functools.partial(cols_out_kernel, nt, nd // group),
        (nd // group,),
        [whole_spec(lhs.shape), pl.BlockSpec((group, depth, ds), lambda j: (j, 0, 0))],
        out_piece_specs(nt, rows, width, group * ds),
        [sds(s, BF) for s in shapes],
        flops=2 * nt * rows * depth * width,
        nbytes=2 * (nt * rows * (depth + width) + depth * width),
    )(lhs, weight)
    return regroup(outs, nt)


def cols_back_kernel(nt, steps, nlhs, *refs):
    lhs, w_ref, outs = refs[:nlhs], refs[nlhs], refs[nlhs + 1 :]
    depth = w_ref.shape[3]
    weights = [w_ref[:, c].reshape(-1, depth) for c in range(nlhs)]
    for slot in range(nt):
        total = dot_nt(lhs[0][slot], weights[0])
        for c in range(1, nlhs):
            total += dot_nt(lhs[c][slot], weights[c])
        store_piece(outs, nt, slot, steps, total)


def mm_back(lhs, weight, nt, group):
    nd, count, ds, depth = weight.shape
    group = shard_group(nd, group)
    rows = lhs[0].shape[1]
    width = nd * ds
    shapes = flat(piece_shapes(nt, rows, width))
    outs = call(
        functools.partial(cols_back_kernel, nt, nd // group, count),
        (nd // group,),
        [whole_spec(a.shape) for a in lhs]
        + [pl.BlockSpec((group, count, ds, depth), lambda j: (j, 0, 0, 0))],
        out_piece_specs(nt, rows, width, group * ds),
        [sds(s, BF) for s in shapes],
        flops=2 * nt * rows * depth * width * count,
        nbytes=2 * (nt * rows * (depth * count + width) + depth * width * count),
    )(*lhs, weight)
    return regroup(outs, nt)


def gateup_kernel(nt, *refs):
    count = len(flat(piece_shapes(nt, 8, 8)))
    pieces, w_ref, (full_ref, gate_ref, up_ref, hid_ref) = (
        refs[:count],
        refs[count],
        refs[count + 1 :],
    )

    @pl.when(pl.program_id(0) == 0)
    def _():
        fill_from_pieces(pieces, full_ref, nt)

    cols = gate_ref.shape[2]
    w_gate = w_ref[:, 0].reshape(-1, cols)
    w_up = w_ref[:, 1].reshape(-1, cols)
    for slot in range(nt):
        a2 = full_ref[slot]
        gate = dot(a2, w_gate)
        up = dot(a2, w_up)
        gate_ref[slot] = gate.astype(BF)
        up_ref[slot] = up.astype(BF)
        hid_ref[slot] = (gate * jax.nn.sigmoid(gate) * up).astype(BF)


def gate_up(pieces, weight, nt):
    nd, _, ds, ff = weight.shape
    rows, width = pieces[0][0].shape
    step = min(512, ff)
    blk = pl.BlockSpec((nt, rows, step), lambda j: (0, 0, j))
    return call(
        functools.partial(gateup_kernel, nt),
        (ff // step,),
        [whole_spec(a.shape) for a in flat(pieces)]
        + [pl.BlockSpec((nd, 2, ds, step), lambda j: (0, 0, 0, j))],
        [whole_spec((nt, rows, width)), blk, blk, blk],
        [sds((nt, rows, width), BF)] + [sds((nt, rows, ff), BF)] * 3,
        flops=4 * nt * rows * width * ff,
        nbytes=2 * (2 * nt * rows * width + 2 * width * ff + 3 * nt * rows * ff),
    )(*flat(pieces), weight)


def gate_back_kernel(nt, full_ref, w_ref, gate_ref, up_ref, gg_ref, gu_ref):
    weight = jnp.concatenate([w_ref[j] for j in range(w_ref.shape[0])], axis=1)
    for slot in range(nt):
        gh = dot_nt(full_ref[slot], weight)
        gate = gate_ref[slot].astype(F32)
        up = up_ref[slot].astype(F32)
        sig = jax.nn.sigmoid(gate)
        gg_ref[slot] = (gh * up * sig * (1.0 + gate * (1.0 - sig))).astype(BF)
        gu_ref[slot] = (gh * gate * sig).astype(BF)


def gate_back(full, weight, gate, up, nt):
    nd, ff, ds = weight.shape
    _, rows, width = full.shape
    step = min(512, ff)
    blk = pl.BlockSpec((nt, rows, step), lambda j: (0, 0, j))
    return call(
        functools.partial(gate_back_kernel, nt),
        (ff // step,),
        [whole_spec(full.shape), pl.BlockSpec((nd, step, ds), lambda j: (0, j, 0)), blk, blk],
        [blk, blk],
        [sds((nt, rows, ff), BF)] * 2,
        flops=2 * nt * rows * width * ff,
        nbytes=2 * (nt * rows * width + width * ff + 4 * nt * rows * ff),
    )(full, weight, gate, up)


def context_back_kernel(nt, *refs):
    count = len(flat(piece_shapes(nt, 8, 8)))
    pieces, w_ref, (full_ref, out_ref) = refs[:count], refs[count], refs[count + 1 :]

    @pl.when(pl.program_id(0) == 0)
    def _():
        fill_from_pieces(pieces, full_ref, nt)

    weight = jnp.concatenate([w_ref[j] for j in range(w_ref.shape[0])], axis=1)
    for slot in range(nt):
        out_ref[slot] = dot_nt(full_ref[slot], weight).astype(BF)


def context_back(pieces, weight, nt):
    nd, hc, ds = weight.shape
    rows, width = pieces[0][0].shape
    step = min(256, hc)
    return call(
        functools.partial(context_back_kernel, nt),
        (hc // step,),
        [whole_spec(a.shape) for a in flat(pieces)]
        + [pl.BlockSpec((nd, step, ds), lambda j: (0, j, 0))],
        [whole_spec((nt, rows, width)), pl.BlockSpec((nt, rows, step), lambda j: (0, 0, j))],
        [sds((nt, rows, width), BF), sds((nt, rows, hc), BF)],
        flops=2 * nt * rows * width * hc,
        nbytes=2 * (2 * nt * rows * width + width * hc + nt * rows * hc),
    )(*flat(pieces), weight)


def middle_kernel(nterms, x_ref, gain_ref, *refs):
    terms, (mid_ref, low_ref) = refs[:nterms], refs[nterms:]
    mid = x_ref[...].astype(F32) + sum_terms(terms)
    mid_ref[...] = mid
    scale = lax.rsqrt(jnp.mean(mid * mid, axis=-1, keepdims=True) + NORM_EPS)
    low_ref[...] = (mid * scale * gain_ref[...]).astype(BF)


def make_middle(x, gain, terms):
    rows, width = x.shape
    tile = min(128, rows)
    blk = pl.BlockSpec((tile, width), lambda i: (i, 0))
    return call(
        functools.partial(middle_kernel, len(terms)),
        (rows // tile,),
        [blk, whole_spec(gain.shape)] + [blk] * len(terms),
        [blk, blk],
        [sds((rows, width), F32), sds((rows, width), BF)],
        nbytes=rows * width * (8 + 2 * len(terms)),
    )(x, gain, *terms)


def sum_terms(terms):
    total = terms[0][...].astype(F32)
    for t in terms[1:]:
        total += t[...].astype(F32)
    return total


def layer_out_kernel(nterms, mid_ref, *refs):
    refs[-1][...] = (mid_ref[...] + sum_terms(refs[:nterms])).astype(BF)


def place(group, groups, rows, tile, width, into):
    steps = rows // tile
    spec = pl.BlockSpec((tile, width), lambda i: (i + group * steps, 0))
    return spec, sds((groups * rows, width), BF), [] if into is None else [into]


def layer_out_rows(mid, terms, group, groups, into):
    rows, width = mid.shape
    tile = min(128, rows)
    blk = pl.BlockSpec((tile, width), lambda i: (i, 0))
    spec, shape, old = place(group, groups, rows, tile, width, into)
    return call(
        functools.partial(layer_out_kernel, len(terms)),
        (rows // tile,),
        [blk] * (1 + len(terms)) + [ANY] * len(old),
        spec,
        shape,
        nbytes=rows * width * (6 + 2 * len(terms)),
        aliases={1 + len(terms): 0} if old else None,
    )(mid, *terms, *old)


def norm_back_kernel(nterms, nouts, first_ref, v_ref, gain_ref, *refs):
    terms, outs, sum_ref = refs[:nterms], refs[-1 - nouts : -1], refs[-1]
    u = sum_terms(terms)
    v = v_ref[...].astype(F32)
    q = lax.rsqrt(jnp.mean(v * v, axis=-1, keepdims=True) + NORM_EPS)
    ug = u * gain_ref[...]
    inner = jnp.mean(ug * v, axis=-1, keepdims=True)
    grad = first_ref[...].astype(F32) + (q * ug - v * (q * q * q * inner))
    for out in outs:
        out[...] = grad.astype(out.dtype)

    @pl.when(pl.program_id(0) == 0)
    def _():
        sum_ref[...] = jnp.zeros_like(sum_ref)

    sum_ref[...] += jnp.sum(u * v * q, axis=0, keepdims=True)


def norm_back(first, v, gain, terms, group=None, groups=None, into=None):
    rows, width = v.shape
    tile = min(128, rows)
    blk = pl.BlockSpec((tile, width), lambda i: (i, 0))
    if group is None:
        specs, shapes, old = [blk, blk], [sds((rows, width), F32), sds((rows, width), BF)], []
    else:
        spec, shape, old = place(group, groups, rows, tile, width, into)
        specs, shapes = [spec], [shape]
    return call(
        functools.partial(norm_back_kernel, len(terms), len(specs)),
        (rows // tile,),
        [blk, blk, whole_spec(gain.shape)] + [blk] * len(terms) + [ANY] * len(old),
        specs + [pl.BlockSpec((1, width), lambda i: (0, 0))],
        shapes + [sds((1, width), F32)],
        nbytes=rows * width * (12 + 2 * len(terms)),
        aliases={3 + len(terms): 0} if old else None,
    )(first, v, gain, *terms, *old)


def wgrad_rows_kernel(groups, nrhs, *refs):
    lhs, rhs, out_ref = refs[:groups], refs[groups : groups * (1 + nrhs)], refs[-1]
    tile = lhs[0].shape[2]
    left = [a[...].reshape(-1, tile).T for a in lhs]
    for c in range(nrhs):
        total = None
        for g in range(groups):
            term = dot(left[g], rhs[c * groups + g][...].reshape(left[g].shape[1], -1))
            total = term if total is None else total + term
        out_ref[0, c] = total.astype(BF)


def wgrad_rows(lhs, rhs, nd, lo=0, hi=None, into=None):
    hi = nd if hi is None else hi
    groups = len(lhs)
    nt, rows, width = lhs[0].shape
    ds = width // nd
    n = rhs[0][0].shape[2]
    old = [] if into is None else [into]
    return call(
        functools.partial(wgrad_rows_kernel, groups, len(rhs)),
        (hi - lo,),
        [pl.BlockSpec((nt, rows, ds), lambda j: (0, 0, j + lo))] * groups
        + [whole_spec(a.shape) for r in rhs for a in r]
        + [ANY] * len(old),
        pl.BlockSpec((1, len(rhs), ds, n), lambda j: (j + lo, 0, 0, 0)),
        sds((nd, len(rhs), ds, n), BF),
        flops=2 * groups * nt * rows * ds * (hi - lo) * n * len(rhs),
        nbytes=2 * groups * nt * rows * (width + n * len(rhs)) + 2 * width * n * len(rhs),
        aliases={groups * (1 + len(rhs)): 0} if old else None,
    )(*lhs, *[a for r in rhs for a in r], *old)


def wgrad_cols_kernel(groups, nd, *refs):
    lhs, rhs, out_ref = refs[:groups], refs[groups:-1], refs[-1]
    tile = lhs[0].shape[2]
    ds = out_ref.shape[2]
    left = [a[...].reshape(-1, tile).T for a in lhs]
    total = None
    for g in range(groups):
        term = dot(left[g], rhs[g][...].reshape(left[g].shape[1], -1))
        total = term if total is None else total + term
    for j in range(nd):
        out_ref[j] = total[:, j * ds : (j + 1) * ds].astype(BF)


def wgrad_cols(lhs, rhs, nd):
    groups = len(lhs)
    nt, rows, m = lhs[0].shape
    width = rhs[0].shape[2]
    tile = min(256, m)
    return call(
        functools.partial(wgrad_cols_kernel, groups, nd),
        (m // tile,),
        [pl.BlockSpec((nt, rows, tile), lambda i: (0, 0, i))] * groups
        + [whole_spec(a.shape) for a in rhs],
        pl.BlockSpec((nd, tile, width // nd), lambda i: (0, i, 0)),
        sds((nd, m, width // nd), BF),
        flops=2 * groups * nt * rows * width * m,
        nbytes=2 * groups * nt * rows * (width + m) + 2 * width * m,
    )(*lhs, *rhs)


def doc_starts(segments):
    row_len = segments.shape[-1]
    ids = jnp.arange(row_len, dtype=jnp.int32)
    change = jnp.concatenate(
        [jnp.ones_like(segments[:, :1], dtype=bool), segments[:, 1:] != segments[:, :-1]], axis=1
    )
    return lax.cummax(jnp.where(change, ids[None, :], 0), axis=1)


def slot_order(blocks, index, nt):
    if nt != 4:
        return blocks
    pairs = jnp.stack([blocks[:, 1], blocks[:, 0], blocks[:, 3], blocks[:, 2]], axis=1)
    blocks = jnp.where(index % 2 == 1, pairs, blocks)
    halves = jnp.stack([blocks[:, 2], blocks[:, 3], blocks[:, 0], blocks[:, 1]], axis=1)
    return jnp.where(index // 2 == 1, halves, blocks)


def per_device(nd, nt, groups, layer_input, segments, qkv_w, out_w, gain1, gateup_w, down_w, gain2, grad_out):
    seqs, local, width = layer_input.shape
    per = seqs // groups
    index = lax.axis_index("tensor").astype(jnp.int32)
    blocks = jnp.arange(nt, dtype=jnp.int32)
    slot_of = blocks ^ index if nt == 4 else blocks

    x = [layer_input[g * per : (g + 1) * per].reshape(per * local, width) for g in range(groups)]
    go = [grad_out[g * per : (g + 1) * per].reshape(per * local, width) for g in range(groups)]
    x_pieces = [gather_pieces(a, nt) for a in x]

    gains = lax.all_gather(jnp.stack([gain1, gain2]), "dp", axis=1, tiled=True).astype(F32)
    g1, g2 = gains[:1], gains[1:]
    full_qkv = lax.all_gather(qkv_w, "dp", axis=0, tiled=False)
    full_out = lax.all_gather(out_w, "dp", axis=0, tiled=False)
    full_gateup = lax.all_gather(gateup_w, "dp", axis=0, tiled=False)
    full_down = lax.all_gather(down_w, "dp", axis=0, tiled=False)

    start_abs = doc_starts(segments)
    pos_abs = jnp.arange(segments.shape[1], dtype=jnp.int32)[None, :] - start_abs
    start_slot = slot_order(start_abs.reshape(seqs, nt, local), index, nt)
    pos_slot = slot_order(pos_abs.reshape(seqs, nt, local), index, nt)
    inv_freq = ROPE_BASE ** (-jnp.arange(HALF, dtype=F32) * 2.0 / HEAD_DIM)
    angles = pos_slot.astype(F32)[..., None] * inv_freq
    cos, sin = jnp.cos(angles), jnp.sin(angles)
    cos = jnp.concatenate([cos] * 4, axis=-1)
    sin = jnp.concatenate([-sin, sin] * 2, axis=-1)

    def table(t, g):
        t = t[g * per : (g + 1) * per]
        return jnp.swapaxes(t, 0, 1).reshape(nt, per * local, PAIR)

    coss = [table(cos, g) for g in range(groups)]
    sins = [table(sin, g) for g in range(groups)]
    starts = [start_slot[g * per : (g + 1) * per] for g in range(groups)]

    def after(value, done):
        return lax.optimization_barrier((value, done))[0]

    Order.last = None
    both = range(groups)
    qkv, ctx, lse, mid, low2, g_mid, g_low = ({} for _ in range(7))

    a1 = [assemble(x_pieces[g], nt, g1) for g in both]
    go_pieces = {0: gather_pieces(after(go[0], flat(x_pieces[-1])[-1]), nt)}
    attn_sum = {}
    for g in both:
        qkv[g] = project_qkv(a1[g], full_qkv, coss[g], sins[g], nt)
        if g > 0:
            attn_sum[g - 1].second()
        ctx[g], lse[g] = attention_forward(qkv[g], starts[g], slot_of, nt)
        attn_sum[g] = Scatter(mm_cols(ctx[g], full_out, nt, 4), nt)
    a2_pieces = {}
    gof = {}
    for g in both:
        if g == groups - 1:
            gof[0] = assemble(go_pieces[0], nt)
            attn_sum[g].second()
        mid[g], low2[g] = make_middle(x[g], g2, attn_sum[g].terms)
        a2_pieces[g] = gather_pieces(low2[g], nt)
    for g in range(1, groups):
        go_pieces[g] = gather_pieces(after(go[g], flat(a2_pieces[groups - 1])[-1]), nt)

    a2, gate, up, hid = zip(*[gate_up(a2_pieces[g], full_gateup, nt) for g in both])
    for g in range(1, groups):
        gof[g] = assemble(go_pieces[g], nt)
    gof = [gof[g] for g in both]
    grad_down = wgrad_cols(hid, gof, nd)
    gg, gu = zip(*[gate_back(gof[g], full_down, gate[g], up[g], nt) for g in both])
    ga2, out_sum, ga1 = {}, {}, {}
    ga2[0] = Scatter(mm_back([gg[0], gu[0]], full_gateup, nt, 2), nt)
    grad_gateup = wgrad_rows(a2, [gg, gu], nd, 0, nd // 2)
    ga2[0].second()
    grad_gateup = wgrad_rows(a2, [gg, gu], nd, nd // 2, nd, grad_gateup)
    sum1, sum2, gm_pieces, gmf, g_qkv = {}, {}, {}, {}, {}

    def residual_back(g):
        g_mid[g], g_low[g], sum2[g] = norm_back(go[g], mid[g], g2, ga2[g].terms)
        gm_pieces[g] = gather_pieces(g_low[g], nt)

    def attention_back(g):
        gmf[g], g_ctx = context_back(gm_pieces[g], full_out, nt)
        g_qkv[g] = attention_backward(
            qkv[g], g_ctx, starts[g], lse[g], coss[g], sins[g], slot_of, nt
        )
        ga1[g] = Scatter(mm_back(g_qkv[g], full_qkv, nt, 4), nt)

    residual_back(0)
    ga2[1] = Scatter(mm_back([gg[1], gu[1]], full_gateup, nt, 2), nt)
    out_sum[0] = Scatter(mm_cols(hid[0], full_down, nt, 2), nt)
    ga2[1].second()
    attention_back(0)
    residual_back(1)
    out_sum[0].second()
    out_sum[1] = Scatter(mm_cols(hid[1], full_down, nt, 2), nt)
    ga1[0].second()
    attention_back(1)
    grad_wout = wgrad_cols([ctx[g] for g in both], [gmf[g] for g in both], nd)
    grad_qkv = wgrad_rows(a1, [[g_qkv[g][c] for g in both] for c in range(3)], nd)
    ga1[1].second()
    out_sum[1].second()
    grad_input = layer_out = None
    for g in both:
        layer_out = layer_out_rows(mid[g], out_sum[g].terms, g, groups, layer_out)
        grad_input, sum1[g] = norm_back(g_mid[g], x[g], g1, ga1[g].terms, g, groups, grad_input)

    def dp_sum(grad):
        return lax.psum_scatter(grad, "dp", scatter_dimension=0, tiled=False).astype(F32)

    gain_sums = jnp.concatenate([sum1[0] + sum1[1], sum2[0] + sum2[1]], axis=0)
    gain_sums = lax.psum(gain_sums, ("dp", "tensor"))
    ds = gain1.shape[0]
    mine = lax.dynamic_slice_in_dim(gain_sums, lax.axis_index("dp") * ds, ds, 1)
    grad_down, grad_gateup = dp_sum(grad_down), dp_sum(grad_gateup)
    return (
        layer_out.reshape(seqs, local, width),
        grad_input.reshape(seqs, local, width),
        dp_sum(grad_qkv),
        dp_sum(grad_wout)[:, :],
        mine[0],
        grad_gateup,
        grad_down,
        mine[1],
    )


def solution(mesh):
    nd, nt = mesh.shape["dp"], mesh.shape["tensor"]
    return jax.shard_map(
        functools.partial(per_device, nd, nt, 2),
        mesh=mesh,
        in_specs=(
            P("dp", "tensor", None),
            P("dp", None),
            P(None, "dp", "tensor"),
            P("tensor", "dp"),
            P("dp"),
            P(None, "dp", "tensor"),
            P("tensor", "dp"),
            P("dp"),
            P("dp", "tensor", None),
        ),
        out_specs=(
            P("dp", "tensor", None),
            P("dp", "tensor", None),
            P(None, "dp", "tensor"),
            P("tensor", "dp"),
            P("dp"),
            P(None, "dp", "tensor"),
            P("tensor", "dp"),
            P("dp"),
        ),
        check_vma=False,
    )
```

```python
import functools

import jax
import jax.numpy as jnp
from jax import lax
from jax.experimental import pallas as pl
from jax.experimental.pallas import tpu as pltpu
from jax.sharding import PartitionSpec as P

HEAD_DIM = 64
HALF = HEAD_DIM // 2
PAIR = 2 * HEAD_DIM
NORM_EPS = 1e-05
ROPE_BASE = 130000.0
MASKED_SCORE = -1e30
BF = jnp.bfloat16
F32 = jnp.float32
VMEM_LIMIT = 60 * 1024 * 1024
SMALL = 3

NT = (((1,), (1,)), ((), ()))


def dot(a, b):
    return jnp.dot(a, b, preferred_element_type=F32)


def dot_nt(a, b):
    return lax.dot_general(a, b, NT, preferred_element_type=F32)


class Order:
    last = None


ANY = pl.BlockSpec(memory_space=pl.ANY)


def call(body, grid, in_specs, out_specs, out_shape, scratch=(), flops=0, nbytes=0, aliases=None, prefetch=0):
    first_extra = prefetch + len(in_specs)

    def run(*args):
        extra = [] if Order.last is None else [Order.last]

        def ordered_body(*refs):
            body(*refs[:first_extra], *refs[first_extra + len(extra) :])

        outs = pl.pallas_call(
            ordered_body,
            grid_spec=pltpu.PrefetchScalarGridSpec(
                num_scalar_prefetch=prefetch,
                grid=grid,
                in_specs=in_specs + [ANY] * len(extra),
                out_specs=out_specs,
                scratch_shapes=list(scratch),
            ),
            out_shape=out_shape,
            input_output_aliases=aliases or {},
            cost_estimate=pl.CostEstimate(flops=flops // SMALL, bytes_accessed=nbytes // SMALL, transcendentals=0),
            compiler_params=pltpu.CompilerParams(vmem_limit_bytes=VMEM_LIMIT),
        )(*args, *extra)
        Order.last = outs[-1] if isinstance(outs, (list, tuple)) else outs
        return outs

    return run


def link_kernel(value_ref, done_ref, out_ref):
    pass


def link(value, done):
    return call(link_kernel, (1,), [ANY, ANY], ANY, sds(value.shape, value.dtype), aliases={0: 0})(value, done)


def whole_spec(shape, buffers=1):
    zeros = (0,) * len(shape)
    return pl.BlockSpec(shape, lambda *_: zeros, pipeline_mode=pl.Buffered(buffers))


def sds(shape, dtype):
    return jax.ShapeDtypeStruct(shape, dtype)


def swap_perm(count, bit):
    return [(i, i ^ bit) for i in range(count)]


def halves_kernel(y_ref, x_ref, left_ref, right_ref):
    left_ref[...] = y_ref[...]
    right_ref[...] = x_ref[...]


def halves(from_y, from_x):
    rows, width = from_y.shape
    half = width // 2
    tile = min(128, rows)

    def spec(which):
        return pl.BlockSpec((tile, half), lambda i: (i, which))

    return call(
        halves_kernel,
        (rows // tile,),
        [spec(0), spec(1)],
        [spec(0), spec(0)],
        [sds((rows, half), BF)] * 2,
        nbytes=rows * half * 8,
    )(from_y, from_x)


class Gather:
    def __init__(self, block, nt):
        self.nt = nt
        if nt != 4:
            full = lax.all_gather(block, "tensor", axis=0, tiled=False)
            self.pieces = [(full[r],) for r in range(nt)]
            return
        self.block = block
        self.from_x = lax.ppermute(block, "tensor", swap_perm(4, 1))
        self.from_y = lax.ppermute(block, "tensor", swap_perm(4, 2))

    def second(self):
        if self.nt != 4:
            return
        left, right = halves(self.from_y, self.from_x)
        diag_x = lax.ppermute(left, "tensor", swap_perm(4, 1))
        diag_y = lax.ppermute(right, "tensor", swap_perm(4, 2))
        self.pieces = [(self.block,), (self.from_x,), (self.from_y,), (diag_x, diag_y)]


def add_halves_kernel(x_ref, for_x_ref, y_ref, for_y_ref, out_x_ref, out_y_ref):
    out_x_ref[...] = (x_ref[...].astype(F32) + for_x_ref[...].astype(F32)).astype(BF)
    out_y_ref[...] = (y_ref[...].astype(F32) + for_y_ref[...].astype(F32)).astype(BF)


def add_halves(to_x, for_x, to_y, for_y):
    rows, width = to_x.shape
    half = width // 2
    tile = min(128, rows)

    def spec(which):
        return pl.BlockSpec((tile, half), lambda i: (i, which))

    return call(
        add_halves_kernel,
        (rows // tile,),
        [spec(1), spec(0), spec(0), spec(0)],
        [spec(1), spec(0)],
        [sds(to_x.shape, BF)] * 2,
        nbytes=rows * half * 12,
        aliases={0: 0, 2: 1},
    )(to_x, for_x, to_y, for_y)


class Scatter:
    def __init__(self, parts, nt):
        self.nt = nt
        if nt != 4:
            full = jnp.stack([p[0] for p in parts])
            self.terms = [lax.psum_scatter(full, "tensor", scatter_dimension=0, tiled=False)]
            return
        (self.own,), (self.to_x,), (self.to_y,), (diag_x, diag_y) = parts
        self.for_y = lax.ppermute(diag_x, "tensor", swap_perm(4, 1))
        self.for_x = lax.ppermute(diag_y, "tensor", swap_perm(4, 2))

    def second(self):
        if self.nt != 4:
            return
        to_x, to_y = add_halves(self.to_x, self.for_x, self.to_y, self.for_y)
        self.terms = [
            self.own,
            lax.ppermute(to_x, "tensor", swap_perm(4, 1)),
            lax.ppermute(to_y, "tensor", swap_perm(4, 2)),
        ]


def piece_shapes(nt, rows, width):
    if nt != 4:
        return [((rows, width),)] * nt
    return [((rows, width),)] * 3 + [((rows, width // 2),) * 2]


def flat(pieces):
    return [a for p in pieces for a in p]


def regroup(items, nt):
    if nt != 4:
        return [(a,) for a in items]
    return [(items[0],), (items[1],), (items[2],), (items[3], items[4])]


def fill_from_pieces(refs, full_ref, nt):
    for slot, part in enumerate(regroup(refs, nt)):
        if len(part) == 1:
            full_ref[slot] = part[0][...]
        else:
            half = part[0].shape[1]
            full_ref[slot, :, :half] = part[0][...]
            full_ref[slot, :, half:] = part[1][...]


def out_piece_specs(nt, rows, width, step):
    specs = []
    half_steps = width // step // 2
    for part in piece_shapes(nt, rows, width):
        if len(part) == 1:
            specs.append(pl.BlockSpec((rows, step), lambda j: (0, j)))
        else:
            specs.append(pl.BlockSpec((rows, step), lambda j: (0, jnp.minimum(j, half_steps - 1))))
            specs.append(pl.BlockSpec((rows, step), lambda j: (0, jnp.maximum(j - half_steps, 0))))
    return specs


def store_piece(outs, nt, slot, steps, value):
    part = regroup(outs, nt)[slot]
    if len(part) == 1:
        part[0][...] = value.astype(BF)
    else:
        j = pl.program_id(0)

        @pl.when(j < steps // 2)
        def _():
            part[0][...] = value.astype(BF)

        @pl.when(j >= steps // 2)
        def _():
            part[1][...] = value.astype(BF)


def turn(v):
    lane = lax.broadcasted_iota(jnp.int32, v.shape, 1)
    return jnp.where(lane % HEAD_DIM < HALF, pltpu.roll(v, PAIR - HALF, 1), pltpu.roll(v, HALF, 1))


def rotate(v, cos, sin):
    return v * cos + turn(v) * sin


def unrotate(u, cos, sin):
    return u * cos + turn(u * sin)


def assemble_kernel(nt, normed, *refs):
    pieces, full_ref = refs[: -1 - normed], refs[-1]
    fill_from_pieces(pieces, full_ref, nt)
    if normed:
        gain = refs[-2][...]
        for slot in range(nt):
            x = full_ref[slot].astype(F32)
            scale = lax.rsqrt(jnp.mean(x * x, axis=-1, keepdims=True) + NORM_EPS)
            full_ref[slot] = (x * scale * gain).astype(BF)


def assemble(pieces, nt, gain=None):
    rows, width = pieces[0][0].shape
    tile = min(64, rows)
    items = flat(pieces)
    extra = [] if gain is None else [gain]
    return call(
        functools.partial(assemble_kernel, nt, len(extra)),
        (rows // tile,),
        [pl.BlockSpec((tile, a.shape[1]), lambda i: (i, 0)) for a in items]
        + [whole_spec(a.shape) for a in extra],
        pl.BlockSpec((nt, tile, width), lambda i: (0, i, 0)),
        sds((nt, rows, width), BF),
        nbytes=4 * nt * rows * width,
    )(*items, *extra)


def qkv_kernel(nt, a1_ref, w_ref, cos_ref, sin_ref, out_ref):
    cols = out_ref.shape[3]
    weight = w_ref[:, 0].reshape(-1, cols)

    @pl.when(pl.program_id(0) < 2)
    def _():
        for slot in range(nt):
            raw = dot(a1_ref[slot], weight)
            cos, sin = cos_ref[slot], sin_ref[slot]
            for p in range(cols // PAIR):
                part = slice(p * PAIR, (p + 1) * PAIR)
                out_ref[0, slot, :, part] = rotate(raw[:, part], cos, sin).astype(BF)

    @pl.when(pl.program_id(0) == 2)
    def _():
        for slot in range(nt):
            out_ref[0, slot] = dot(a1_ref[slot], weight).astype(BF)


def project_qkv(a1, weight, cos, sin, nt):
    nd, _, ds, hc = weight.shape
    _, rows, width = a1.shape
    return call(
        functools.partial(qkv_kernel, nt),
        (3,),
        [
            whole_spec(a1.shape),
            pl.BlockSpec((nd, 1, ds, hc), lambda c: (0, c, 0, 0)),
            whole_spec(cos.shape),
            whole_spec(sin.shape),
        ],
        pl.BlockSpec((1, nt, rows, hc), lambda c: (c, 0, 0, 0)),
        sds((3, nt, rows, hc), BF),
        flops=2 * nt * rows * width * hc * 3,
        nbytes=2 * (nt * rows * width + 3 * width * hc + 3 * nt * rows * hc),
    )(a1, weight, cos, sin)


def allowed_block(start, key_block, query_block, size):
    key_id = lax.broadcasted_iota(jnp.int32, (size, size), 0) + key_block * size
    ok = key_id >= start
    if key_block == query_block:
        ok &= lax.broadcasted_iota(jnp.int32, (size, size), 1) + query_block * size >= key_id
    return ok


def attn_fwd_kernel(nt, slot_ref, q_ref, k_ref, v_ref, start_ref, ctx_ref, lse_ref, vt_ref):
    size = q_ref.shape[1]
    for b in range(nt):
        vt_ref[b] = v_ref[slot_ref[b]].T
    lane = lax.broadcasted_iota(jnp.int32, (size, PAIR), 1)
    for p in range(nt):
        slot = slot_ref[p]
        q = q_ref[slot] * BF(HEAD_DIM**-0.5)
        start = start_ref[0, pl.ds(slot, 1), :]
        outs = []
        for h in range(2):
            qh = jnp.where((lane >= HEAD_DIM) == (h == 1), q, BF(0))
            scores = []
            for b in range(p + 1):
                s = dot_nt(k_ref[slot_ref[b]], qh)
                scores.append(jnp.where(allowed_block(start, b, p, size), s, MASKED_SCORE))
            top = functools.reduce(
                jnp.maximum, [jnp.max(s, axis=0, keepdims=True) for s in scores]
            )
            total = jnp.zeros((1, size), F32)
            acc = jnp.zeros((HEAD_DIM, size), F32)
            for b, s in enumerate(scores):
                e = jnp.exp(s - top)
                total += jnp.sum(e, axis=0, keepdims=True)
                acc += dot(vt_ref[b, h * HEAD_DIM : (h + 1) * HEAD_DIM, :], e.astype(BF))
            outs.append(acc / total)
            lse_ref[0, 0, pl.ds(2 * p + h, 1), :] = top + jnp.log(total)
        ctx_ref[slot] = jnp.concatenate(outs, axis=0).T.astype(BF)


def qkv_specs(nt, size):
    def spec(c):
        return pl.BlockSpec((None, nt, size, PAIR), lambda s, g, _: (c, 0, s, g))

    return [spec(c) for c in range(3)]


def attention_forward(qkv, start, slot_of, nt):
    _, _, rows, hc = qkv.shape
    seqs = start.shape[0]
    size = rows // seqs
    pairs = hc // PAIR
    blk = pl.BlockSpec((nt, size, PAIR), lambda s, g, _: (0, s, g))
    return call(
        functools.partial(attn_fwd_kernel, nt),
        (seqs, pairs),
        qkv_specs(nt, size) + [pl.BlockSpec((1, nt, size), lambda s, g, _: (s, 0, 0))],
        [blk, pl.BlockSpec((1, 1, 2 * nt, size), lambda s, g, _: (s, g, 0, 0))],
        [sds((nt, rows, hc), BF), sds((seqs, pairs, 2 * nt, size), F32)],
        scratch=[pltpu.VMEM((nt, PAIR, size), BF)],
        flops=seqs * pairs * 2 * 4 * (nt * size) ** 2 * 128,
        nbytes=8 * nt * rows * hc,
        prefetch=1,
    )(slot_of, qkv, qkv, qkv, start)


def attn_bwd_kernel(
    nt, slot_ref, q_ref, k_ref, v_ref, go_ref, start_ref, lse_ref, cos_ref, sin_ref,
    gq_ref, gk_ref, gv_ref, kt_ref, dk_ref, dv_ref,
):
    size = q_ref.shape[1]
    scale = HEAD_DIM**-0.5
    for b in range(nt):
        kt_ref[b] = k_ref[slot_ref[b]].T
    dk_ref[...] = jnp.zeros_like(dk_ref)
    dv_ref[...] = jnp.zeros_like(dv_ref)
    lane = lax.broadcasted_iota(jnp.int32, (size, PAIR), 1)
    for p in range(nt):
        slot = slot_ref[p]
        q = q_ref[slot] * BF(scale)
        go = go_ref[slot]
        start = start_ref[0, pl.ds(slot, 1), :]
        outs = []
        for h in range(2):
            mine = (lane >= HEAD_DIM) == (h == 1)
            qh = jnp.where(mine, q, BF(0))
            goh = jnp.where(mine, go, BF(0))
            lse = lse_ref[0, 0, pl.ds(2 * p + h, 1), :]
            probs, grads = [], []
            inner = jnp.zeros((1, size), F32)
            for b in range(p + 1):
                key_slot = slot_ref[b]
                s = dot_nt(k_ref[key_slot], qh)
                s = jnp.where(allowed_block(start, b, p, size), s, MASKED_SCORE)
                e = jnp.exp(s - lse)
                g = dot_nt(v_ref[key_slot], goh)
                inner += jnp.sum(e * g, axis=0, keepdims=True)
                probs.append(e)
                grads.append(g)
            dqt = jnp.zeros((HEAD_DIM, size), F32)
            for b in range(p + 1):
                ds = (probs[b] * (grads[b] - inner)).astype(BF)
                dv_ref[b] += dot(probs[b].astype(BF), goh)
                dk_ref[b] += dot(ds, qh)
                dqt += dot(kt_ref[b, h * HEAD_DIM : (h + 1) * HEAD_DIM, :], ds)
            outs.append(dqt)
        dq = jnp.concatenate(outs, axis=0).T * scale
        gq_ref[slot] = unrotate(dq, cos_ref[slot], sin_ref[slot]).astype(BF)
    for b in range(nt):
        slot = slot_ref[b]
        gk_ref[slot] = unrotate(dk_ref[b], cos_ref[slot], sin_ref[slot]).astype(BF)
        gv_ref[slot] = dv_ref[b].astype(BF)


def attention_backward(qkv, go, start, lse, cos, sin, slot_of, nt):
    _, _, rows, hc = qkv.shape
    seqs = start.shape[0]
    size = rows // seqs
    pairs = hc // PAIR
    blk = pl.BlockSpec((nt, size, PAIR), lambda s, g, _: (0, s, g))
    table = pl.BlockSpec((nt, size, PAIR), lambda s, g, _: (0, s, 0))
    return call(
        functools.partial(attn_bwd_kernel, nt),
        (seqs, pairs),
        qkv_specs(nt, size)
        + [
            blk,
            pl.BlockSpec((1, nt, size), lambda s, g, _: (s, 0, 0)),
            pl.BlockSpec((1, 1, 2 * nt, size), lambda s, g, _: (s, g, 0, 0)),
            table, table,
        ],
        [blk, blk, blk],
        [sds((nt, rows, hc), BF)] * 3,
        scratch=[
            pltpu.VMEM((nt, PAIR, size), BF),
            pltpu.VMEM((nt, size, PAIR), F32),
            pltpu.VMEM((nt, size, PAIR), F32),
        ],
        flops=seqs * pairs * 2 * 10 * (nt * size) ** 2 * 128,
        nbytes=14 * nt * rows * hc,
        prefetch=1,
    )(slot_of, qkv, qkv, qkv, go, start, lse, cos, sin)


def shard_group(nd, count):
    while nd % count or nd // count % 2:
        count //= 2
    return max(count, 1)


def cols_out_kernel(nt, steps, lhs_ref, w_ref, *outs):
    for slot in range(nt):
        lhs = lhs_ref[slot]
        parts = [dot(lhs, w_ref[j]) for j in range(w_ref.shape[0])]
        store_piece(outs, nt, slot, steps, jnp.concatenate(parts, axis=1))


def mm_cols(lhs, weight, nt, group):
    nd, depth, ds = weight.shape
    group = shard_group(nd, group)
    rows = lhs.shape[1]
    width = nd * ds
    shapes = flat(piece_shapes(nt, rows, width))
    outs = call(
        functools.partial(cols_out_kernel, nt, nd // group),
        (nd // group,),
        [whole_spec(lhs.shape), pl.BlockSpec((group, depth, ds), lambda j: (j, 0, 0))],
        out_piece_specs(nt, rows, width, group * ds),
        [sds(s, BF) for s in shapes],
        flops=2 * nt * rows * depth * width,
        nbytes=2 * (nt * rows * (depth + width) + depth * width),
    )(lhs, weight)
    return regroup(outs, nt)


def cols_back_kernel(nt, steps, nlhs, *refs):
    lhs, w_refs, outs = refs[:nlhs], refs[nlhs : 2 * nlhs], refs[2 * nlhs :]
    depth = w_refs[0].shape[3]
    weights = [w[:, 0].reshape(-1, depth) for w in w_refs]
    for slot in range(nt):
        total = dot_nt(lhs[0][slot], weights[0])
        for c in range(1, nlhs):
            total += dot_nt(lhs[c][slot], weights[c])
        store_piece(outs, nt, slot, steps, total)


def mm_back(lhs, weight, channels, nt, group):
    nd, _, ds, depth = weight.shape
    count = len(lhs)
    group = shard_group(nd, group)
    rows = lhs[0].shape[1]
    width = nd * ds
    shapes = flat(piece_shapes(nt, rows, width))

    def spec(c):
        return pl.BlockSpec((group, 1, ds, depth), lambda j: (j, c, 0, 0))

    outs = call(
        functools.partial(cols_back_kernel, nt, nd // group, count),
        (nd // group,),
        [whole_spec(a.shape) for a in lhs] + [spec(c) for c in channels],
        out_piece_specs(nt, rows, width, group * ds),
        [sds(s, BF) for s in shapes],
        flops=2 * nt * rows * depth * width * count,
        nbytes=2 * (nt * rows * (depth * count + width) + depth * width * count),
    )(*lhs, *[weight] * count)
    return regroup(outs, nt)


def gateup_kernel(nt, *refs):
    count = len(flat(piece_shapes(nt, 8, 8)))
    pieces, w_ref, (full_ref, gate_ref, up_ref, hid_ref) = (
        refs[:count],
        refs[count],
        refs[count + 1 :],
    )

    @pl.when(pl.program_id(0) == 0)
    def _():
        fill_from_pieces(pieces, full_ref, nt)

    cols = gate_ref.shape[2]
    w_gate = w_ref[:, 0].reshape(-1, cols)
    w_up = w_ref[:, 1].reshape(-1, cols)
    for slot in range(nt):
        a2 = full_ref[slot]
        gate = dot(a2, w_gate)
        up = dot(a2, w_up)
        gate_ref[slot] = gate.astype(BF)
        up_ref[slot] = up.astype(BF)
        hid_ref[slot] = (gate * jax.nn.sigmoid(gate) * up).astype(BF)


def gate_up(pieces, weight, nt):
    nd, _, ds, ff = weight.shape
    rows, width = pieces[0][0].shape
    step = min(512, ff)
    blk = pl.BlockSpec((nt, rows, step), lambda j: (0, 0, j))
    return call(
        functools.partial(gateup_kernel, nt),
        (ff // step,),
        [whole_spec(a.shape) for a in flat(pieces)]
        + [pl.BlockSpec((nd, 2, ds, step), lambda j: (0, 0, 0, j))],
        [whole_spec((nt, rows, width)), blk, blk, blk],
        [sds((nt, rows, width), BF)] + [sds((nt, rows, ff), BF)] * 3,
        flops=4 * nt * rows * width * ff,
        nbytes=2 * (2 * nt * rows * width + 2 * width * ff + 3 * nt * rows * ff),
    )(*flat(pieces), weight)


def gate_back_kernel(nt, full_ref, w_ref, gate_ref, up_ref, gg_ref, gu_ref):
    weight = jnp.concatenate([w_ref[j] for j in range(w_ref.shape[0])], axis=1)
    for slot in range(nt):
        gh = dot_nt(full_ref[slot], weight)
        gate = gate_ref[slot].astype(F32)
        up = up_ref[slot].astype(F32)
        sig = jax.nn.sigmoid(gate)
        gg_ref[slot] = (gh * up * sig * (1.0 + gate * (1.0 - sig))).astype(BF)
        gu_ref[slot] = (gh * gate * sig).astype(BF)


def gate_back(full, weight, gate, up, nt):
    nd, ff, ds = weight.shape
    _, rows, width = full.shape
    step = min(512, ff)
    blk = pl.BlockSpec((nt, rows, step), lambda j: (0, 0, j))
    return call(
        functools.partial(gate_back_kernel, nt),
        (ff // step,),
        [whole_spec(full.shape), pl.BlockSpec((nd, step, ds), lambda j: (0, j, 0)), blk, blk],
        [blk, blk],
        [sds((nt, rows, ff), BF)] * 2,
        flops=2 * nt * rows * width * ff,
        nbytes=2 * (nt * rows * width + width * ff + 4 * nt * rows * ff),
    )(full, weight, gate, up)


def context_back_kernel(nt, *refs):
    count = len(flat(piece_shapes(nt, 8, 8)))
    pieces, w_ref, (full_ref, out_ref) = refs[:count], refs[count], refs[count + 1 :]

    @pl.when(pl.program_id(0) == 0)
    def _():
        fill_from_pieces(pieces, full_ref, nt)

    weight = w_ref[:, 0].reshape(-1, w_ref.shape[3])
    for slot in range(nt):
        out_ref[slot] = dot(full_ref[slot], weight).astype(BF)


def context_back(pieces, weight, channel, nt):
    nd, _, ds, hc = weight.shape
    rows, width = pieces[0][0].shape
    step = min(256, hc)
    return call(
        functools.partial(context_back_kernel, nt),
        (hc // step,),
        [whole_spec(a.shape) for a in flat(pieces)]
        + [pl.BlockSpec((nd, 1, ds, step), lambda j: (0, channel, 0, j))],
        [whole_spec((nt, rows, width)), pl.BlockSpec((nt, rows, step), lambda j: (0, 0, j))],
        [sds((nt, rows, width), BF), sds((nt, rows, hc), BF)],
        flops=2 * nt * rows * width * hc,
        nbytes=2 * (2 * nt * rows * width + width * hc + nt * rows * hc),
    )(*flat(pieces), weight)


def middle_kernel(nterms, x_ref, gain_ref, *refs):
    terms, (mid_ref, low_ref) = refs[:nterms], refs[nterms:]
    mid = x_ref[...].astype(F32) + sum_terms(terms)
    mid_ref[...] = mid
    scale = lax.rsqrt(jnp.mean(mid * mid, axis=-1, keepdims=True) + NORM_EPS)
    low_ref[...] = (mid * scale * gain_ref[...]).astype(BF)


def make_middle(x, gain, terms):
    rows, width = x.shape
    tile = min(128, rows)
    blk = pl.BlockSpec((tile, width), lambda i: (i, 0))
    return call(
        functools.partial(middle_kernel, len(terms)),
        (rows // tile,),
        [blk, whole_spec(gain.shape)] + [blk] * len(terms),
        [blk, blk],
        [sds((rows, width), F32), sds((rows, width), BF)],
        nbytes=rows * width * (8 + 2 * len(terms)),
    )(x, gain, *terms)


def sum_terms(terms):
    total = terms[0][...].astype(F32)
    for t in terms[1:]:
        total += t[...].astype(F32)
    return total


def layer_out_kernel(nterms, mid_ref, *refs):
    refs[-1][...] = (mid_ref[...] + sum_terms(refs[:nterms])).astype(BF)


def place(group, groups, rows, tile, width, into):
    steps = rows // tile
    spec = pl.BlockSpec((tile, width), lambda i: (i + group * steps, 0))
    return spec, sds((groups * rows, width), BF), [] if into is None else [into]


def layer_out_rows(mid, terms, group, groups, into):
    rows, width = mid.shape
    tile = min(128, rows)
    blk = pl.BlockSpec((tile, width), lambda i: (i, 0))
    spec, shape, old = place(group, groups, rows, tile, width, into)
    return call(
        functools.partial(layer_out_kernel, len(terms)),
        (rows // tile,),
        [blk] * (1 + len(terms)) + [ANY] * len(old),
        spec,
        shape,
        nbytes=rows * width * (6 + 2 * len(terms)),
        aliases={1 + len(terms): 0} if old else None,
    )(mid, *terms, *old)


def norm_back_kernel(nterms, nouts, first_ref, v_ref, gain_ref, *refs):
    terms, outs, sum_ref = refs[:nterms], refs[-1 - nouts : -1], refs[-1]
    u = sum_terms(terms)
    v = v_ref[...].astype(F32)
    q = lax.rsqrt(jnp.mean(v * v, axis=-1, keepdims=True) + NORM_EPS)
    ug = u * gain_ref[...]
    inner = jnp.mean(ug * v, axis=-1, keepdims=True)
    grad = first_ref[...].astype(F32) + (q * ug - v * (q * q * q * inner))
    for out in outs:
        out[...] = grad.astype(out.dtype)

    @pl.when(pl.program_id(0) == 0)
    def _():
        sum_ref[...] = jnp.zeros_like(sum_ref)

    sum_ref[...] += jnp.sum(u * v * q, axis=0, keepdims=True)


def norm_back(first, v, gain, terms, group=None, groups=None, into=None):
    rows, width = v.shape
    tile = min(128, rows)
    blk = pl.BlockSpec((tile, width), lambda i: (i, 0))
    if group is None:
        specs, shapes, old = [blk, blk], [sds((rows, width), F32), sds((rows, width), BF)], []
    else:
        spec, shape, old = place(group, groups, rows, tile, width, into)
        specs, shapes = [spec], [shape]
    return call(
        functools.partial(norm_back_kernel, len(terms), len(specs)),
        (rows // tile,),
        [blk, blk, whole_spec(gain.shape)] + [blk] * len(terms) + [ANY] * len(old),
        specs + [pl.BlockSpec((1, width), lambda i: (0, 0))],
        shapes + [sds((1, width), F32)],
        nbytes=rows * width * (12 + 2 * len(terms)),
        aliases={3 + len(terms): 0} if old else None,
    )(first, v, gain, *terms, *old)


def wgrad_rows_kernel(groups, which, *refs):
    nlhs = groups * (max(which) + 1)
    lhs, rhs, out_ref = refs[:nlhs], refs[nlhs : nlhs + groups * len(which)], refs[-1]
    tile = lhs[0].shape[2]
    left = [a[...].reshape(-1, tile).T for a in lhs]
    for c, w in enumerate(which):
        total = None
        for g in range(groups):
            a = left[w * groups + g]
            term = dot(a, rhs[c * groups + g][...].reshape(a.shape[1], -1))
            total = term if total is None else total + term
        out_ref[0, c] = total.astype(BF)


def wgrad_rows(lhs, rhs, which, nd, lo=0, hi=None, into=None):
    hi = nd if hi is None else hi
    groups = len(lhs[0])
    nt, rows, width = lhs[0][0].shape
    ds = width // nd
    n = rhs[0][0].shape[2]
    old = [] if into is None else [into]
    return call(
        functools.partial(wgrad_rows_kernel, groups, which),
        (hi - lo,),
        [pl.BlockSpec((nt, rows, ds), lambda j: (0, 0, j + lo))] * (groups * len(lhs))
        + [whole_spec(a.shape) for r in rhs for a in r]
        + [ANY] * len(old),
        pl.BlockSpec((1, len(rhs), ds, n), lambda j: (j + lo, 0, 0, 0)),
        sds((nd, len(rhs), ds, n), BF),
        flops=2 * groups * nt * rows * ds * (hi - lo) * n * len(rhs),
        nbytes=2 * groups * nt * rows * (width + n * len(rhs)) + 2 * width * n * len(rhs),
        aliases={groups * (len(lhs) + len(rhs)): 0} if old else None,
    )(*[a for l in lhs for a in l], *[a for r in rhs for a in r], *old)


def wgrad_cols_kernel(groups, nd, *refs):
    lhs, rhs, out_ref = refs[:groups], refs[groups:-1], refs[-1]
    tile = lhs[0].shape[2]
    ds = out_ref.shape[2]
    left = [a[...].reshape(-1, tile).T for a in lhs]
    total = None
    for g in range(groups):
        term = dot(left[g], rhs[g][...].reshape(left[g].shape[1], -1))
        total = term if total is None else total + term
    for j in range(nd):
        out_ref[j] = total[:, j * ds : (j + 1) * ds].astype(BF)


def wgrad_cols(lhs, rhs, nd):
    groups = len(lhs)
    nt, rows, m = lhs[0].shape
    width = rhs[0].shape[2]
    tile = min(256, m)
    return call(
        functools.partial(wgrad_cols_kernel, groups, nd),
        (m // tile,),
        [pl.BlockSpec((nt, rows, tile), lambda i: (0, 0, i))] * groups
        + [whole_spec(a.shape) for a in rhs],
        pl.BlockSpec((nd, tile, width // nd), lambda i: (0, i, 0)),
        sds((nd, m, width // nd), BF),
        flops=2 * groups * nt * rows * width * m,
        nbytes=2 * groups * nt * rows * (width + m) + 2 * width * m,
    )(*lhs, *rhs)


def doc_starts(segments):
    row_len = segments.shape[-1]
    ids = jnp.arange(row_len, dtype=jnp.int32)
    change = jnp.concatenate(
        [jnp.ones_like(segments[:, :1], dtype=bool), segments[:, 1:] != segments[:, :-1]], axis=1
    )
    return lax.cummax(jnp.where(change, ids[None, :], 0), axis=1)


def slot_order(blocks, index, nt):
    if nt != 4:
        return blocks
    pairs = jnp.stack([blocks[:, 1], blocks[:, 0], blocks[:, 3], blocks[:, 2]], axis=1)
    blocks = jnp.where(index % 2 == 1, pairs, blocks)
    halves = jnp.stack([blocks[:, 2], blocks[:, 3], blocks[:, 0], blocks[:, 1]], axis=1)
    return jnp.where(index // 2 == 1, halves, blocks)


def per_device(nd, nt, groups, layer_input, segments, qkv_w, out_w, gain1, gateup_w, down_w, gain2, grad_out):
    seqs, local, width = layer_input.shape
    per = seqs // groups
    index = lax.axis_index("tensor").astype(jnp.int32)
    blocks = jnp.arange(nt, dtype=jnp.int32)
    slot_of = blocks ^ index if nt == 4 else blocks

    x = [layer_input[g * per : (g + 1) * per].reshape(per * local, width) for g in range(groups)]
    go = [grad_out[g * per : (g + 1) * per].reshape(per * local, width) for g in range(groups)]
    Order.last = None
    x_all = [Gather(a, nt) for a in x]

    gains = lax.all_gather(jnp.stack([gain1, gain2]), "dp", axis=1, tiled=True).astype(F32)
    g1, g2 = gains[:1], gains[1:]
    qkvo_w = jnp.concatenate([qkv_w, out_w.T[None]])
    full_qkvo = lax.all_gather(qkvo_w, "dp", axis=0, tiled=False)
    full_gateup = lax.all_gather(gateup_w, "dp", axis=0, tiled=False)
    full_down = lax.all_gather(down_w, "dp", axis=0, tiled=False)

    start_abs = doc_starts(segments)
    pos_abs = jnp.arange(segments.shape[1], dtype=jnp.int32)[None, :] - start_abs
    start_slot = slot_order(start_abs.reshape(seqs, nt, local), index, nt)
    pos_slot = slot_order(pos_abs.reshape(seqs, nt, local), index, nt)
    inv_freq = ROPE_BASE ** (-jnp.arange(HALF, dtype=F32) * 2.0 / HEAD_DIM)
    angles = pos_slot.astype(F32)[..., None] * inv_freq
    cos, sin = jnp.cos(angles), jnp.sin(angles)
    cos = jnp.concatenate([cos] * 4, axis=-1)
    sin = jnp.concatenate([-sin, sin] * 2, axis=-1)

    def table(t, g):
        t = t[g * per : (g + 1) * per]
        return jnp.swapaxes(t, 0, 1).reshape(nt, per * local, PAIR)

    coss = [table(cos, g) for g in range(groups)]
    sins = [table(sin, g) for g in range(groups)]
    starts = [start_slot[g * per : (g + 1) * per] for g in range(groups)]

    both = range(groups)
    qkv, ctx, lse, mid, low2, g_mid, g_low = ({} for _ in range(7))
    attn_sum, a2_all, ga2, out_sum, ga1 = ({} for _ in range(5))
    sum1, sum2, gm_all, gmf, g_qkv = ({} for _ in range(5))

    def dp_sum(grad):
        return lax.psum_scatter(grad, "dp", scatter_dimension=0, tiled=False)

    def project(g):
        qkv[g] = project_qkv(a1[g], full_qkvo, coss[g], sins[g], nt)

    def attend(g):
        ctx[g], lse[g] = attention_forward(qkv[g], starts[g], slot_of, nt)
        attn_sum[g] = Scatter(mm_back([ctx[g]], full_qkvo, [3], nt, 4), nt)

    def middle(g):
        mid[g], low2[g] = make_middle(x[g], g2, attn_sum[g].terms)
        a2_all[g] = Gather(low2[g], nt)

    def second_back(g):
        ga2[g] = Scatter(mm_back([gg[g], gu[g]], full_gateup, [0, 1], nt, 2), nt)

    def project_out(g):
        out_sum[g] = Scatter(mm_cols(hid[g], full_down, nt, 2), nt)

    def residual_back(g):
        g_mid[g], g_low[g], sum2[g] = norm_back(go[g], mid[g], g2, ga2[g].terms)
        gm_all[g] = Gather(g_low[g], nt)

    def attention_back(g):
        gmf[g], g_ctx = context_back(gm_all[g].pieces, full_qkvo, 3, nt)
        g_qkv[g] = attention_backward(
            qkv[g], g_ctx, starts[g], lse[g], coss[g], sins[g], slot_of, nt
        )

    def input_back(g):
        ga1[g] = Scatter(mm_back(g_qkv[g], full_qkvo, [0, 1, 2], nt, 4), nt)

    for g in both:
        x_all[g].second()
    a1 = [assemble(x_all[g].pieces, nt, g1) for g in both]
    go_all = [Gather(link(go[g], a1[-1]), nt) for g in both]
    project(0)
    attend(0)
    project(1)
    attn_sum[0].second()
    go_all[0].second()
    attend(1)
    go_all[1].second()
    middle(0)
    attn_sum[1].second()
    a2_all[0].second()
    middle(1)
    gof = [assemble(go_all[g].pieces, nt) for g in both]
    a2_all[1].second()

    a2, gate, up, hid = zip(*[gate_up(a2_all[g].pieces, full_gateup, nt) for g in both])
    grad_down = dp_sum(wgrad_cols(hid, gof, nd))
    gg, gu = zip(*[gate_back(gof[g], full_down, gate[g], up[g], nt) for g in both])
    grad_gateup = wgrad_rows([a2], [gg, gu], [0, 0], nd, 0, nd // 2)
    grad_gateup = wgrad_rows([a2], [gg, gu], [0, 0], nd, nd // 2, nd, grad_gateup)
    grad_gateup = dp_sum(link(grad_gateup, grad_down))
    second_back(0)
    second_back(1)
    ga2[0].second()
    project_out(0)
    ga2[1].second()
    residual_back(0)
    project_out(1)
    gm_all[0].second()
    residual_back(1)
    out_sum[0].second()
    attention_back(0)
    gm_all[1].second()
    input_back(0)
    attention_back(1)
    ga1[0].second()
    input_back(1)
    grad_qkvo = wgrad_rows(
        [a1, [gmf[g] for g in both]],
        [[g_qkv[g][c] for g in both] for c in range(3)] + [[ctx[g] for g in both]],
        [0, 0, 0, 1],
        nd,
    )
    out_sum[1].second()
    grad_qkvo = dp_sum(link(grad_qkvo, grad_gateup))
    layer_out = layer_out_rows(mid[0], out_sum[0].terms, 0, groups, None)
    grad_input, sum1[0] = norm_back(g_mid[0], x[0], g1, ga1[0].terms, 0, groups, None)
    ga1[1].second()
    layer_out = layer_out_rows(mid[1], out_sum[1].terms, 1, groups, layer_out)
    grad_input, sum1[1] = norm_back(g_mid[1], x[1], g1, ga1[1].terms, 1, groups, grad_input)

    gain_sums = jnp.concatenate([sum1[0] + sum1[1], sum2[0] + sum2[1]], axis=0)
    gain_sums = lax.psum(gain_sums, ("dp", "tensor"))
    ds = gain1.shape[0]
    mine = lax.dynamic_slice_in_dim(gain_sums, lax.axis_index("dp") * ds, ds, 1)
    return (
        layer_out.reshape(seqs, local, width),
        grad_input.reshape(seqs, local, width),
        grad_qkvo[:3].astype(F32),
        grad_qkvo[3].T.astype(F32),
        mine[0],
        grad_gateup.astype(F32),
        grad_down.astype(F32),
        mine[1],
    )


def solution(mesh):
    nd, nt = mesh.shape["dp"], mesh.shape["tensor"]
    return jax.shard_map(
        functools.partial(per_device, nd, nt, 2),
        mesh=mesh,
        in_specs=(
            P("dp", "tensor", None),
            P("dp", None),
            P(None, "dp", "tensor"),
            P("tensor", "dp"),
            P("dp"),
            P(None, "dp", "tensor"),
            P("tensor", "dp"),
            P("dp"),
            P("dp", "tensor", None),
        ),
        out_specs=(
            P("dp", "tensor", None),
            P("dp", "tensor", None),
            P(None, "dp", "tensor"),
            P("tensor", "dp"),
            P("dp"),
            P(None, "dp", "tensor"),
            P("tensor", "dp"),
            P("dp"),
        ),
        check_vma=False,
    )
```

```python
import functools

import jax
import jax.numpy as jnp
import numpy as np
from jax import lax
from jax.experimental import pallas as pl
from jax.experimental.pallas import tpu as pltpu
from jax.sharding import PartitionSpec as P

HEAD_DIM = 64
HALF = HEAD_DIM // 2
PAIR = 2 * HEAD_DIM
NORM_EPS = 1e-05
ROPE_BASE = 130000.0
MASKED_SCORE = -1e30
BF = jnp.bfloat16
F32 = jnp.float32
VMEM_SLACK = 8 * 1024 * 1024
VMEM_SMALL = 24 * 1024 * 1024
VMEM_LARGE = 44 * 1024 * 1024
PIN_BYTES = 3 * 1024 * 1024
SMALL = 3

NT = (((1,), (1,)), ((), ()))


def dot(a, b):
    return jnp.dot(a, b, preferred_element_type=F32)


def dot_nt(a, b):
    return lax.dot_general(a, b, NT, preferred_element_type=F32)


class Order:
    last = None


HBM = pl.BlockSpec(memory_space=pltpu.HBM)
ANY = pl.BlockSpec(memory_space=pl.ANY)


def is_large(array):
    return array.size * array.dtype.itemsize >= PIN_BYTES


def pin(array):
    return pltpu.with_memory_space_constraint(array, pltpu.HBM) if is_large(array) else array


def pinned(shape):
    return pltpu.HBM(shape.shape, shape.dtype) if is_large(shape) else shape


def block_bytes(spec, dtype):
    if spec.block_shape is None:
        return 0
    count = 2 if spec.pipeline_mode is None else spec.pipeline_mode.buffer_count
    return count * int(np.prod([d for d in spec.block_shape if d])) * np.dtype(dtype).itemsize


def call(body, grid, in_specs, out_specs, out_shape, scratch=(), flops=0, nbytes=0, aliases=None, prefetch=0):
    first_extra = prefetch + len(in_specs)
    many = isinstance(out_shape, (list, tuple))
    out_blocks = list(zip(out_specs, out_shape)) if many else [(out_specs, out_shape)]

    def run(*args):
        extra = [] if Order.last is None or any(a is Order.last for a in args) else [pin(Order.last)]

        blocks = list(zip(in_specs, args[prefetch:])) + out_blocks
        vmem = VMEM_SLACK + sum(block_bytes(spec, a.dtype) for spec, a in blocks)
        vmem += sum(int(np.prod(m.shape)) * np.dtype(m.dtype).itemsize for m in scratch)
        if vmem > VMEM_SMALL:
            vmem = VMEM_LARGE

        args = [pin(a) for a in args]

        def ordered_body(*refs):
            body(*refs[:first_extra], *refs[first_extra + len(extra) :])

        outs = pl.pallas_call(
            ordered_body,
            grid_spec=pltpu.PrefetchScalarGridSpec(
                num_scalar_prefetch=prefetch,
                grid=grid,
                in_specs=in_specs + [ANY] * len(extra),
                out_specs=out_specs,
                scratch_shapes=list(scratch),
            ),
            out_shape=[pinned(a) for a in out_shape] if many else pinned(out_shape),
            input_output_aliases=aliases or {},
            cost_estimate=pl.CostEstimate(flops=flops // SMALL, bytes_accessed=nbytes // SMALL, transcendentals=0),
            compiler_params=pltpu.CompilerParams(vmem_limit_bytes=vmem),
        )(*args, *extra)
        Order.last = outs[-1] if isinstance(outs, (list, tuple)) else outs
        return outs

    return run


def link_kernel(value_ref, done_ref, out_ref):
    pass


def link(value, done):
    return call(link_kernel, (1,), [HBM, HBM], HBM, sds(value.shape, value.dtype), aliases={0: 0})(value, done)


def whole_spec(shape, buffers=1):
    zeros = (0,) * len(shape)
    return pl.BlockSpec(shape, lambda *_: zeros, pipeline_mode=pl.Buffered(buffers))


def sds(shape, dtype):
    return jax.ShapeDtypeStruct(shape, dtype)


def swap_perm(count, bit):
    return [(i, i ^ bit) for i in range(count)]


def halves_kernel(y_ref, x_ref, left_ref, right_ref):
    left_ref[...] = y_ref[...]
    right_ref[...] = x_ref[...]


def halves(from_y, from_x):
    rows, width = from_y.shape
    half = width // 2
    tile = min(128, rows)

    def spec(which):
        return pl.BlockSpec((tile, half), lambda i: (i, which))

    return call(
        halves_kernel,
        (rows // tile,),
        [spec(0), spec(1)],
        [spec(0), spec(0)],
        [sds((rows, half), BF)] * 2,
        nbytes=rows * half * 8,
    )(from_y, from_x)


class Gather:
    def __init__(self, block, nt):
        self.nt = nt
        if nt != 4:
            full = lax.all_gather(block, "tensor", axis=0, tiled=False)
            self.pieces = [(full[r],) for r in range(nt)]
            return
        self.block = block
        self.from_x = lax.ppermute(block, "tensor", swap_perm(4, 1))
        self.from_y = lax.ppermute(block, "tensor", swap_perm(4, 2))

    def second(self):
        if self.nt != 4:
            return
        left, right = halves(self.from_y, self.from_x)
        diag_x = lax.ppermute(left, "tensor", swap_perm(4, 1))
        diag_y = lax.ppermute(right, "tensor", swap_perm(4, 2))
        self.pieces = [(self.block,), (self.from_x,), (self.from_y,), (diag_x, diag_y)]


def add_halves_kernel(x_ref, for_x_ref, y_ref, for_y_ref, out_x_ref, out_y_ref):
    out_x_ref[...] = (x_ref[...].astype(F32) + for_x_ref[...].astype(F32)).astype(BF)
    out_y_ref[...] = (y_ref[...].astype(F32) + for_y_ref[...].astype(F32)).astype(BF)


def add_halves(to_x, for_x, to_y, for_y):
    rows, width = to_x.shape
    half = width // 2
    tile = min(128, rows)

    def spec(which):
        return pl.BlockSpec((tile, half), lambda i: (i, which))

    return call(
        add_halves_kernel,
        (rows // tile,),
        [spec(1), spec(0), spec(0), spec(0)],
        [spec(1), spec(0)],
        [sds(to_x.shape, BF)] * 2,
        nbytes=rows * half * 12,
        aliases={0: 0, 2: 1},
    )(to_x, for_x, to_y, for_y)


class Scatter:
    def __init__(self, parts, nt):
        self.nt = nt
        if nt != 4:
            full = jnp.stack([p[0] for p in parts])
            self.terms = [lax.psum_scatter(full, "tensor", scatter_dimension=0, tiled=False)]
            return
        (self.own,), (self.to_x,), (self.to_y,), (diag_x, diag_y) = parts
        self.for_y = lax.ppermute(diag_x, "tensor", swap_perm(4, 1))
        self.for_x = lax.ppermute(diag_y, "tensor", swap_perm(4, 2))

    def second(self):
        if self.nt != 4:
            return
        to_x, to_y = add_halves(self.to_x, self.for_x, self.to_y, self.for_y)
        self.terms = [
            self.own,
            lax.ppermute(to_x, "tensor", swap_perm(4, 1)),
            lax.ppermute(to_y, "tensor", swap_perm(4, 2)),
        ]


def piece_shapes(nt, rows, width):
    if nt != 4:
        return [((rows, width),)] * nt
    return [((rows, width),)] * 3 + [((rows, width // 2),) * 2]


def flat(pieces):
    return [a for p in pieces for a in p]


def regroup(items, nt):
    if nt != 4:
        return [(a,) for a in items]
    return [(items[0],), (items[1],), (items[2],), (items[3], items[4])]


def fill_from_pieces(refs, full_ref, nt):
    for slot, part in enumerate(regroup(refs, nt)):
        if len(part) == 1:
            full_ref[slot] = part[0][...]
        else:
            half = part[0].shape[1]
            full_ref[slot, :, :half] = part[0][...]
            full_ref[slot, :, half:] = part[1][...]


def out_piece_specs(nt, rows, width, step):
    specs = []
    half_steps = width // step // 2
    for part in piece_shapes(nt, rows, width):
        if len(part) == 1:
            specs.append(pl.BlockSpec((rows, step), lambda j: (0, j)))
        else:
            specs.append(pl.BlockSpec((rows, step), lambda j: (0, jnp.minimum(j, half_steps - 1))))
            specs.append(pl.BlockSpec((rows, step), lambda j: (0, jnp.maximum(j - half_steps, 0))))
    return specs


def store_piece(outs, nt, slot, steps, value):
    part = regroup(outs, nt)[slot]
    if len(part) == 1:
        part[0][...] = value.astype(BF)
    else:
        j = pl.program_id(0)

        @pl.when(j < steps // 2)
        def _():
            part[0][...] = value.astype(BF)

        @pl.when(j >= steps // 2)
        def _():
            part[1][...] = value.astype(BF)


def turn(v):
    lane = lax.broadcasted_iota(jnp.int32, v.shape, 1)
    return jnp.where(lane % HEAD_DIM < HALF, pltpu.roll(v, PAIR - HALF, 1), pltpu.roll(v, HALF, 1))


def rotate(v, cos, sin):
    return v * cos + turn(v) * sin


def unrotate(u, cos, sin):
    return u * cos + turn(u * sin)


def assemble_kernel(nt, count, normed, *refs):
    full_ref = refs[-1]
    fill_from_pieces(refs[:count], full_ref, nt)
    if normed:
        gain = refs[count][...]
        for slot in range(nt):
            x = full_ref[slot].astype(F32)
            scale = lax.rsqrt(jnp.mean(x * x, axis=-1, keepdims=True) + NORM_EPS)
            full_ref[slot] = (x * scale * gain).astype(BF)


def assemble(pieces, nt, group, groups, gain=None, ready=()):
    rows, width = pieces[0][0].shape
    rows //= groups
    tile = min(64, rows)
    first = group * (rows // tile)
    items = flat(pieces)
    extra = [] if gain is None else [gain]
    return call(
        functools.partial(assemble_kernel, nt, len(items), len(extra)),
        (rows // tile,),
        [pl.BlockSpec((tile, a.shape[1]), lambda i: (i + first, 0)) for a in items]
        + [whole_spec(a.shape) for a in extra]
        + [ANY] * len(ready),
        pl.BlockSpec((nt, tile, width), lambda i: (0, i, 0)),
        sds((nt, rows, width), BF),
        nbytes=4 * nt * rows * width,
    )(*items, *extra, *ready)


def qkv_kernel(nt, a1_ref, w_ref, cos_ref, sin_ref, out_ref):
    cols = out_ref.shape[3]
    weight = w_ref[:, 0].reshape(-1, cols)

    @pl.when(pl.program_id(0) < 2)
    def _():
        for slot in range(nt):
            raw = dot(a1_ref[slot], weight)
            cos, sin = cos_ref[slot], sin_ref[slot]
            for p in range(cols // PAIR):
                part = slice(p * PAIR, (p + 1) * PAIR)
                out_ref[0, slot, :, part] = rotate(raw[:, part], cos, sin).astype(BF)

    @pl.when(pl.program_id(0) == 2)
    def _():
        for slot in range(nt):
            out_ref[0, slot] = dot(a1_ref[slot], weight).astype(BF)


def project_qkv(a1, weight, cos, sin, nt):
    nd, _, ds, hc = weight.shape
    _, rows, width = a1.shape
    return call(
        functools.partial(qkv_kernel, nt),
        (3,),
        [
            whole_spec(a1.shape),
            pl.BlockSpec((nd, 1, ds, hc), lambda c: (0, c, 0, 0)),
            whole_spec(cos.shape),
            whole_spec(sin.shape),
        ],
        pl.BlockSpec((1, nt, rows, hc), lambda c: (c, 0, 0, 0)),
        sds((3, nt, rows, hc), BF),
        flops=2 * nt * rows * width * hc * 3,
        nbytes=2 * (nt * rows * width + 3 * width * hc + 3 * nt * rows * hc),
    )(a1, weight, cos, sin)


def allowed_block(start, key_block, query_block, size):
    key_id = lax.broadcasted_iota(jnp.int32, (size, size), 0) + key_block * size
    ok = key_id >= start
    if key_block == query_block:
        ok &= lax.broadcasted_iota(jnp.int32, (size, size), 1) + query_block * size >= key_id
    return ok


def attn_fwd_kernel(nt, slot_ref, q_ref, k_ref, v_ref, start_ref, ctx_ref, lse_ref, vt_ref):
    size = q_ref.shape[1]
    for b in range(nt):
        vt_ref[b] = v_ref[slot_ref[b]].T
    lane = lax.broadcasted_iota(jnp.int32, (size, PAIR), 1)
    for p in range(nt):
        slot = slot_ref[p]
        q = q_ref[slot] * BF(HEAD_DIM**-0.5)
        start = start_ref[0, pl.ds(slot, 1), :]
        outs = []
        for h in range(2):
            qh = jnp.where((lane >= HEAD_DIM) == (h == 1), q, BF(0))
            scores = []
            for b in range(p + 1):
                s = dot_nt(k_ref[slot_ref[b]], qh)
                scores.append(jnp.where(allowed_block(start, b, p, size), s, MASKED_SCORE))
            top = functools.reduce(
                jnp.maximum, [jnp.max(s, axis=0, keepdims=True) for s in scores]
            )
            total = jnp.zeros((1, size), F32)
            acc = jnp.zeros((HEAD_DIM, size), F32)
            for b, s in enumerate(scores):
                e = jnp.exp(s - top)
                total += jnp.sum(e, axis=0, keepdims=True)
                acc += dot(vt_ref[b, h * HEAD_DIM : (h + 1) * HEAD_DIM, :], e.astype(BF))
            outs.append(acc / total)
            lse_ref[0, 0, pl.ds(2 * p + h, 1), :] = top + jnp.log(total)
        ctx_ref[slot] = jnp.concatenate(outs, axis=0).T.astype(BF)


def qkv_specs(nt, size):
    def spec(c):
        return pl.BlockSpec((None, nt, size, PAIR), lambda s, g, _: (c, 0, s, g))

    return [spec(c) for c in range(3)]


def attention_forward(qkv, start, slot_of, nt):
    _, _, rows, hc = qkv.shape
    seqs = start.shape[0]
    size = rows // seqs
    pairs = hc // PAIR
    blk = pl.BlockSpec((nt, size, PAIR), lambda s, g, _: (0, s, g))
    return call(
        functools.partial(attn_fwd_kernel, nt),
        (seqs, pairs),
        qkv_specs(nt, size) + [pl.BlockSpec((1, nt, size), lambda s, g, _: (s, 0, 0))],
        [blk, pl.BlockSpec((1, 1, 2 * nt, size), lambda s, g, _: (s, g, 0, 0))],
        [sds((nt, rows, hc), BF), sds((seqs, pairs, 2 * nt, size), F32)],
        scratch=[pltpu.VMEM((nt, PAIR, size), BF)],
        flops=seqs * pairs * 2 * 4 * (nt * size) ** 2 * 128,
        nbytes=8 * nt * rows * hc,
        prefetch=1,
    )(slot_of, qkv, qkv, qkv, start)


def attn_bwd_kernel(
    nt, slot_ref, q_ref, k_ref, v_ref, go_ref, start_ref, lse_ref, cos_ref, sin_ref,
    gq_ref, gk_ref, gv_ref, kt_ref, dk_ref, dv_ref,
):
    size = q_ref.shape[1]
    scale = HEAD_DIM**-0.5
    for b in range(nt):
        kt_ref[b] = k_ref[slot_ref[b]].T
    dk_ref[...] = jnp.zeros_like(dk_ref)
    dv_ref[...] = jnp.zeros_like(dv_ref)
    lane = lax.broadcasted_iota(jnp.int32, (size, PAIR), 1)
    for p in range(nt):
        slot = slot_ref[p]
        q = q_ref[slot] * BF(scale)
        go = go_ref[slot]
        start = start_ref[0, pl.ds(slot, 1), :]
        outs = []
        for h in range(2):
            mine = (lane >= HEAD_DIM) == (h == 1)
            qh = jnp.where(mine, q, BF(0))
            goh = jnp.where(mine, go, BF(0))
            lse = lse_ref[0, 0, pl.ds(2 * p + h, 1), :]
            probs, grads = [], []
            inner = jnp.zeros((1, size), F32)
            for b in range(p + 1):
                key_slot = slot_ref[b]
                s = dot_nt(k_ref[key_slot], qh)
                s = jnp.where(allowed_block(start, b, p, size), s, MASKED_SCORE)
                e = jnp.exp(s - lse)
                g = dot_nt(v_ref[key_slot], goh)
                inner += jnp.sum(e * g, axis=0, keepdims=True)
                probs.append(e)
                grads.append(g)
            dqt = jnp.zeros((HEAD_DIM, size), F32)
            for b in range(p + 1):
                ds = (probs[b] * (grads[b] - inner)).astype(BF)
                dv_ref[b] += dot(probs[b].astype(BF), goh)
                dk_ref[b] += dot(ds, qh)
                dqt += dot(kt_ref[b, h * HEAD_DIM : (h + 1) * HEAD_DIM, :], ds)
            outs.append(dqt)
        dq = jnp.concatenate(outs, axis=0).T * scale
        gq_ref[slot] = unrotate(dq, cos_ref[slot], sin_ref[slot]).astype(BF)
    for b in range(nt):
        slot = slot_ref[b]
        gk_ref[slot] = unrotate(dk_ref[b], cos_ref[slot], sin_ref[slot]).astype(BF)
        gv_ref[slot] = dv_ref[b].astype(BF)


def attention_backward(qkv, go, start, lse, cos, sin, slot_of, nt):
    _, _, rows, hc = qkv.shape
    seqs = start.shape[0]
    size = rows // seqs
    pairs = hc // PAIR
    blk = pl.BlockSpec((nt, size, PAIR), lambda s, g, _: (0, s, g))
    table = pl.BlockSpec((nt, size, PAIR), lambda s, g, _: (0, s, 0))
    return call(
        functools.partial(attn_bwd_kernel, nt),
        (seqs, pairs),
        qkv_specs(nt, size)
        + [
            blk,
            pl.BlockSpec((1, nt, size), lambda s, g, _: (s, 0, 0)),
            pl.BlockSpec((1, 1, 2 * nt, size), lambda s, g, _: (s, g, 0, 0)),
            table, table,
        ],
        [blk, blk, blk],
        [sds((nt, rows, hc), BF)] * 3,
        scratch=[
            pltpu.VMEM((nt, PAIR, size), BF),
            pltpu.VMEM((nt, size, PAIR), F32),
            pltpu.VMEM((nt, size, PAIR), F32),
        ],
        flops=seqs * pairs * 2 * 10 * (nt * size) ** 2 * 128,
        nbytes=14 * nt * rows * hc,
        prefetch=1,
    )(slot_of, qkv, qkv, qkv, go, start, lse, cos, sin)


def shard_group(nd, count):
    while nd % count or nd // count % 2:
        count //= 2
    return max(count, 1)


def cols_out_kernel(nt, steps, lhs_ref, w_ref, *outs):
    for slot in range(nt):
        lhs = lhs_ref[slot]
        parts = [dot(lhs, w_ref[j]) for j in range(w_ref.shape[0])]
        store_piece(outs, nt, slot, steps, jnp.concatenate(parts, axis=1))


def mm_cols(lhs, weight, nt, group):
    nd, depth, ds = weight.shape
    group = shard_group(nd, group)
    rows = lhs.shape[1]
    width = nd * ds
    shapes = flat(piece_shapes(nt, rows, width))
    outs = call(
        functools.partial(cols_out_kernel, nt, nd // group),
        (nd // group,),
        [whole_spec(lhs.shape), pl.BlockSpec((group, depth, ds), lambda j: (j, 0, 0))],
        out_piece_specs(nt, rows, width, group * ds),
        [sds(s, BF) for s in shapes],
        flops=2 * nt * rows * depth * width,
        nbytes=2 * (nt * rows * (depth + width) + depth * width),
    )(lhs, weight)
    return regroup(outs, nt)


def cols_back_kernel(nt, steps, nlhs, nseen, *refs):
    lhs, w_refs, outs = refs[:nlhs], refs[nlhs : 2 * nlhs], refs[2 * nlhs + nseen :]
    depth = w_refs[0].shape[3]
    weights = [w[:, 0].reshape(-1, depth) for w in w_refs]
    sums = None
    for slot in range(nt):
        total = dot_nt(lhs[0][slot], weights[0])
        for c in range(1, nlhs):
            total += dot_nt(lhs[c][slot], weights[c])
        if nseen:
            part = jnp.sum(total * refs[2 * nlhs][slot].astype(F32), axis=0, keepdims=True)
            sums = part if sums is None else sums + part
        store_piece(outs[: len(outs) - nseen], nt, slot, steps, total)
    if nseen:
        outs[-1][...] = sums


def mm_back(lhs, weight, channels, nt, group, seen=None):
    nd, _, ds, depth = weight.shape
    count = len(lhs)
    group = shard_group(nd, group)
    rows = lhs[0].shape[1]
    width = nd * ds
    shapes = flat(piece_shapes(nt, rows, width))
    step = group * ds
    more = [] if seen is None else [seen]

    def spec(c):
        return pl.BlockSpec((group, 1, ds, depth), lambda j: (j, c, 0, 0))

    outs = call(
        functools.partial(cols_back_kernel, nt, nd // group, count, len(more)),
        (nd // group,),
        [whole_spec(a.shape) for a in lhs]
        + [spec(c) for c in channels]
        + [pl.BlockSpec((nt, rows, step), lambda j: (0, 0, j)) for _ in more],
        out_piece_specs(nt, rows, width, step) + [pl.BlockSpec((1, step), lambda j: (0, j)) for _ in more],
        [sds(s, BF) for s in shapes] + [sds((1, width), F32) for _ in more],
        flops=2 * nt * rows * depth * width * count,
        nbytes=2 * (nt * rows * (depth * count + width) + depth * width * count),
    )(*lhs, *[weight] * count, *more)
    return regroup(outs[: len(shapes)], nt), outs[len(shapes) :]


def gateup_kernel(nt, *refs):
    count = len(flat(piece_shapes(nt, 8, 8)))
    pieces, w_ref, (full_ref, gate_ref, up_ref, hid_ref) = (
        refs[:count],
        refs[count],
        refs[count + 1 :],
    )

    @pl.when(pl.program_id(0) == 0)
    def _():
        fill_from_pieces(pieces, full_ref, nt)

    cols = gate_ref.shape[2]
    w_gate = w_ref[:, 0].reshape(-1, cols)
    w_up = w_ref[:, 1].reshape(-1, cols)
    for slot in range(nt):
        a2 = full_ref[slot]
        gate = dot(a2, w_gate)
        up = dot(a2, w_up)
        gate_ref[slot] = gate.astype(BF)
        up_ref[slot] = up.astype(BF)
        hid_ref[slot] = (gate * jax.nn.sigmoid(gate) * up).astype(BF)


def gate_up(pieces, weight, nt):
    nd, _, ds, ff = weight.shape
    rows, width = pieces[0][0].shape
    step = min(512, ff)
    blk = pl.BlockSpec((nt, rows, step), lambda j: (0, 0, j))
    return call(
        functools.partial(gateup_kernel, nt),
        (ff // step,),
        [whole_spec(a.shape) for a in flat(pieces)]
        + [pl.BlockSpec((nd, 2, ds, step), lambda j: (0, 0, 0, j))],
        [whole_spec((nt, rows, width)), blk, blk, blk],
        [sds((nt, rows, width), BF)] + [sds((nt, rows, ff), BF)] * 3,
        flops=4 * nt * rows * width * ff,
        nbytes=2 * (2 * nt * rows * width + 2 * width * ff + 3 * nt * rows * ff),
    )(*flat(pieces), weight)


def gate_back_kernel(nt, full_ref, w_ref, gate_ref, up_ref, gg_ref, gu_ref):
    weight = jnp.concatenate([w_ref[j] for j in range(w_ref.shape[0])], axis=1)
    for slot in range(nt):
        gh = dot_nt(full_ref[slot], weight)
        gate = gate_ref[slot].astype(F32)
        up = up_ref[slot].astype(F32)
        sig = jax.nn.sigmoid(gate)
        gg_ref[slot] = (gh * up * sig * (1.0 + gate * (1.0 - sig))).astype(BF)
        gu_ref[slot] = (gh * gate * sig).astype(BF)


def gate_back(full, weight, gate, up, nt):
    nd, ff, ds = weight.shape
    _, rows, width = full.shape
    step = min(512, ff)
    blk = pl.BlockSpec((nt, rows, step), lambda j: (0, 0, j))
    return call(
        functools.partial(gate_back_kernel, nt),
        (ff // step,),
        [whole_spec(full.shape), pl.BlockSpec((nd, step, ds), lambda j: (0, j, 0)), blk, blk],
        [blk, blk],
        [sds((nt, rows, ff), BF)] * 2,
        flops=2 * nt * rows * width * ff,
        nbytes=2 * (nt * rows * width + width * ff + 4 * nt * rows * ff),
    )(full, weight, gate, up)


def context_back_kernel(nt, *refs):
    count = len(flat(piece_shapes(nt, 8, 8)))
    pieces, w_ref, (full_ref, out_ref) = refs[:count], refs[count], refs[count + 1 :]

    @pl.when(pl.program_id(0) == 0)
    def _():
        fill_from_pieces(pieces, full_ref, nt)

    weight = w_ref[:, 0].reshape(-1, w_ref.shape[3])
    for slot in range(nt):
        out_ref[slot] = dot(full_ref[slot], weight).astype(BF)


def context_back(pieces, weight, channel, nt):
    nd, _, ds, hc = weight.shape
    rows, width = pieces[0][0].shape
    step = min(256, hc)
    return call(
        functools.partial(context_back_kernel, nt),
        (hc // step,),
        [whole_spec(a.shape) for a in flat(pieces)]
        + [pl.BlockSpec((nd, 1, ds, step), lambda j: (0, channel, 0, j))],
        [whole_spec((nt, rows, width)), pl.BlockSpec((nt, rows, step), lambda j: (0, 0, j))],
        [sds((nt, rows, width), BF), sds((nt, rows, hc), BF)],
        flops=2 * nt * rows * width * hc,
        nbytes=2 * (2 * nt * rows * width + width * hc + nt * rows * hc),
    )(*flat(pieces), weight)


def middle_kernel(nterms, x_ref, gain_ref, *refs):
    terms, (mid_ref, low_ref) = refs[:nterms], refs[nterms:]
    mid = x_ref[...].astype(F32) + sum_terms(terms)
    mid_ref[...] = mid
    scale = lax.rsqrt(jnp.mean(mid * mid, axis=-1, keepdims=True) + NORM_EPS)
    low_ref[...] = (mid * scale * gain_ref[...]).astype(BF)


def make_middle(x, gain, terms):
    rows, width = x.shape
    tile = min(128, rows)
    blk = pl.BlockSpec((tile, width), lambda i: (i, 0))
    return call(
        functools.partial(middle_kernel, len(terms)),
        (rows // tile,),
        [blk, whole_spec(gain.shape)] + [blk] * len(terms),
        [blk, blk],
        [sds((rows, width), F32), sds((rows, width), BF)],
        nbytes=rows * width * (8 + 2 * len(terms)),
    )(x, gain, *terms)


def sum_terms(terms):
    total = terms[0][...].astype(F32)
    for t in terms[1:]:
        total += t[...].astype(F32)
    return total


def layer_out_kernel(nterms, mid_ref, *refs):
    refs[-1][...] = (mid_ref[...] + sum_terms(refs[:nterms])).astype(BF)


def place(group, groups, rows, tile, width, into):
    steps = rows // tile
    spec = pl.BlockSpec((tile, width), lambda i: (i + group * steps, 0))
    return spec, sds((groups * rows, width), BF), [] if into is None else [into]


def layer_out_rows(mid, terms, group, groups, into):
    rows, width = mid.shape
    tile = min(128, rows)
    blk = pl.BlockSpec((tile, width), lambda i: (i, 0))
    spec, shape, old = place(group, groups, rows, tile, width, into)
    return call(
        functools.partial(layer_out_kernel, len(terms)),
        (rows // tile,),
        [blk] * (1 + len(terms)) + [HBM] * len(old),
        spec,
        shape,
        nbytes=rows * width * (6 + 2 * len(terms)),
        aliases={1 + len(terms): 0} if old else None,
    )(mid, *terms, *old)


def norm_back_kernel(nterms, nouts, first_ref, v_ref, gain_ref, *refs):
    terms, outs, sums = refs[:nterms], refs[len(refs) - nouts :], []
    if nouts == 3:
        outs, sums = outs[:2], outs[2:]
    u = sum_terms(terms)
    v = v_ref[...].astype(F32)
    q = lax.rsqrt(jnp.mean(v * v, axis=-1, keepdims=True) + NORM_EPS)
    ug = u * gain_ref[...]
    inner = jnp.mean(ug * v, axis=-1, keepdims=True)
    grad = first_ref[...].astype(F32) + (q * ug - v * (q * q * q * inner))
    for out in outs:
        out[...] = grad.astype(out.dtype)
    for sum_ref in sums:

        @pl.when(pl.program_id(0) == 0)
        def _():
            sum_ref[...] = jnp.zeros_like(sum_ref)

        sum_ref[...] += jnp.sum(u * v * q, axis=0, keepdims=True)


def norm_back(first, v, gain, terms):
    rows, width = v.shape
    tile = min(128, rows)
    blk = pl.BlockSpec((tile, width), lambda i: (i, 0))
    return call(
        functools.partial(norm_back_kernel, len(terms), 3),
        (rows // tile,),
        [blk, blk, whole_spec(gain.shape)] + [blk] * len(terms),
        [blk, blk, pl.BlockSpec((1, width), lambda i: (0, 0))],
        [sds((rows, width), F32), sds((rows, width), BF), sds((1, width), F32)],
        nbytes=rows * width * (12 + 2 * len(terms)),
    )(first, v, gain, *terms)


def norm_back_rows(first, v, gain, terms, group, groups, into):
    rows, width = v.shape
    tile = min(128, rows)
    blk = pl.BlockSpec((tile, width), lambda i: (i, 0))
    spec, shape, old = place(group, groups, rows, tile, width, into)
    return call(
        functools.partial(norm_back_kernel, len(terms), 1),
        (rows // tile,),
        [blk, blk, whole_spec(gain.shape)] + [blk] * len(terms) + [HBM] * len(old),
        spec,
        shape,
        nbytes=rows * width * (12 + 2 * len(terms)),
        aliases={3 + len(terms): 0} if old else None,
    )(first, v, gain, *terms, *old)


def wgrad_rows_kernel(groups, which, nmore, *refs):
    nlhs = groups * (max(which) + 1)
    lhs, rhs, out_ref = refs[:nlhs], refs[nlhs : nlhs + groups * len(which)], refs[-1]
    tile = lhs[0].shape[2]
    left = [a[...].reshape(-1, tile).T for a in lhs]
    for c, w in enumerate(which):
        total = None
        for g in range(groups):
            a = left[w * groups + g]
            term = dot(a, rhs[c * groups + g][...].reshape(a.shape[1], -1))
            total = term if total is None else total + term
        out_ref[0, c * tile : (c + 1) * tile] = total.astype(BF)
    if nmore:
        out_ref[0, len(which) * tile :] = refs[-2][0]


def wgrad_rows(lhs, rhs, which, nd, more=None):
    groups = len(lhs[0])
    nt, rows, width = lhs[0][0].shape
    ds = width // nd
    n = rhs[0][0].shape[2]
    more = [] if more is None else [more]
    height = len(rhs) * ds + sum(a.shape[1] for a in more)
    return call(
        functools.partial(wgrad_rows_kernel, groups, which, len(more)),
        (nd,),
        [pl.BlockSpec((nt, rows, ds), lambda j: (0, 0, j))] * (groups * len(lhs))
        + [whole_spec(a.shape) for r in rhs for a in r]
        + [pl.BlockSpec((1,) + a.shape[1:], lambda j: (j, 0, 0)) for a in more],
        pl.BlockSpec((1, height, n), lambda j: (j, 0, 0)),
        sds((nd, height, n), BF),
        flops=2 * groups * nt * rows * width * n * len(rhs),
        nbytes=2 * groups * nt * rows * (width + n * len(rhs)) + 2 * width * n * len(rhs),
    )(*[a for l in lhs for a in l], *[a for r in rhs for a in r], *more)


def wgrad_cols_kernel(groups, nd, *refs):
    lhs, rhs, out_ref = refs[:groups], refs[groups:-1], refs[-1]
    tile = lhs[0].shape[2]
    ds = out_ref.shape[2]
    left = [a[...].reshape(-1, tile).T for a in lhs]
    total = None
    for g in range(groups):
        term = dot(left[g], rhs[g][...].reshape(left[g].shape[1], -1))
        total = term if total is None else total + term
    for j in range(nd):
        out_ref[j] = total[:, j * ds : (j + 1) * ds].astype(BF)


def wgrad_cols(lhs, rhs, nd):
    groups = len(lhs)
    nt, rows, m = lhs[0].shape
    width = rhs[0].shape[2]
    tile = min(256, m)
    return call(
        functools.partial(wgrad_cols_kernel, groups, nd),
        (m // tile,),
        [pl.BlockSpec((nt, rows, tile), lambda i: (0, 0, i))] * groups
        + [whole_spec(a.shape) for a in rhs],
        pl.BlockSpec((nd, tile, width // nd), lambda i: (0, i, 0)),
        sds((nd, m, width // nd), BF),
        flops=2 * groups * nt * rows * width * m,
        nbytes=2 * groups * nt * rows * (width + m) + 2 * width * m,
    )(*lhs, *rhs)


def doc_starts(segments):
    row_len = segments.shape[-1]
    ids = jnp.arange(row_len, dtype=jnp.int32)
    change = jnp.concatenate(
        [jnp.ones_like(segments[:, :1], dtype=bool), segments[:, 1:] != segments[:, :-1]], axis=1
    )
    return lax.cummax(jnp.where(change, ids[None, :], 0), axis=1)


def tensor_sum(value, nt):
    if nt != 4:
        return lax.psum(value, "tensor")
    value = value + lax.ppermute(value, "tensor", swap_perm(4, 1))
    return value + lax.ppermute(value, "tensor", swap_perm(4, 2))


def slot_order(blocks, index, nt):
    if nt != 4:
        return blocks
    pairs = jnp.stack([blocks[:, 1], blocks[:, 0], blocks[:, 3], blocks[:, 2]], axis=1)
    blocks = jnp.where(index % 2 == 1, pairs, blocks)
    halves = jnp.stack([blocks[:, 2], blocks[:, 3], blocks[:, 0], blocks[:, 1]], axis=1)
    return jnp.where(index // 2 == 1, halves, blocks)


def per_device(nd, nt, groups, layer_input, segments, qkv_w, out_w, gain1, gateup_w, down_w, gain2, grad_out):
    seqs, local, width = layer_input.shape
    per = seqs // groups
    index = lax.axis_index("tensor").astype(jnp.int32)
    blocks = jnp.arange(nt, dtype=jnp.int32)
    slot_of = blocks ^ index if nt == 4 else blocks

    x = [layer_input[g * per : (g + 1) * per].reshape(per * local, width) for g in range(groups)]
    go = [grad_out[g * per : (g + 1) * per].reshape(per * local, width) for g in range(groups)]
    Order.last = None
    x_all = Gather(layer_input.reshape(seqs * local, width), nt)

    gains = lax.all_gather(jnp.stack([gain1, gain2]), "dp", axis=1, tiled=True).astype(F32)
    g1, g2 = gains[:1], gains[1:]
    qkvo_w = jnp.concatenate([qkv_w, out_w.T[None]])
    full_qkvo = lax.all_gather(qkvo_w, "dp", axis=0, tiled=False)
    full_gateup = lax.all_gather(gateup_w, "dp", axis=0, tiled=False)
    full_down = lax.all_gather(down_w, "dp", axis=0, tiled=False)

    start_abs = doc_starts(segments)
    pos_abs = jnp.arange(segments.shape[1], dtype=jnp.int32)[None, :] - start_abs
    start_slot = slot_order(start_abs.reshape(seqs, nt, local), index, nt)
    pos_slot = slot_order(pos_abs.reshape(seqs, nt, local), index, nt)
    inv_freq = ROPE_BASE ** (-jnp.arange(HALF, dtype=F32) * 2.0 / HEAD_DIM)
    angles = pos_slot.astype(F32)[..., None] * inv_freq
    cos, sin = jnp.cos(angles), jnp.sin(angles)
    cos = jnp.concatenate([cos] * 4, axis=-1)
    sin = jnp.concatenate([-sin, sin] * 2, axis=-1)

    def table(t, g):
        t = t[g * per : (g + 1) * per]
        return jnp.swapaxes(t, 0, 1).reshape(nt, per * local, PAIR)

    coss = [table(cos, g) for g in range(groups)]
    sins = [table(sin, g) for g in range(groups)]
    starts = [start_slot[g * per : (g + 1) * per] for g in range(groups)]

    both = range(groups)
    qkv, ctx, lse, mid, low2, g_mid, g_low = ({} for _ in range(7))
    attn_sum, a2_all, ga2, out_sum, ga1 = ({} for _ in range(5))
    sum1, sum2, gm_all, gmf, g_qkv = ({} for _ in range(5))

    def dp_sum(grad):
        return lax.psum_scatter(grad, "dp", scatter_dimension=0, tiled=False)

    def project(g):
        qkv[g] = project_qkv(a1[g], full_qkvo, coss[g], sins[g], nt)

    def attend(g):
        ctx[g], lse[g] = attention_forward(qkv[g], starts[g], slot_of, nt)
        attn_sum[g] = Scatter(mm_back([ctx[g]], full_qkvo, [3], nt, 4)[0], nt)

    def middle(g):
        mid[g], low2[g] = make_middle(x[g], g2, attn_sum[g].terms)
        a2_all[g] = Gather(low2[g], nt)

    def second_back(g):
        ga2[g] = Scatter(mm_back([gg[g], gu[g]], full_gateup, [0, 1], nt, 2)[0], nt)

    def project_out(g):
        out_sum[g] = Scatter(mm_cols(hid[g], full_down, nt, 2), nt)

    def residual_back(g):
        g_mid[g], g_low[g], sum2[g] = norm_back(go[g], mid[g], g2, ga2[g].terms)
        gm_all[g] = Gather(g_low[g], nt)

    def attention_back(g):
        gmf[g], g_ctx = context_back(gm_all[g].pieces, full_qkvo, 3, nt)
        g_qkv[g] = attention_backward(
            qkv[g], g_ctx, starts[g], lse[g], coss[g], sins[g], slot_of, nt
        )

    def input_back(g):
        parts, (sum1[g],) = mm_back(g_qkv[g], full_qkvo, [0, 1, 2], nt, 4, a1[g])
        ga1[g] = Scatter(parts, nt)

    def up_projection(g):
        a2[g], gate[g], up[g], hid[g] = gate_up(a2_all[g].pieces, full_gateup, nt)

    def hidden_back(g):
        gg[g], gu[g] = gate_back(gof[g], full_down, gate[g], up[g], nt)

    def finish(g, grad_input):
        return norm_back_rows(g_mid[g], x[g], g1, ga1[g].terms, g, groups, grad_input)

    def by_group(held):
        return [held[g] for g in both]

    a2, gate, up, hid, gg, gu = ({} for _ in range(6))
    x_all.second()
    a1 = [assemble(x_all.pieces, nt, 0, groups, g1, coss + sins)]
    go_all = Gather(link(grad_out.reshape(seqs * local, width), a1[0]), nt)
    project(0)
    attend(0)
    a1.append(assemble(x_all.pieces, nt, 1, groups, g1))
    project(1)
    go_all.second()
    attn_sum[0].second()
    attend(1)
    middle(0)
    attn_sum[1].second()
    a2_all[0].second()
    middle(1)
    up_projection(0)
    a2_all[1].second()
    gof = [assemble(go_all.pieces, nt, g, groups) for g in both]
    up_projection(1)
    hidden_back(0)
    grad_down = dp_sum(wgrad_cols(by_group(hid), gof, nd))
    second_back(0)
    hidden_back(1)
    ga2[0].second()
    second_back(1)
    residual_back(0)
    grad_gateup = wgrad_rows([by_group(a2)], [by_group(gg), by_group(gu)], [0, 0], nd)
    grad_gateup = dp_sum(link(grad_gateup, grad_down))
    ga2[1].second()
    project_out(1)
    gm_all[0].second()
    residual_back(1)
    project_out(0)
    attention_back(0)
    gm_all[1].second()
    input_back(0)
    out_sum[1].second()
    attention_back(1)
    ga1[0].second()
    input_back(1)
    ds = gain1.shape[0]
    gains = tensor_sum(jnp.concatenate([(sum1[0] + sum1[1]) / g1, sum2[0] + sum2[1]]), nt)
    gains = jnp.swapaxes(gains.reshape(2, nd, ds), 0, 1).astype(BF)
    gains = jnp.pad(gains, ((0, 0), (0, 14), (0, qkv_w.shape[2] - ds)))
    out_sum[0].second()
    grad_qkvo = wgrad_rows(
        [a1, by_group(gmf)],
        [[g_qkv[g][c] for g in both] for c in range(3)] + [by_group(ctx)],
        [0, 0, 0, 1],
        nd,
        gains,
    )
    grad_qkvo = dp_sum(link(grad_qkvo, grad_gateup))
    layer_out = layer_out_rows(mid[1], out_sum[1].terms, 1, groups, None)
    ga1[1].second()
    grad_input = finish(0, None)
    layer_out = layer_out_rows(mid[0], out_sum[0].terms, 0, groups, layer_out)
    grad_input = finish(1, grad_input)
    return (
        layer_out.reshape(seqs, local, width),
        grad_input.reshape(seqs, local, width),
        grad_qkvo[: 3 * ds].astype(F32).reshape(3, ds, -1),
        grad_qkvo[3 * ds : 4 * ds].T.astype(F32),
        grad_qkvo[4 * ds, :ds].astype(F32),
        grad_gateup.astype(F32).reshape(2, ds, -1),
        grad_down.astype(F32),
        grad_qkvo[4 * ds + 1, :ds].astype(F32),
    )


def solution(mesh):
    nd, nt = mesh.shape["dp"], mesh.shape["tensor"]
    return jax.shard_map(
        functools.partial(per_device, nd, nt, 2),
        mesh=mesh,
        in_specs=(
            P("dp", "tensor", None),
            P("dp", None),
            P(None, "dp", "tensor"),
            P("tensor", "dp"),
            P("dp"),
            P(None, "dp", "tensor"),
            P("tensor", "dp"),
            P("dp"),
            P("dp", "tensor", None),
        ),
        out_specs=(
            P("dp", "tensor", None),
            P("dp", "tensor", None),
            P(None, "dp", "tensor"),
            P("tensor", "dp"),
            P("dp"),
            P(None, "dp", "tensor"),
            P("tensor", "dp"),
            P("dp"),
        ),
        check_vma=False,
    )
```

```python
import functools

import jax
import jax.numpy as jnp
import numpy as np
from jax import lax
from jax.experimental import pallas as pl
from jax.experimental.pallas import tpu as pltpu
from jax.sharding import PartitionSpec as P

HEAD_DIM = 64
HALF = HEAD_DIM // 2
PAIR = 2 * HEAD_DIM
NORM_EPS = 1e-05
ROPE_BASE = 130000.0
MASKED_SCORE = -1e30
BF = jnp.bfloat16
F32 = jnp.float32
VMEM_SLACK = 8 * 1024 * 1024
VMEM_SMALL = 24 * 1024 * 1024
VMEM_LARGE = 40 * 1024 * 1024
PIN_BYTES = 3 * 1024 * 1024
PIN_BYTES_LARGE = 1024 * 1024
SMALL = 3

NT = (((1,), (1,)), ((), ()))


def dot(a, b):
    return jnp.dot(a, b, preferred_element_type=F32)


def dot_nt(a, b):
    return lax.dot_general(a, b, NT, preferred_element_type=F32)


class Order:
    last = None


HBM = pl.BlockSpec(memory_space=pltpu.HBM)
ANY = pl.BlockSpec(memory_space=pl.ANY)


def is_large(array, least=None):
    return array.size * array.dtype.itemsize >= (least or PIN_BYTES)


def pin(array, least=None):
    return pltpu.with_memory_space_constraint(array, pltpu.HBM) if is_large(array, least) else array


def pinned(shape):
    return pltpu.HBM(shape.shape, shape.dtype) if is_large(shape) else shape


def block_bytes(spec, dtype):
    if spec.block_shape is None:
        return 0
    count = 2 if spec.pipeline_mode is None else spec.pipeline_mode.buffer_count
    return count * int(np.prod([d for d in spec.block_shape if d])) * np.dtype(dtype).itemsize


def call(body, grid, in_specs, out_specs, out_shape, scratch=(), flops=0, nbytes=0, aliases=None, prefetch=0):
    first_extra = prefetch + len(in_specs)
    many = isinstance(out_shape, (list, tuple))
    out_blocks = list(zip(out_specs, out_shape)) if many else [(out_specs, out_shape)]

    def run(*args):
        extra = [] if Order.last is None or any(a is Order.last for a in args) else [pin(Order.last)]

        blocks = list(zip(in_specs, args[prefetch:])) + out_blocks
        vmem = VMEM_SLACK + sum(block_bytes(spec, a.dtype) for spec, a in blocks)
        vmem += sum(int(np.prod(m.shape)) * np.dtype(m.dtype).itemsize for m in scratch)
        least = PIN_BYTES
        if vmem > VMEM_SMALL:
            vmem, least = VMEM_LARGE, PIN_BYTES_LARGE

        args = [pin(a, least) for a in args]

        def ordered_body(*refs):
            body(*refs[:first_extra], *refs[first_extra + len(extra) :])

        outs = pl.pallas_call(
            ordered_body,
            grid_spec=pltpu.PrefetchScalarGridSpec(
                num_scalar_prefetch=prefetch,
                grid=grid,
                in_specs=in_specs + [ANY] * len(extra),
                out_specs=out_specs,
                scratch_shapes=list(scratch),
            ),
            out_shape=[pinned(a) for a in out_shape] if many else pinned(out_shape),
            input_output_aliases=aliases or {},
            cost_estimate=pl.CostEstimate(flops=flops // SMALL, bytes_accessed=nbytes // SMALL, transcendentals=0),
            compiler_params=pltpu.CompilerParams(vmem_limit_bytes=vmem),
        )(*args, *extra)
        Order.last = outs[-1] if isinstance(outs, (list, tuple)) else outs
        return outs

    return run


def link_kernel(value_ref, done_ref, out_ref):
    pass


def link(value, done):
    return call(link_kernel, (1,), [HBM, HBM], HBM, sds(value.shape, value.dtype), aliases={0: 0})(value, done)


def whole_spec(shape, buffers=1):
    zeros = (0,) * len(shape)
    return pl.BlockSpec(shape, lambda *_: zeros, pipeline_mode=pl.Buffered(buffers))


def sds(shape, dtype):
    return jax.ShapeDtypeStruct(shape, dtype)


def swap_perm(count, bit):
    return [(i, i ^ bit) for i in range(count)]


def halves_kernel(y_ref, x_ref, left_ref, right_ref):
    left_ref[...] = y_ref[...]
    right_ref[...] = x_ref[...]


def halves(from_y, from_x):
    rows, width = from_y.shape
    half = width // 2
    tile = min(128, rows)

    def spec(which):
        return pl.BlockSpec((tile, half), lambda i: (i, which))

    return call(
        halves_kernel,
        (rows // tile,),
        [spec(0), spec(1)],
        [spec(0), spec(0)],
        [sds((rows, half), BF)] * 2,
        nbytes=rows * half * 8,
    )(from_y, from_x)


class Gather:
    def __init__(self, block, nt, direct=False):
        self.nt = nt
        if nt != 4:
            full = lax.all_gather(block, "tensor", axis=0, tiled=False)
            self.pieces = [(full[r],) for r in range(nt)]
            return
        self.block = block
        self.from_x = lax.ppermute(block, "tensor", swap_perm(4, 1))
        self.from_y = lax.ppermute(block, "tensor", swap_perm(4, 2))
        if direct:
            diag = lax.ppermute(block, "tensor", swap_perm(4, 3))
            self.pieces = [(block,), (self.from_x,), (self.from_y,), (diag,)]

    def second(self):
        if self.nt != 4:
            return
        left, right = halves(self.from_y, self.from_x)
        diag_x = lax.ppermute(left, "tensor", swap_perm(4, 1))
        diag_y = lax.ppermute(right, "tensor", swap_perm(4, 2))
        self.pieces = [(self.block,), (self.from_x,), (self.from_y,), (diag_x, diag_y)]


def add_halves_kernel(x_ref, for_x_ref, y_ref, for_y_ref, out_x_ref, out_y_ref):
    out_x_ref[...] = (x_ref[...].astype(F32) + for_x_ref[...].astype(F32)).astype(BF)
    out_y_ref[...] = (y_ref[...].astype(F32) + for_y_ref[...].astype(F32)).astype(BF)


def add_halves(to_x, for_x, to_y, for_y):
    rows, width = to_x.shape
    half = width // 2
    tile = min(128, rows)

    def spec(which):
        return pl.BlockSpec((tile, half), lambda i: (i, which))

    return call(
        add_halves_kernel,
        (rows // tile,),
        [spec(1), spec(0), spec(0), spec(0)],
        [spec(1), spec(0)],
        [sds(to_x.shape, BF)] * 2,
        nbytes=rows * half * 12,
        aliases={0: 0, 2: 1},
    )(to_x, for_x, to_y, for_y)


class Scatter:
    def __init__(self, parts, nt):
        self.nt = nt
        if nt != 4:
            full = jnp.stack([p[0] for p in parts])
            self.terms = [lax.psum_scatter(full, "tensor", scatter_dimension=0, tiled=False)]
            return
        (self.own,), (self.to_x,), (self.to_y,), (diag_x, diag_y) = parts
        self.for_y = lax.ppermute(diag_x, "tensor", swap_perm(4, 1))
        self.for_x = lax.ppermute(diag_y, "tensor", swap_perm(4, 2))

    def second(self):
        if self.nt != 4:
            return
        to_x, to_y = add_halves(self.to_x, self.for_x, self.to_y, self.for_y)
        self.terms = [
            self.own,
            lax.ppermute(to_x, "tensor", swap_perm(4, 1)),
            lax.ppermute(to_y, "tensor", swap_perm(4, 2)),
        ]


def piece_shapes(nt, rows, width):
    if nt != 4:
        return [((rows, width),)] * nt
    return [((rows, width),)] * 3 + [((rows, width // 2),) * 2]


def flat(pieces):
    return [a for p in pieces for a in p]


def regroup(items, nt):
    if len(items) == nt:
        return [(a,) for a in items]
    return [(items[0],), (items[1],), (items[2],), (items[3], items[4])]


def fill_from_pieces(refs, full_ref, nt):
    for slot, part in enumerate(regroup(refs, nt)):
        if len(part) == 1:
            full_ref[slot] = part[0][...]
        else:
            half = part[0].shape[1]
            full_ref[slot, :, :half] = part[0][...]
            full_ref[slot, :, half:] = part[1][...]


def out_piece_specs(nt, rows, width, step):
    specs = []
    half_steps = width // step // 2
    for part in piece_shapes(nt, rows, width):
        if len(part) == 1:
            specs.append(pl.BlockSpec((rows, step), lambda j: (0, j)))
        else:
            specs.append(pl.BlockSpec((rows, step), lambda j: (0, jnp.minimum(j, half_steps - 1))))
            specs.append(pl.BlockSpec((rows, step), lambda j: (0, jnp.maximum(j - half_steps, 0))))
    return specs


def store_piece(outs, nt, slot, steps, value):
    part = regroup(outs, nt)[slot]
    if len(part) == 1:
        part[0][...] = value.astype(BF)
    else:
        j = pl.program_id(0)

        @pl.when(j < steps // 2)
        def _():
            part[0][...] = value.astype(BF)

        @pl.when(j >= steps // 2)
        def _():
            part[1][...] = value.astype(BF)


def turn(v):
    lane = lax.broadcasted_iota(jnp.int32, v.shape, 1)
    return jnp.where(lane % HEAD_DIM < HALF, pltpu.roll(v, PAIR - HALF, 1), pltpu.roll(v, HALF, 1))


def rotate(v, cos, sin):
    return v * cos + turn(v) * sin


def unrotate(u, cos, sin):
    return u * cos + turn(u * sin)


def assemble_kernel(nt, count, normed, *refs):
    full_ref = refs[-1]
    fill_from_pieces(refs[:count], full_ref, nt)
    if normed:
        gain = refs[count][...]
        for slot in range(nt):
            x = full_ref[slot].astype(F32)
            scale = lax.rsqrt(jnp.mean(x * x, axis=-1, keepdims=True) + NORM_EPS)
            full_ref[slot] = (x * scale * gain).astype(BF)


def assemble(pieces, nt, group, groups, gain=None, ready=()):
    rows, width = pieces[0][0].shape
    rows //= groups
    tile = min(64, rows)
    first = group * (rows // tile)
    items = flat(pieces)
    extra = [] if gain is None else [gain]
    return call(
        functools.partial(assemble_kernel, nt, len(items), len(extra)),
        (rows // tile,),
        [pl.BlockSpec((tile, a.shape[1]), lambda i: (i + first, 0)) for a in items]
        + [whole_spec(a.shape) for a in extra]
        + [ANY] * len(ready),
        pl.BlockSpec((nt, tile, width), lambda i: (0, i, 0)),
        sds((nt, rows, width), BF),
        nbytes=4 * nt * rows * width,
    )(*items, *extra, *ready)


def qkv_kernel(nt, a1_ref, w_ref, cos_ref, sin_ref, out_ref):
    cols = out_ref.shape[3]
    weight = w_ref[:, 0].reshape(-1, cols)

    @pl.when(pl.program_id(0) < 2)
    def _():
        for slot in range(nt):
            raw = dot(a1_ref[slot], weight)
            cos, sin = cos_ref[slot], sin_ref[slot]
            for p in range(cols // PAIR):
                part = slice(p * PAIR, (p + 1) * PAIR)
                out_ref[0, slot, :, part] = rotate(raw[:, part], cos, sin).astype(BF)

    @pl.when(pl.program_id(0) == 2)
    def _():
        for slot in range(nt):
            out_ref[0, slot] = dot(a1_ref[slot], weight).astype(BF)


def project_qkv(a1, weight, cos, sin, nt):
    nd, _, ds, hc = weight.shape
    _, rows, width = a1.shape
    return call(
        functools.partial(qkv_kernel, nt),
        (3,),
        [
            whole_spec(a1.shape),
            pl.BlockSpec((nd, 1, ds, hc), lambda c: (0, c, 0, 0)),
            whole_spec(cos.shape),
            whole_spec(sin.shape),
        ],
        pl.BlockSpec((1, nt, rows, hc), lambda c: (c, 0, 0, 0)),
        sds((3, nt, rows, hc), BF),
        flops=2 * nt * rows * width * hc * 3,
        nbytes=2 * (nt * rows * width + 3 * width * hc + 3 * nt * rows * hc),
    )(a1, weight, cos, sin)


def allowed_block(start, key_block, query_block, size):
    key_id = lax.broadcasted_iota(jnp.int32, (size, size), 0) + key_block * size
    ok = key_id >= start
    if key_block == query_block:
        ok &= lax.broadcasted_iota(jnp.int32, (size, size), 1) + query_block * size >= key_id
    return ok


def attn_fwd_kernel(nt, slot_ref, q_ref, k_ref, v_ref, start_ref, ctx_ref, lse_ref, vt_ref):
    size = q_ref.shape[1]
    for b in range(nt):
        vt_ref[b] = v_ref[slot_ref[b]].T
    lane = lax.broadcasted_iota(jnp.int32, (size, PAIR), 1)
    for p in range(nt):
        slot = slot_ref[p]
        q = q_ref[slot] * BF(HEAD_DIM**-0.5)
        start = start_ref[0, pl.ds(slot, 1), :]
        outs = []
        for h in range(2):
            qh = jnp.where((lane >= HEAD_DIM) == (h == 1), q, BF(0))
            scores = []
            for b in range(p + 1):
                s = dot_nt(k_ref[slot_ref[b]], qh)
                scores.append(jnp.where(allowed_block(start, b, p, size), s, MASKED_SCORE))
            top = functools.reduce(
                jnp.maximum, [jnp.max(s, axis=0, keepdims=True) for s in scores]
            )
            total = jnp.zeros((1, size), F32)
            acc = jnp.zeros((HEAD_DIM, size), F32)
            for b, s in enumerate(scores):
                e = jnp.exp(s - top)
                total += jnp.sum(e, axis=0, keepdims=True)
                acc += dot(vt_ref[b, h * HEAD_DIM : (h + 1) * HEAD_DIM, :], e.astype(BF))
            outs.append(acc / total)
            lse_ref[0, 0, pl.ds(2 * p + h, 1), :] = top + jnp.log(total)
        ctx_ref[slot] = jnp.concatenate(outs, axis=0).T.astype(BF)


def qkv_specs(nt, size):
    def spec(c):
        return pl.BlockSpec((None, nt, size, PAIR), lambda s, g, _: (c, 0, s, g))

    return [spec(c) for c in range(3)]


def attention_forward(qkv, start, slot_of, nt):
    _, _, rows, hc = qkv.shape
    seqs = start.shape[0]
    size = rows // seqs
    pairs = hc // PAIR
    blk = pl.BlockSpec((nt, size, PAIR), lambda s, g, _: (0, s, g))
    return call(
        functools.partial(attn_fwd_kernel, nt),
        (seqs, pairs),
        qkv_specs(nt, size) + [pl.BlockSpec((1, nt, size), lambda s, g, _: (s, 0, 0))],
        [blk, pl.BlockSpec((1, 1, 2 * nt, size), lambda s, g, _: (s, g, 0, 0))],
        [sds((nt, rows, hc), BF), sds((seqs, pairs, 2 * nt, size), F32)],
        scratch=[pltpu.VMEM((nt, PAIR, size), BF)],
        flops=seqs * pairs * 2 * 4 * (nt * size) ** 2 * 128,
        nbytes=8 * nt * rows * hc,
        prefetch=1,
    )(slot_of, qkv, qkv, qkv, start)


def attn_bwd_kernel(
    nt, slot_ref, q_ref, k_ref, v_ref, go_ref, start_ref, lse_ref, cos_ref, sin_ref,
    gq_ref, gk_ref, gv_ref, kt_ref, dk_ref, dv_ref,
):
    size = q_ref.shape[1]
    scale = HEAD_DIM**-0.5
    for b in range(nt):
        kt_ref[b] = k_ref[slot_ref[b]].T
    dk_ref[...] = jnp.zeros_like(dk_ref)
    dv_ref[...] = jnp.zeros_like(dv_ref)
    lane = lax.broadcasted_iota(jnp.int32, (size, PAIR), 1)
    for p in range(nt):
        slot = slot_ref[p]
        q = q_ref[slot] * BF(scale)
        go = go_ref[slot]
        start = start_ref[0, pl.ds(slot, 1), :]
        outs = []
        for h in range(2):
            mine = (lane >= HEAD_DIM) == (h == 1)
            qh = jnp.where(mine, q, BF(0))
            goh = jnp.where(mine, go, BF(0))
            lse = lse_ref[0, 0, pl.ds(2 * p + h, 1), :]
            probs, grads = [], []
            inner = jnp.zeros((1, size), F32)
            for b in range(p + 1):
                key_slot = slot_ref[b]
                s = dot_nt(k_ref[key_slot], qh)
                s = jnp.where(allowed_block(start, b, p, size), s, MASKED_SCORE)
                e = jnp.exp(s - lse)
                g = dot_nt(v_ref[key_slot], goh)
                inner += jnp.sum(e * g, axis=0, keepdims=True)
                probs.append(e)
                grads.append(g)
            dqt = jnp.zeros((HEAD_DIM, size), F32)
            for b in range(p + 1):
                ds = (probs[b] * (grads[b] - inner)).astype(BF)
                dv_ref[b] += dot(probs[b].astype(BF), goh)
                dk_ref[b] += dot(ds, qh)
                dqt += dot(kt_ref[b, h * HEAD_DIM : (h + 1) * HEAD_DIM, :], ds)
            outs.append(dqt)
        dq = jnp.concatenate(outs, axis=0).T * scale
        gq_ref[slot] = unrotate(dq, cos_ref[slot], sin_ref[slot]).astype(BF)
    for b in range(nt):
        slot = slot_ref[b]
        gk_ref[slot] = unrotate(dk_ref[b], cos_ref[slot], sin_ref[slot]).astype(BF)
        gv_ref[slot] = dv_ref[b].astype(BF)


def attention_backward(qkv, go, start, lse, cos, sin, slot_of, nt):
    _, _, rows, hc = qkv.shape
    seqs = start.shape[0]
    size = rows // seqs
    pairs = hc // PAIR
    blk = pl.BlockSpec((nt, size, PAIR), lambda s, g, _: (0, s, g))
    table = pl.BlockSpec((nt, size, PAIR), lambda s, g, _: (0, s, 0))
    return call(
        functools.partial(attn_bwd_kernel, nt),
        (seqs, pairs),
        qkv_specs(nt, size)
        + [
            blk,
            pl.BlockSpec((1, nt, size), lambda s, g, _: (s, 0, 0)),
            pl.BlockSpec((1, 1, 2 * nt, size), lambda s, g, _: (s, g, 0, 0)),
            table, table,
        ],
        [blk, blk, blk],
        [sds((nt, rows, hc), BF)] * 3,
        scratch=[
            pltpu.VMEM((nt, PAIR, size), BF),
            pltpu.VMEM((nt, size, PAIR), F32),
            pltpu.VMEM((nt, size, PAIR), F32),
        ],
        flops=seqs * pairs * 2 * 10 * (nt * size) ** 2 * 128,
        nbytes=14 * nt * rows * hc,
        prefetch=1,
    )(slot_of, qkv, qkv, qkv, go, start, lse, cos, sin)


def shard_group(nd, count):
    while nd % count or nd // count % 2:
        count //= 2
    return max(count, 1)


def cols_out_kernel(nt, steps, lhs_ref, w_ref, *outs):
    for slot in range(nt):
        lhs = lhs_ref[slot]
        parts = [dot(lhs, w_ref[j]) for j in range(w_ref.shape[0])]
        store_piece(outs, nt, slot, steps, jnp.concatenate(parts, axis=1))


def mm_cols(lhs, weight, nt, group):
    nd, depth, ds = weight.shape
    group = shard_group(nd, group)
    rows = lhs.shape[1]
    width = nd * ds
    shapes = flat(piece_shapes(nt, rows, width))
    outs = call(
        functools.partial(cols_out_kernel, nt, nd // group),
        (nd // group,),
        [whole_spec(lhs.shape), pl.BlockSpec((group, depth, ds), lambda j: (j, 0, 0))],
        out_piece_specs(nt, rows, width, group * ds),
        [sds(s, BF) for s in shapes],
        flops=2 * nt * rows * depth * width,
        nbytes=2 * (nt * rows * (depth + width) + depth * width),
    )(lhs, weight)
    return regroup(outs, nt)


def cols_back_kernel(nt, steps, nlhs, nseen, *refs):
    lhs, w_refs, outs = refs[:nlhs], refs[nlhs : 2 * nlhs], refs[2 * nlhs + nseen :]
    depth = w_refs[0].shape[3]
    weights = [w[:, 0].reshape(-1, depth) for w in w_refs]
    sums = None
    for slot in range(nt):
        total = dot_nt(lhs[0][slot], weights[0])
        for c in range(1, nlhs):
            total += dot_nt(lhs[c][slot], weights[c])
        if nseen:
            part = jnp.sum(total * refs[2 * nlhs][slot].astype(F32), axis=0, keepdims=True)
            sums = part if sums is None else sums + part
        store_piece(outs[: len(outs) - nseen], nt, slot, steps, total)
    if nseen:
        outs[-1][...] = sums


def mm_back(lhs, weight, channels, nt, group, seen=None):
    nd, _, ds, depth = weight.shape
    count = len(lhs)
    group = shard_group(nd, group)
    rows = lhs[0].shape[1]
    width = nd * ds
    shapes = flat(piece_shapes(nt, rows, width))
    step = group * ds
    more = [] if seen is None else [seen]

    def spec(c):
        return pl.BlockSpec((group, 1, ds, depth), lambda j: (j, c, 0, 0))

    outs = call(
        functools.partial(cols_back_kernel, nt, nd // group, count, len(more)),
        (nd // group,),
        [whole_spec(a.shape) for a in lhs]
        + [spec(c) for c in channels]
        + [pl.BlockSpec((nt, rows, step), lambda j: (0, 0, j)) for _ in more],
        out_piece_specs(nt, rows, width, step) + [pl.BlockSpec((1, step), lambda j: (0, j)) for _ in more],
        [sds(s, BF) for s in shapes] + [sds((1, width), F32) for _ in more],
        flops=2 * nt * rows * depth * width * count,
        nbytes=2 * (nt * rows * (depth * count + width) + depth * width * count),
    )(*lhs, *[weight] * count, *more)
    return regroup(outs[: len(shapes)], nt), outs[len(shapes) :]


def gateup_kernel(nt, *refs):
    count = len(flat(piece_shapes(nt, 8, 8)))
    pieces, w_ref, (full_ref, silu_ref, slope_ref, hid_ref) = (
        refs[:count],
        refs[count],
        refs[count + 1 :],
    )

    @pl.when(pl.program_id(0) == 0)
    def _():
        fill_from_pieces(pieces, full_ref, nt)

    cols = hid_ref.shape[2]
    w_gate = w_ref[:, 0].reshape(-1, cols)
    w_up = w_ref[:, 1].reshape(-1, cols)
    for slot in range(nt):
        a2 = full_ref[slot]
        gate = dot(a2, w_gate)
        up = dot(a2, w_up)
        sig = 0.5 + 0.5 * jnp.tanh(0.5 * gate)
        silu = gate * sig
        silu_ref[slot] = silu.astype(BF)
        slope_ref[slot] = (up * (sig + silu - silu * sig)).astype(BF)
        hid_ref[slot] = (silu * up).astype(BF)


def gate_up(pieces, weight, nt):
    nd, _, ds, ff = weight.shape
    rows, width = pieces[0][0].shape
    step = min(512, ff)
    blk = pl.BlockSpec((nt, rows, step), lambda j: (0, 0, j))
    return call(
        functools.partial(gateup_kernel, nt),
        (ff // step,),
        [whole_spec(a.shape) for a in flat(pieces)]
        + [pl.BlockSpec((nd, 2, ds, step), lambda j: (0, 0, 0, j))],
        [whole_spec((nt, rows, width)), blk, blk, blk],
        [sds((nt, rows, width), BF)] + [sds((nt, rows, ff), BF)] * 3,
        flops=4 * nt * rows * width * ff,
        nbytes=2 * (2 * nt * rows * width + 2 * width * ff + 3 * nt * rows * ff),
    )(*flat(pieces), weight)


def gate_back_kernel(nt, full_ref, w_ref, silu_ref, slope_ref, gg_ref, gu_ref):
    weight = jnp.concatenate([w_ref[j] for j in range(w_ref.shape[0])], axis=1)
    for slot in range(nt):
        gh = dot_nt(full_ref[slot], weight)
        gg_ref[slot] = (gh * slope_ref[slot].astype(F32)).astype(BF)
        gu_ref[slot] = (gh * silu_ref[slot].astype(F32)).astype(BF)


def gate_back(full, weight, silu, slope, nt):
    nd, ff, ds = weight.shape
    _, rows, width = full.shape
    step = min(512, ff)
    blk = pl.BlockSpec((nt, rows, step), lambda j: (0, 0, j))
    return call(
        functools.partial(gate_back_kernel, nt),
        (ff // step,),
        [whole_spec(full.shape), pl.BlockSpec((nd, step, ds), lambda j: (0, j, 0)), blk, blk],
        [blk, blk],
        [sds((nt, rows, ff), BF)] * 2,
        flops=2 * nt * rows * width * ff,
        nbytes=2 * (nt * rows * width + width * ff + 4 * nt * rows * ff),
    )(full, weight, silu, slope)


def context_back_kernel(nt, *refs):
    pieces, w_ref, (full_ref, out_ref) = refs[:-3], refs[-3], refs[-2:]

    @pl.when(pl.program_id(0) == 0)
    def _():
        fill_from_pieces(pieces, full_ref, nt)

    weight = w_ref[:, 0].reshape(-1, w_ref.shape[3])
    for slot in range(nt):
        out_ref[slot] = dot(full_ref[slot], weight).astype(BF)


def context_back(pieces, weight, channel, nt):
    nd, _, ds, hc = weight.shape
    rows, width = pieces[0][0].shape
    step = min(256, hc)
    return call(
        functools.partial(context_back_kernel, nt),
        (hc // step,),
        [whole_spec(a.shape) for a in flat(pieces)]
        + [pl.BlockSpec((nd, 1, ds, step), lambda j: (0, channel, 0, j))],
        [whole_spec((nt, rows, width)), pl.BlockSpec((nt, rows, step), lambda j: (0, 0, j))],
        [sds((nt, rows, width), BF), sds((nt, rows, hc), BF)],
        flops=2 * nt * rows * width * hc,
        nbytes=2 * (2 * nt * rows * width + width * hc + nt * rows * hc),
    )(*flat(pieces), weight)


def middle_kernel(nterms, x_ref, gain_ref, *refs):
    terms, (mid_ref, low_ref) = refs[:nterms], refs[nterms:]
    mid = x_ref[...].astype(F32) + sum_terms(terms)
    mid_ref[...] = mid
    scale = lax.rsqrt(jnp.mean(mid * mid, axis=-1, keepdims=True) + NORM_EPS)
    low_ref[...] = (mid * scale * gain_ref[...]).astype(BF)


def make_middle(x, gain, terms):
    rows, width = x.shape
    tile = min(128, rows)
    blk = pl.BlockSpec((tile, width), lambda i: (i, 0))
    return call(
        functools.partial(middle_kernel, len(terms)),
        (rows // tile,),
        [blk, whole_spec(gain.shape)] + [blk] * len(terms),
        [blk, blk],
        [sds((rows, width), F32), sds((rows, width), BF)],
        nbytes=rows * width * (8 + 2 * len(terms)),
    )(x, gain, *terms)


def sum_terms(terms):
    total = terms[0][...].astype(F32)
    for t in terms[1:]:
        total += t[...].astype(F32)
    return total


def layer_out_kernel(nterms, mid_ref, *refs):
    refs[-1][...] = (mid_ref[...] + sum_terms(refs[:nterms])).astype(BF)


def place(group, groups, rows, tile, width, into):
    steps = rows // tile
    spec = pl.BlockSpec((tile, width), lambda i: (i + group * steps, 0))
    return spec, sds((groups * rows, width), BF), [] if into is None else [into]


def layer_out_rows(mid, terms, group, groups, into):
    rows, width = mid.shape
    tile = min(128, rows)
    blk = pl.BlockSpec((tile, width), lambda i: (i, 0))
    spec, shape, old = place(group, groups, rows, tile, width, into)
    return call(
        functools.partial(layer_out_kernel, len(terms)),
        (rows // tile,),
        [blk] * (1 + len(terms)) + [HBM] * len(old),
        spec,
        shape,
        nbytes=rows * width * (6 + 2 * len(terms)),
        aliases={1 + len(terms): 0} if old else None,
    )(mid, *terms, *old)


def norm_back_kernel(nterms, nouts, first_ref, v_ref, gain_ref, *refs):
    terms, outs, sums = refs[:nterms], refs[len(refs) - nouts :], []
    if nouts == 3:
        outs, sums = outs[:2], outs[2:]
    u = sum_terms(terms)
    v = v_ref[...].astype(F32)
    q = lax.rsqrt(jnp.mean(v * v, axis=-1, keepdims=True) + NORM_EPS)
    ug = u * gain_ref[...]
    inner = jnp.mean(ug * v, axis=-1, keepdims=True)
    grad = first_ref[...].astype(F32) + (q * ug - v * (q * q * q * inner))
    for out in outs:
        out[...] = grad.astype(out.dtype)
    for sum_ref in sums:

        @pl.when(pl.program_id(0) == 0)
        def _():
            sum_ref[...] = jnp.zeros_like(sum_ref)

        sum_ref[...] += jnp.sum(u * v * q, axis=0, keepdims=True)


def norm_back(first, v, gain, terms):
    rows, width = v.shape
    tile = min(128, rows)
    blk = pl.BlockSpec((tile, width), lambda i: (i, 0))
    return call(
        functools.partial(norm_back_kernel, len(terms), 3),
        (rows // tile,),
        [blk, blk, whole_spec(gain.shape)] + [blk] * len(terms),
        [blk, blk, pl.BlockSpec((1, width), lambda i: (0, 0))],
        [sds((rows, width), F32), sds((rows, width), BF), sds((1, width), F32)],
        nbytes=rows * width * (12 + 2 * len(terms)),
    )(first, v, gain, *terms)


def norm_back_rows(first, v, gain, terms, group, groups, into):
    rows, width = v.shape
    tile = min(128, rows)
    blk = pl.BlockSpec((tile, width), lambda i: (i, 0))
    spec, shape, old = place(group, groups, rows, tile, width, into)
    return call(
        functools.partial(norm_back_kernel, len(terms), 1),
        (rows // tile,),
        [blk, blk, whole_spec(gain.shape)] + [blk] * len(terms) + [HBM] * len(old),
        spec,
        shape,
        nbytes=rows * width * (12 + 2 * len(terms)),
        aliases={3 + len(terms): 0} if old else None,
    )(first, v, gain, *terms, *old)


def wgrad_rows_kernel(groups, which, nmore, *refs):
    nlhs = groups * (max(which) + 1)
    lhs, rhs, out_ref = refs[:nlhs], refs[nlhs : nlhs + groups * len(which)], refs[-1]
    tile = lhs[0].shape[2]
    left = [a[...].reshape(-1, tile).T for a in lhs]
    for c, w in enumerate(which):
        total = None
        for g in range(groups):
            a = left[w * groups + g]
            term = dot(a, rhs[c * groups + g][...].reshape(a.shape[1], -1))
            total = term if total is None else total + term
        out_ref[0, c * tile : (c + 1) * tile] = total.astype(BF)
    if nmore:
        out_ref[0, len(which) * tile :] = refs[-2][0]


def wgrad_rows(lhs, rhs, which, nd, more=None):
    groups = len(lhs[0])
    nt, rows, width = lhs[0][0].shape
    ds = width // nd
    n = rhs[0][0].shape[2]
    more = [] if more is None else [more]
    height = len(rhs) * ds + sum(a.shape[1] for a in more)
    return call(
        functools.partial(wgrad_rows_kernel, groups, which, len(more)),
        (nd,),
        [pl.BlockSpec((nt, rows, ds), lambda j: (0, 0, j))] * (groups * len(lhs))
        + [whole_spec(a.shape) for r in rhs for a in r]
        + [pl.BlockSpec((1,) + a.shape[1:], lambda j: (j, 0, 0)) for a in more],
        pl.BlockSpec((1, height, n), lambda j: (j, 0, 0)),
        sds((nd, height, n), BF),
        flops=2 * groups * nt * rows * width * n * len(rhs),
        nbytes=2 * groups * nt * rows * (width + n * len(rhs)) + 2 * width * n * len(rhs),
    )(*[a for l in lhs for a in l], *[a for r in rhs for a in r], *more)


def wgrad_cols_kernel(groups, nd, *refs):
    lhs, rhs, out_ref = refs[:groups], refs[groups:-1], refs[-1]
    tile = lhs[0].shape[2]
    ds = out_ref.shape[2]
    left = [a[...].reshape(-1, tile).T for a in lhs]
    total = None
    for g in range(groups):
        term = dot(left[g], rhs[g][...].reshape(left[g].shape[1], -1))
        total = term if total is None else total + term
    for j in range(nd):
        out_ref[j] = total[:, j * ds : (j + 1) * ds].astype(BF)


def wgrad_cols(lhs, rhs, nd):
    groups = len(lhs)
    nt, rows, m = lhs[0].shape
    width = rhs[0].shape[2]
    tile = min(256, m)
    return call(
        functools.partial(wgrad_cols_kernel, groups, nd),
        (m // tile,),
        [pl.BlockSpec((nt, rows, tile), lambda i: (0, 0, i))] * groups
        + [whole_spec(a.shape) for a in rhs],
        pl.BlockSpec((nd, tile, width // nd), lambda i: (0, i, 0)),
        sds((nd, m, width // nd), BF),
        flops=2 * groups * nt * rows * width * m,
        nbytes=2 * groups * nt * rows * (width + m) + 2 * width * m,
    )(*lhs, *rhs)


def doc_starts(segments):
    row_len = segments.shape[-1]
    ids = jnp.arange(row_len, dtype=jnp.int32)
    change = jnp.concatenate(
        [jnp.ones_like(segments[:, :1], dtype=bool), segments[:, 1:] != segments[:, :-1]], axis=1
    )
    return lax.cummax(jnp.where(change, ids[None, :], 0), axis=1)


def tensor_sum(value, nt):
    if nt != 4:
        return lax.psum(value, "tensor")
    value = value + lax.ppermute(value, "tensor", swap_perm(4, 1))
    return value + lax.ppermute(value, "tensor", swap_perm(4, 2))


def slot_order(blocks, index, nt):
    if nt != 4:
        return blocks
    pairs = jnp.stack([blocks[:, 1], blocks[:, 0], blocks[:, 3], blocks[:, 2]], axis=1)
    blocks = jnp.where(index % 2 == 1, pairs, blocks)
    halves = jnp.stack([blocks[:, 2], blocks[:, 3], blocks[:, 0], blocks[:, 1]], axis=1)
    return jnp.where(index // 2 == 1, halves, blocks)


def per_device(nd, nt, groups, layer_input, segments, qkv_w, out_w, gain1, gateup_w, down_w, gain2, grad_out):
    seqs, local, width = layer_input.shape
    per = seqs // groups
    index = lax.axis_index("tensor").astype(jnp.int32)
    blocks = jnp.arange(nt, dtype=jnp.int32)
    slot_of = blocks ^ index if nt == 4 else blocks

    x = [layer_input[g * per : (g + 1) * per].reshape(per * local, width) for g in range(groups)]
    go = [grad_out[g * per : (g + 1) * per].reshape(per * local, width) for g in range(groups)]
    Order.last = None
    x_all = Gather(layer_input.reshape(seqs * local, width), nt)

    gains = lax.all_gather(jnp.stack([gain1, gain2]), "dp", axis=1, tiled=True).astype(F32)
    g1, g2 = gains[:1], gains[1:]
    qkvo_w = jnp.concatenate([qkv_w, out_w.T[None]])
    full_qkvo = lax.all_gather(qkvo_w, "dp", axis=0, tiled=False)
    full_gateup = lax.all_gather(gateup_w, "dp", axis=0, tiled=False)
    full_down = lax.all_gather(down_w, "dp", axis=0, tiled=False)

    start_abs = doc_starts(segments)
    pos_abs = jnp.arange(segments.shape[1], dtype=jnp.int32)[None, :] - start_abs
    start_slot = slot_order(start_abs.reshape(seqs, nt, local), index, nt)
    pos_slot = slot_order(pos_abs.reshape(seqs, nt, local), index, nt)
    inv_freq = ROPE_BASE ** (-jnp.arange(HALF, dtype=F32) * 2.0 / HEAD_DIM)
    angles = pos_slot.astype(F32)[..., None] * inv_freq
    cos, sin = jnp.cos(angles), jnp.sin(angles)
    cos = jnp.concatenate([cos] * 4, axis=-1)
    sin = jnp.concatenate([-sin, sin] * 2, axis=-1)

    def table(t, g):
        t = t[g * per : (g + 1) * per]
        return jnp.swapaxes(t, 0, 1).reshape(nt, per * local, PAIR)

    coss = [table(cos, g) for g in range(groups)]
    sins = [table(sin, g) for g in range(groups)]
    starts = [start_slot[g * per : (g + 1) * per] for g in range(groups)]

    both = range(groups)
    qkv, ctx, lse, mid, low2, g_mid, g_low = ({} for _ in range(7))
    attn_sum, a2_all, ga2, out_sum, ga1 = ({} for _ in range(5))
    sum1, sum2, gm_all, gmf, g_qkv, g_ctx = ({} for _ in range(6))

    def dp_sum(grad):
        return lax.psum_scatter(grad, "dp", scatter_dimension=0, tiled=False)

    def project(g):
        qkv[g] = project_qkv(a1[g], full_qkvo, coss[g], sins[g], nt)

    def attend(g):
        ctx[g], lse[g] = attention_forward(qkv[g], starts[g], slot_of, nt)
        attn_sum[g] = Scatter(mm_back([ctx[g]], full_qkvo, [3], nt, 4)[0], nt)

    def middle(g):
        mid[g], low2[g] = make_middle(x[g], g2, attn_sum[g].terms)
        a2_all[g] = Gather(low2[g], nt)

    def second_back(g):
        ga2[g] = Scatter(mm_back([gg[g], gu[g]], full_gateup, [0, 1], nt, 2)[0], nt)

    def project_out(g):
        out_sum[g] = Scatter(mm_cols(hid[g], full_down, nt, 2), nt)

    def residual_back(g):
        g_mid[g], g_low[g], sum2[g] = norm_back(go[g], mid[g], g2, ga2[g].terms)
        gm_all[g] = Gather(g_low[g], nt)

    def attention_back_start(g):
        gmf[g], g_ctx[g] = context_back(gm_all[g].pieces, full_qkvo, 3, nt)

    def attention_back(g):
        g_qkv[g] = attention_backward(
            qkv[g], g_ctx[g], starts[g], lse[g], coss[g], sins[g], slot_of, nt
        )

    def input_back(g):
        parts, (sum1[g],) = mm_back(g_qkv[g], full_qkvo, [0, 1, 2], nt, 4, a1[g])
        ga1[g] = Scatter(parts, nt)

    def up_projection(g):
        a2[g], silu[g], slope[g], hid[g] = gate_up(a2_all[g].pieces, full_gateup, nt)

    def hidden_back(g):
        gg[g], gu[g] = gate_back(gof[g], full_down, silu[g], slope[g], nt)

    def finish(g, grad_input):
        return norm_back_rows(g_mid[g], x[g], g1, ga1[g].terms, g, groups, grad_input)

    def by_group(held):
        return [held[g] for g in both]

    def gather_cotangent(g):
        go_all[g] = Gather(link(go[g], flat(x_all.pieces)[-1]), nt)

    a2, silu, slope, hid, gg, gu, go_all, gof = ({} for _ in range(8))
    x_all.second()
    gather_cotangent(0)
    gather_cotangent(1)
    a1 = [assemble(x_all.pieces, nt, 0, groups, g1, coss + sins)]
    project(0)
    attend(0)
    go_all[0].second()
    a1.append(assemble(x_all.pieces, nt, 1, groups, g1))
    project(1)
    attn_sum[0].second()
    attend(1)
    middle(0)
    gof[0] = assemble(go_all[0].pieces, nt, 0, 1)
    attn_sum[1].second()
    a2_all[0].second()
    middle(1)
    go_all[1].second()
    up_projection(0)
    a2_all[1].second()
    gof[1] = assemble(go_all[1].pieces, nt, 0, 1)
    up_projection(1)
    hidden_back(0)
    grad_down = dp_sum(wgrad_cols(by_group(hid), by_group(gof), nd))
    second_back(0)
    hidden_back(1)
    ga2[0].second()
    second_back(1)
    residual_back(0)
    grad_gateup = wgrad_rows([by_group(a2)], [by_group(gg), by_group(gu)], [0, 0], nd)
    ga2[1].second()
    gm_all[0].second()
    grad_gateup = dp_sum(link(grad_gateup, grad_down))
    project_out(0)
    residual_back(1)
    project_out(1)
    attention_back_start(0)
    attention_back(0)
    gm_all[1].second()
    out_sum[0].second()
    input_back(0)
    out_sum[1].second()
    attention_back_start(1)
    attention_back(1)
    input_back(1)
    ds = gain1.shape[0]
    gains = tensor_sum(jnp.concatenate([(sum1[0] + sum1[1]) / g1, sum2[0] + sum2[1]]), nt)
    gains = jnp.swapaxes(gains.reshape(2, nd, ds), 0, 1).astype(BF)
    gains = jnp.pad(gains, ((0, 0), (0, 14), (0, qkv_w.shape[2] - ds)))
    layer_out = layer_out_rows(mid[0], out_sum[0].terms, 0, groups, None)
    grad_qkvo = wgrad_rows(
        [a1, by_group(gmf)],
        [[g_qkv[g][c] for g in both] for c in range(3)] + [by_group(ctx)],
        [0, 0, 0, 1],
        nd,
        gains,
    )
    ga1[1].second()
    grad_qkvo = dp_sum(link(grad_qkvo, grad_gateup))
    layer_out = layer_out_rows(mid[1], out_sum[1].terms, 1, groups, layer_out)
    ga1[0].second()
    grad_input = finish(1, None)
    grad_input = finish(0, grad_input)
    return (
        layer_out.reshape(seqs, local, width),
        grad_input.reshape(seqs, local, width),
        grad_qkvo[: 3 * ds].astype(F32).reshape(3, ds, -1),
        grad_qkvo[3 * ds : 4 * ds].T.astype(F32),
        grad_qkvo[4 * ds, :ds].astype(F32),
        grad_gateup.astype(F32).reshape(2, ds, -1),
        grad_down.astype(F32),
        grad_qkvo[4 * ds + 1, :ds].astype(F32),
    )


def solution(mesh):
    nd, nt = mesh.shape["dp"], mesh.shape["tensor"]
    return jax.shard_map(
        functools.partial(per_device, nd, nt, 2),
        mesh=mesh,
        in_specs=(
            P("dp", "tensor", None),
            P("dp", None),
            P(None, "dp", "tensor"),
            P("tensor", "dp"),
            P("dp"),
            P(None, "dp", "tensor"),
            P("tensor", "dp"),
            P("dp"),
            P("dp", "tensor", None),
        ),
        out_specs=(
            P("dp", "tensor", None),
            P("dp", "tensor", None),
            P(None, "dp", "tensor"),
            P("tensor", "dp"),
            P("dp"),
            P(None, "dp", "tensor"),
            P("tensor", "dp"),
            P("dp"),
        ),
        check_vma=False,
    )
```

```python
import functools

import jax
import jax.numpy as jnp
import numpy as np
from jax import lax
from jax.experimental import pallas as pl
from jax.experimental.pallas import tpu as pltpu
from jax.sharding import PartitionSpec as P

HEAD_DIM = 64
HALF = HEAD_DIM // 2
PAIR = 2 * HEAD_DIM
NORM_EPS = 1e-05
ROPE_BASE = 130000.0
MASKED_SCORE = -1e30
BF = jnp.bfloat16
F32 = jnp.float32
VMEM_SLACK = 8 * 1024 * 1024
VMEM_SMALL = 24 * 1024 * 1024
VMEM_LARGE = 40 * 1024 * 1024
PIN_BYTES = 3 * 1024 * 1024
PIN_BYTES_LARGE = 1024 * 1024
SMALL = 3

NT = (((1,), (1,)), ((), ()))


def dot(a, b):
    return jnp.dot(a, b, preferred_element_type=F32)


def dot_nt(a, b):
    return lax.dot_general(a, b, NT, preferred_element_type=F32)


class Order:
    last = None


HBM = pl.BlockSpec(memory_space=pltpu.HBM)
ANY = pl.BlockSpec(memory_space=pl.ANY)


def is_large(array, least=None):
    return array.size * array.dtype.itemsize >= (least or PIN_BYTES)


def pin(array, least=None):
    return pltpu.with_memory_space_constraint(array, pltpu.HBM) if is_large(array, least) else array


def pinned(shape):
    return pltpu.HBM(shape.shape, shape.dtype) if is_large(shape) else shape


def block_bytes(spec, dtype):
    if spec.block_shape is None:
        return 0
    count = 2 if spec.pipeline_mode is None else spec.pipeline_mode.buffer_count
    return count * int(np.prod([d for d in spec.block_shape if d])) * np.dtype(dtype).itemsize


def call(body, grid, in_specs, out_specs, out_shape, scratch=(), flops=0, nbytes=0, aliases=None, prefetch=0):
    first_extra = prefetch + len(in_specs)
    many = isinstance(out_shape, (list, tuple))
    out_blocks = list(zip(out_specs, out_shape)) if many else [(out_specs, out_shape)]

    def run(*args):
        extra = [] if Order.last is None or any(a is Order.last for a in args) else [pin(Order.last)]

        blocks = list(zip(in_specs, args[prefetch:])) + out_blocks
        vmem = VMEM_SLACK + sum(block_bytes(spec, a.dtype) for spec, a in blocks)
        vmem += sum(int(np.prod(m.shape)) * np.dtype(m.dtype).itemsize for m in scratch)
        least = PIN_BYTES
        if vmem > VMEM_SMALL:
            vmem, least = VMEM_LARGE, PIN_BYTES_LARGE

        args = [pin(a, least) for a in args]

        def ordered_body(*refs):
            body(*refs[:first_extra], *refs[first_extra + len(extra) :])

        outs = pl.pallas_call(
            ordered_body,
            grid_spec=pltpu.PrefetchScalarGridSpec(
                num_scalar_prefetch=prefetch,
                grid=grid,
                in_specs=in_specs + [ANY] * len(extra),
                out_specs=out_specs,
                scratch_shapes=list(scratch),
            ),
            out_shape=[pinned(a) for a in out_shape] if many else pinned(out_shape),
            input_output_aliases=aliases or {},
            cost_estimate=pl.CostEstimate(flops=flops // SMALL, bytes_accessed=nbytes // SMALL, transcendentals=0),
            compiler_params=pltpu.CompilerParams(vmem_limit_bytes=vmem),
        )(*args, *extra)
        Order.last = outs[-1] if isinstance(outs, (list, tuple)) else outs
        return outs

    return run


def link_kernel(value_ref, done_ref, out_ref):
    pass


def link(value, done):
    return call(link_kernel, (1,), [HBM, HBM], HBM, sds(value.shape, value.dtype), aliases={0: 0})(value, done)


def whole_spec(shape, buffers=1):
    zeros = (0,) * len(shape)
    return pl.BlockSpec(shape, lambda *_: zeros, pipeline_mode=pl.Buffered(buffers))


def sds(shape, dtype):
    return jax.ShapeDtypeStruct(shape, dtype)


def swap_perm(count, bit):
    return [(i, i ^ bit) for i in range(count)]


def halves_kernel(y_ref, x_ref, left_ref, right_ref):
    left_ref[...] = y_ref[...]
    right_ref[...] = x_ref[...]


def halves(from_y, from_x, axis=1):
    rows, width = from_y.shape
    shape = (rows, width // 2) if axis else (rows // 2, width)
    tile = min(128, shape[0])
    steps = shape[0] // tile
    first = pl.BlockSpec((tile, shape[1]), lambda i: (i, 0))
    second = pl.BlockSpec((tile, shape[1]), (lambda i: (i, 1)) if axis else (lambda i: (i + steps, 0)))
    return call(
        halves_kernel,
        (steps,),
        [first, second],
        [first, first],
        [sds(shape, BF)] * 2,
        nbytes=rows * width * 4,
    )(from_y, from_x)


class Gather:
    def __init__(self, block, nt, direct=False):
        self.nt = nt
        if nt != 4:
            full = lax.all_gather(block, "tensor", axis=0, tiled=False)
            self.pieces = [(full[r],) for r in range(nt)]
            return
        self.block = block
        self.from_x = lax.ppermute(block, "tensor", swap_perm(4, 1))
        self.from_y = lax.ppermute(block, "tensor", swap_perm(4, 2))
        if direct:
            diag = lax.ppermute(block, "tensor", swap_perm(4, 3))
            self.pieces = [(block,), (self.from_x,), (self.from_y,), (diag,)]

    def second(self):
        if self.nt != 4:
            return
        left, right = halves(self.from_y, self.from_x)
        diag_x = lax.ppermute(left, "tensor", swap_perm(4, 1))
        diag_y = lax.ppermute(right, "tensor", swap_perm(4, 2))
        self.pieces = [(self.block,), (self.from_x,), (self.from_y,), (diag_x, diag_y)]


def add_halves_kernel(x_ref, for_x_ref, y_ref, for_y_ref, out_x_ref, out_y_ref):
    out_x_ref[...] = (x_ref[...].astype(F32) + for_x_ref[...].astype(F32)).astype(BF)
    out_y_ref[...] = (y_ref[...].astype(F32) + for_y_ref[...].astype(F32)).astype(BF)


def add_halves(to_x, for_x, to_y, for_y):
    rows, width = to_x.shape
    half = width // 2
    tile = min(128, rows)

    def spec(which):
        return pl.BlockSpec((tile, half), lambda i: (i, which))

    return call(
        add_halves_kernel,
        (rows // tile,),
        [spec(1), spec(0), spec(0), spec(0)],
        [spec(1), spec(0)],
        [sds(to_x.shape, BF)] * 2,
        nbytes=rows * half * 12,
        aliases={0: 0, 2: 1},
    )(to_x, for_x, to_y, for_y)


class Scatter:
    def __init__(self, parts, nt):
        self.nt = nt
        if nt != 4:
            full = jnp.stack([p[0] for p in parts])
            self.terms = [lax.psum_scatter(full, "tensor", scatter_dimension=0, tiled=False)]
            return
        (self.own,), (self.to_x,), (self.to_y,), (diag_x, diag_y) = parts
        self.for_y = lax.ppermute(diag_x, "tensor", swap_perm(4, 1))
        self.for_x = lax.ppermute(diag_y, "tensor", swap_perm(4, 2))

    def second(self):
        if self.nt != 4:
            return
        to_x, to_y = add_halves(self.to_x, self.for_x, self.to_y, self.for_y)
        self.terms = [
            self.own,
            lax.ppermute(to_x, "tensor", swap_perm(4, 1)),
            lax.ppermute(to_y, "tensor", swap_perm(4, 2)),
        ]


class HeadWeights:
    def __init__(self, full, channel, nd):
        _, _, ds, hc = full.shape
        half = nd // 2
        core = (lax.axis_index("dp") % 2).astype(jnp.int32)
        self.full, self.channel, self.nd, self.core = full, channel, nd, core.reshape(1)
        part = lax.dynamic_slice(full, (core * half, channel, 0, 0), (half, 1, ds, hc)).reshape(half * ds, hc)
        self.from_x = lax.ppermute(part, "tensor", swap_perm(4, 1))
        self.from_y = lax.ppermute(part, "tensor", swap_perm(4, 2))

    def second(self):
        top, bottom = halves(self.from_y, self.from_x, axis=0)
        diag = [
            lax.ppermute(top, "tensor", swap_perm(4, 1)),
            lax.ppermute(bottom, "tensor", swap_perm(4, 2)),
        ]
        self.mine = [self.from_x, self.from_y] + diag
        self.other = [lax.ppermute(a, "dp", swap_perm(self.nd, 1)) for a in self.mine]

    def specs(self):
        _, _, ds, hc = self.full.shape
        block = (self.nd // 2, 1, ds, hc)
        return [
            pl.BlockSpec(block, lambda i, core: (core[0], self.channel, 0, 0), pipeline_mode=pl.Buffered(1)),
            pl.BlockSpec(block, lambda i, core: (1 - core[0], self.channel, 0, 0), pipeline_mode=pl.Buffered(1)),
        ] + [whole_spec(a.shape) for a in self.mine + self.other]

    def arrays(self):
        return [self.full, self.full] + self.mine + self.other


def exchange_slots(blocks):
    return [lax.ppermute(blocks[r], "tensor", swap_perm(4, r)) for r in range(1, 4)]


def piece_shapes(nt, rows, width):
    if nt != 4:
        return [((rows, width),)] * nt
    return [((rows, width),)] * 3 + [((rows, width // 2),) * 2]


def flat(pieces):
    return [a for p in pieces for a in p]


def regroup(items, nt):
    if len(items) == nt:
        return [(a,) for a in items]
    return [(items[0],), (items[1],), (items[2],), (items[3], items[4])]


def fill_from_pieces(refs, full_ref, nt):
    for slot, part in enumerate(regroup(refs, nt)):
        if len(part) == 1:
            full_ref[slot] = part[0][...]
        else:
            half = part[0].shape[1]
            full_ref[slot, :, :half] = part[0][...]
            full_ref[slot, :, half:] = part[1][...]


def out_piece_specs(nt, rows, width, step):
    specs = []
    half_steps = width // step // 2
    for part in piece_shapes(nt, rows, width):
        if len(part) == 1:
            specs.append(pl.BlockSpec((rows, step), lambda j: (0, j)))
        else:
            specs.append(pl.BlockSpec((rows, step), lambda j: (0, jnp.minimum(j, half_steps - 1))))
            specs.append(pl.BlockSpec((rows, step), lambda j: (0, jnp.maximum(j - half_steps, 0))))
    return specs


def store_piece(outs, nt, slot, steps, value):
    part = regroup(outs, nt)[slot]
    if len(part) == 1:
        part[0][...] = value.astype(BF)
    else:
        j = pl.program_id(0)

        @pl.when(j < steps // 2)
        def _():
            part[0][...] = value.astype(BF)

        @pl.when(j >= steps // 2)
        def _():
            part[1][...] = value.astype(BF)


def turn(v):
    lane = lax.broadcasted_iota(jnp.int32, v.shape, 1)
    return jnp.where(lane % HEAD_DIM < HALF, pltpu.roll(v, PAIR - HALF, 1), pltpu.roll(v, HALF, 1))


def rotate(v, cos, sin):
    return v * cos + turn(v) * sin


def unrotate(u, cos, sin):
    return u * cos + turn(u * sin)


def assemble_kernel(nt, count, normed, *refs):
    full_ref = refs[-1]
    fill_from_pieces(refs[:count], full_ref, nt)
    if normed:
        gain = refs[count][...]
        for slot in range(nt):
            x = full_ref[slot].astype(F32)
            scale = lax.rsqrt(jnp.mean(x * x, axis=-1, keepdims=True) + NORM_EPS)
            full_ref[slot] = (x * scale * gain).astype(BF)


def assemble(pieces, nt, group, groups, gain=None, ready=()):
    rows, width = pieces[0][0].shape
    rows //= groups
    tile = min(64, rows)
    first = group * (rows // tile)
    items = flat(pieces)
    extra = [] if gain is None else [gain]
    return call(
        functools.partial(assemble_kernel, nt, len(items), len(extra)),
        (rows // tile,),
        [pl.BlockSpec((tile, a.shape[1]), lambda i: (i + first, 0)) for a in items]
        + [whole_spec(a.shape) for a in extra]
        + [ANY] * len(ready),
        pl.BlockSpec((nt, tile, width), lambda i: (0, i, 0)),
        sds((nt, rows, width), BF),
        nbytes=4 * nt * rows * width,
    )(*items, *extra, *ready)


def qkv_kernel(nt, a1_ref, w_ref, cos_ref, sin_ref, out_ref):
    cols = out_ref.shape[3]
    weight = w_ref[:, 0].reshape(-1, cols)

    @pl.when(pl.program_id(0) < 2)
    def _():
        for slot in range(nt):
            raw = dot(a1_ref[slot], weight)
            cos, sin = cos_ref[slot], sin_ref[slot]
            for p in range(cols // PAIR):
                part = slice(p * PAIR, (p + 1) * PAIR)
                out_ref[0, slot, :, part] = rotate(raw[:, part], cos, sin).astype(BF)

    @pl.when(pl.program_id(0) == 2)
    def _():
        for slot in range(nt):
            out_ref[0, slot] = dot(a1_ref[slot], weight).astype(BF)


def project_qkv(a1, weight, cos, sin, nt):
    nd, _, ds, hc = weight.shape
    _, rows, width = a1.shape
    return call(
        functools.partial(qkv_kernel, nt),
        (3,),
        [
            whole_spec(a1.shape),
            pl.BlockSpec((nd, 1, ds, hc), lambda c: (0, c, 0, 0)),
            whole_spec(cos.shape),
            whole_spec(sin.shape),
        ],
        pl.BlockSpec((1, nt, rows, hc), lambda c: (c, 0, 0, 0)),
        sds((3, nt, rows, hc), BF),
        flops=2 * nt * rows * width * hc * 3,
        nbytes=2 * (nt * rows * width + 3 * width * hc + 3 * nt * rows * hc),
    )(a1, weight, cos, sin)


def allowed_block(start, key_block, query_block, size):
    key_id = lax.broadcasted_iota(jnp.int32, (size, size), 0) + key_block * size
    ok = key_id >= start
    if key_block == query_block:
        ok &= lax.broadcasted_iota(jnp.int32, (size, size), 1) + query_block * size >= key_id
    return ok


def attn_fwd_kernel(nt, slot_ref, q_ref, k_ref, v_ref, start_ref, ctx_ref, lse_ref, vt_ref):
    size = q_ref.shape[1]
    for b in range(nt):
        vt_ref[b] = v_ref[slot_ref[b]].T
    lane = lax.broadcasted_iota(jnp.int32, (size, PAIR), 1)
    for p in range(nt):
        slot = slot_ref[p]
        q = q_ref[slot] * BF(HEAD_DIM**-0.5)
        start = start_ref[0, pl.ds(slot, 1), :]
        outs = []
        for h in range(2):
            qh = jnp.where((lane >= HEAD_DIM) == (h == 1), q, BF(0))
            scores = []
            for b in range(p + 1):
                s = dot_nt(k_ref[slot_ref[b]], qh)
                scores.append(jnp.where(allowed_block(start, b, p, size), s, MASKED_SCORE))
            top = functools.reduce(
                jnp.maximum, [jnp.max(s, axis=0, keepdims=True) for s in scores]
            )
            total = jnp.zeros((1, size), F32)
            acc = jnp.zeros((HEAD_DIM, size), F32)
            for b, s in enumerate(scores):
                e = jnp.exp(s - top)
                total += jnp.sum(e, axis=0, keepdims=True)
                acc += dot(vt_ref[b, h * HEAD_DIM : (h + 1) * HEAD_DIM, :], e.astype(BF))
            outs.append(acc / total)
            lse_ref[0, 0, pl.ds(2 * p + h, 1), :] = top + jnp.log(total)
        ctx_ref[slot] = jnp.concatenate(outs, axis=0).T.astype(BF)


def qkv_specs(nt, size):
    def spec(c):
        return pl.BlockSpec((None, nt, size, PAIR), lambda s, g, _: (c, 0, s, g))

    return [spec(c) for c in range(3)]


def attention_forward(qkv, start, slot_of, nt):
    _, _, rows, hc = qkv.shape
    seqs = start.shape[0]
    size = rows // seqs
    pairs = hc // PAIR
    blk = pl.BlockSpec((nt, size, PAIR), lambda s, g, _: (0, s, g))
    return call(
        functools.partial(attn_fwd_kernel, nt),
        (seqs, pairs),
        qkv_specs(nt, size) + [pl.BlockSpec((1, nt, size), lambda s, g, _: (s, 0, 0))],
        [blk, pl.BlockSpec((1, 1, 2 * nt, size), lambda s, g, _: (s, g, 0, 0))],
        [sds((nt, rows, hc), BF), sds((seqs, pairs, 2 * nt, size), F32)],
        scratch=[pltpu.VMEM((nt, PAIR, size), BF)],
        flops=seqs * pairs * 2 * 4 * (nt * size) ** 2 * 128,
        nbytes=8 * nt * rows * hc,
        prefetch=1,
    )(slot_of, qkv, qkv, qkv, start)


def attn_bwd_kernel(
    nt, slot_ref, q_ref, k_ref, v_ref, go_ref, start_ref, lse_ref, cos_ref, sin_ref,
    gq_ref, gk_ref, gv_ref, kt_ref, dk_ref, dv_ref,
):
    size = q_ref.shape[1]
    scale = HEAD_DIM**-0.5
    for b in range(nt):
        kt_ref[b] = k_ref[slot_ref[b]].T
    dk_ref[...] = jnp.zeros_like(dk_ref)
    dv_ref[...] = jnp.zeros_like(dv_ref)
    lane = lax.broadcasted_iota(jnp.int32, (size, PAIR), 1)
    for p in range(nt):
        slot = slot_ref[p]
        q = q_ref[slot] * BF(scale)
        go = go_ref[slot]
        start = start_ref[0, pl.ds(slot, 1), :]
        outs = []
        for h in range(2):
            mine = (lane >= HEAD_DIM) == (h == 1)
            qh = jnp.where(mine, q, BF(0))
            goh = jnp.where(mine, go, BF(0))
            lse = lse_ref[0, 0, pl.ds(2 * p + h, 1), :]
            probs, grads = [], []
            inner = jnp.zeros((1, size), F32)
            for b in range(p + 1):
                key_slot = slot_ref[b]
                s = dot_nt(k_ref[key_slot], qh)
                s = jnp.where(allowed_block(start, b, p, size), s, MASKED_SCORE)
                e = jnp.exp(s - lse)
                g = dot_nt(v_ref[key_slot], goh)
                inner += jnp.sum(e * g, axis=0, keepdims=True)
                probs.append(e)
                grads.append(g)
            dqt = jnp.zeros((HEAD_DIM, size), F32)
            for b in range(p + 1):
                ds = (probs[b] * (grads[b] - inner)).astype(BF)
                dv_ref[b] += dot(probs[b].astype(BF), goh)
                dk_ref[b] += dot(ds, qh)
                dqt += dot(kt_ref[b, h * HEAD_DIM : (h + 1) * HEAD_DIM, :], ds)
            outs.append(dqt)
        dq = jnp.concatenate(outs, axis=0).T * scale
        gq_ref[slot] = unrotate(dq, cos_ref[slot], sin_ref[slot]).astype(BF)
    for b in range(nt):
        slot = slot_ref[b]
        gk_ref[slot] = unrotate(dk_ref[b], cos_ref[slot], sin_ref[slot]).astype(BF)
        gv_ref[slot] = dv_ref[b].astype(BF)


def attention_backward(qkv, go, start, lse, cos, sin, slot_of, nt):
    _, _, rows, hc = qkv.shape
    seqs = start.shape[0]
    size = rows // seqs
    pairs = hc // PAIR
    blk = pl.BlockSpec((nt, size, PAIR), lambda s, g, _: (0, s, g))
    table = pl.BlockSpec((nt, size, PAIR), lambda s, g, _: (0, s, 0))
    return call(
        functools.partial(attn_bwd_kernel, nt),
        (seqs, pairs),
        qkv_specs(nt, size)
        + [
            blk,
            pl.BlockSpec((1, nt, size), lambda s, g, _: (s, 0, 0)),
            pl.BlockSpec((1, 1, 2 * nt, size), lambda s, g, _: (s, g, 0, 0)),
            table, table,
        ],
        [blk, blk, blk],
        [sds((nt, rows, hc), BF)] * 3,
        scratch=[
            pltpu.VMEM((nt, PAIR, size), BF),
            pltpu.VMEM((nt, size, PAIR), F32),
            pltpu.VMEM((nt, size, PAIR), F32),
        ],
        flops=seqs * pairs * 2 * 10 * (nt * size) ** 2 * 128,
        nbytes=14 * nt * rows * hc,
        prefetch=1,
    )(slot_of, qkv, qkv, qkv, go, start, lse, cos, sin)


def shard_group(nd, count):
    while nd % count or nd // count % 2:
        count //= 2
    return max(count, 1)


def cols_out_kernel(nt, steps, lhs_ref, w_ref, *outs):
    for slot in range(nt):
        lhs = lhs_ref[slot]
        parts = [dot(lhs, w_ref[j]) for j in range(w_ref.shape[0])]
        store_piece(outs, nt, slot, steps, jnp.concatenate(parts, axis=1))


def mm_cols(lhs, weight, nt, group):
    nd, depth, ds = weight.shape
    group = shard_group(nd, group)
    rows = lhs.shape[1]
    width = nd * ds
    shapes = flat(piece_shapes(nt, rows, width))
    outs = call(
        functools.partial(cols_out_kernel, nt, nd // group),
        (nd // group,),
        [whole_spec(lhs.shape), pl.BlockSpec((group, depth, ds), lambda j: (j, 0, 0))],
        out_piece_specs(nt, rows, width, group * ds),
        [sds(s, BF) for s in shapes],
        flops=2 * nt * rows * depth * width,
        nbytes=2 * (nt * rows * (depth + width) + depth * width),
    )(lhs, weight)
    return regroup(outs, nt)


def cols_back_kernel(nt, steps, nlhs, nseen, *refs):
    lhs, w_refs, outs = refs[:nlhs], refs[nlhs : 2 * nlhs], refs[2 * nlhs + nseen :]
    depth = w_refs[0].shape[3]
    weights = [w[:, 0].reshape(-1, depth) for w in w_refs]
    sums = None
    for slot in range(nt):
        total = dot_nt(lhs[0][slot], weights[0])
        for c in range(1, nlhs):
            total += dot_nt(lhs[c][slot], weights[c])
        if nseen:
            part = jnp.sum(total * refs[2 * nlhs][slot].astype(F32), axis=0, keepdims=True)
            sums = part if sums is None else sums + part
        store_piece(outs[: len(outs) - nseen], nt, slot, steps, total)
    if nseen:
        outs[-1][...] = sums


def mm_back(lhs, weight, channels, nt, group, seen=None):
    nd, _, ds, depth = weight.shape
    count = len(lhs)
    group = shard_group(nd, group)
    rows = lhs[0].shape[1]
    width = nd * ds
    shapes = flat(piece_shapes(nt, rows, width))
    step = group * ds
    more = [] if seen is None else [seen]

    def spec(c):
        return pl.BlockSpec((group, 1, ds, depth), lambda j: (j, c, 0, 0))

    outs = call(
        functools.partial(cols_back_kernel, nt, nd // group, count, len(more)),
        (nd // group,),
        [whole_spec(a.shape) for a in lhs]
        + [spec(c) for c in channels]
        + [pl.BlockSpec((nt, rows, step), lambda j: (0, 0, j)) for _ in more],
        out_piece_specs(nt, rows, width, step) + [pl.BlockSpec((1, step), lambda j: (0, j)) for _ in more],
        [sds(s, BF) for s in shapes] + [sds((1, width), F32) for _ in more],
        flops=2 * nt * rows * depth * width * count,
        nbytes=2 * (nt * rows * (depth * count + width) + depth * width * count),
    )(*lhs, *[weight] * count, *more)
    return regroup(outs[: len(shapes)], nt), outs[len(shapes) :]


def gateup_kernel(nt, *refs):
    count = len(flat(piece_shapes(nt, 8, 8)))
    pieces, w_ref, (full_ref, silu_ref, slope_ref, hid_ref) = (
        refs[:count],
        refs[count],
        refs[count + 1 :],
    )

    @pl.when(pl.program_id(0) == 0)
    def _():
        fill_from_pieces(pieces, full_ref, nt)

    cols = hid_ref.shape[2]
    w_gate = w_ref[:, 0].reshape(-1, cols)
    w_up = w_ref[:, 1].reshape(-1, cols)
    for slot in range(nt):
        a2 = full_ref[slot]
        gate = dot(a2, w_gate)
        up = dot(a2, w_up)
        sig = 0.5 + 0.5 * jnp.tanh(0.5 * gate)
        silu = gate * sig
        silu_ref[slot] = silu.astype(BF)
        slope_ref[slot] = (up * (sig + silu - silu * sig)).astype(BF)
        hid_ref[slot] = (silu * up).astype(BF)


def gate_up(pieces, weight, nt):
    nd, _, ds, ff = weight.shape
    rows, width = pieces[0][0].shape
    step = min(512, ff)
    blk = pl.BlockSpec((nt, rows, step), lambda j: (0, 0, j))
    return call(
        functools.partial(gateup_kernel, nt),
        (ff // step,),
        [whole_spec(a.shape) for a in flat(pieces)]
        + [pl.BlockSpec((nd, 2, ds, step), lambda j: (0, 0, 0, j))],
        [whole_spec((nt, rows, width)), blk, blk, blk],
        [sds((nt, rows, width), BF)] + [sds((nt, rows, ff), BF)] * 3,
        flops=4 * nt * rows * width * ff,
        nbytes=2 * (2 * nt * rows * width + 2 * width * ff + 3 * nt * rows * ff),
    )(*flat(pieces), weight)


def gate_back_kernel(nt, full_ref, w_ref, silu_ref, slope_ref, gg_ref, gu_ref):
    weight = jnp.concatenate([w_ref[j] for j in range(w_ref.shape[0])], axis=1)
    for slot in range(nt):
        gh = dot_nt(full_ref[slot], weight)
        gg_ref[slot] = (gh * slope_ref[slot].astype(F32)).astype(BF)
        gu_ref[slot] = (gh * silu_ref[slot].astype(F32)).astype(BF)


def gate_back(full, weight, silu, slope, nt):
    nd, ff, ds = weight.shape
    _, rows, width = full.shape
    step = min(512, ff)
    blk = pl.BlockSpec((nt, rows, step), lambda j: (0, 0, j))
    return call(
        functools.partial(gate_back_kernel, nt),
        (ff // step,),
        [whole_spec(full.shape), pl.BlockSpec((nd, step, ds), lambda j: (0, j, 0)), blk, blk],
        [blk, blk],
        [sds((nt, rows, ff), BF)] * 2,
        flops=2 * nt * rows * width * ff,
        nbytes=2 * (nt * rows * width + width * ff + 4 * nt * rows * ff),
    )(full, weight, silu, slope)


def context_back_kernel(nt, *refs):
    pieces, w_ref, (full_ref, out_ref) = refs[:-3], refs[-3], refs[-2:]

    @pl.when(pl.program_id(0) == 0)
    def _():
        fill_from_pieces(pieces, full_ref, nt)

    weight = w_ref[:, 0].reshape(-1, w_ref.shape[3])
    for slot in range(nt):
        out_ref[slot] = dot(full_ref[slot], weight).astype(BF)


def context_back(pieces, weight, channel, nt):
    nd, _, ds, hc = weight.shape
    rows, width = pieces[0][0].shape
    step = min(256, hc)
    return call(
        functools.partial(context_back_kernel, nt),
        (hc // step,),
        [whole_spec(a.shape) for a in flat(pieces)]
        + [pl.BlockSpec((nd, 1, ds, step), lambda j: (0, channel, 0, j))],
        [whole_spec((nt, rows, width)), pl.BlockSpec((nt, rows, step), lambda j: (0, 0, j))],
        [sds((nt, rows, width), BF), sds((nt, rows, hc), BF)],
        flops=2 * nt * rows * width * hc,
        nbytes=2 * (2 * nt * rows * width + width * hc + nt * rows * hc),
    )(*flat(pieces), weight)


def middle_kernel(nterms, x_ref, gain_ref, *refs):
    terms, (mid_ref, low_ref) = refs[:nterms], refs[nterms:]
    mid = x_ref[...].astype(F32) + sum_terms(terms)
    mid_ref[...] = mid
    scale = lax.rsqrt(jnp.mean(mid * mid, axis=-1, keepdims=True) + NORM_EPS)
    low_ref[...] = (mid * scale * gain_ref[...]).astype(BF)


def make_middle(x, gain, terms):
    rows, width = x.shape
    tile = min(128, rows)
    blk = pl.BlockSpec((tile, width), lambda i: (i, 0))
    return call(
        functools.partial(middle_kernel, len(terms)),
        (rows // tile,),
        [blk, whole_spec(gain.shape)] + [blk] * len(terms),
        [blk, blk],
        [sds((rows, width), F32), sds((rows, width), BF)],
        nbytes=rows * width * (8 + 2 * len(terms)),
    )(x, gain, *terms)


def sum_terms(terms):
    total = terms[0][...].astype(F32)
    for t in terms[1:]:
        total += t[...].astype(F32)
    return total


def layer_out_kernel(nterms, mid_ref, *refs):
    refs[-1][...] = (mid_ref[...] + sum_terms(refs[:nterms])).astype(BF)


def place(group, groups, rows, tile, width, into):
    steps = rows // tile
    spec = pl.BlockSpec((tile, width), lambda i: (i + group * steps, 0))
    return spec, sds((groups * rows, width), BF), [] if into is None else [into]


def layer_out_rows(mid, terms, group, groups, into):
    rows, width = mid.shape
    tile = min(128, rows)
    blk = pl.BlockSpec((tile, width), lambda i: (i, 0))
    spec, shape, old = place(group, groups, rows, tile, width, into)
    return call(
        functools.partial(layer_out_kernel, len(terms)),
        (rows // tile,),
        [blk] * (1 + len(terms)) + [HBM] * len(old),
        spec,
        shape,
        nbytes=rows * width * (6 + 2 * len(terms)),
        aliases={1 + len(terms): 0} if old else None,
    )(mid, *terms, *old)


def out_middle_kernel(core_ref, own_ref, *refs):
    others, weights, (x_ref, gain_ref, mid_ref, low_ref) = refs[:3], refs[3:13], refs[13:]
    hc = own_ref.shape[2]
    half = x_ref.shape[1] // 2
    for part, own, (wx, wy, wd0, wd1) in (
        (core_ref[0], weights[0], weights[2:6]),
        (1 - core_ref[0], weights[1], weights[6:10]),
    ):
        total = dot_nt(own_ref[0], own[:, 0].reshape(-1, hc))
        total += dot_nt(others[0][...], wx[...])
        total += dot_nt(others[1][...], wy[...])
        diag = others[2][...]
        total += jnp.concatenate([dot_nt(diag, wd0[...]), dot_nt(diag, wd1[...])], axis=1)
        mid_ref[:, pl.ds(pl.multiple_of(part * half, half), half)] = total
    mid = x_ref[...].astype(F32) + mid_ref[...]
    mid_ref[...] = mid
    scale = lax.rsqrt(jnp.mean(mid * mid, axis=-1, keepdims=True) + NORM_EPS)
    low_ref[...] = (mid * scale * gain_ref[...]).astype(BF)


def out_middle(ctx, received, weights, x, gain):
    rows, width = x.shape
    hc = ctx.shape[2]
    return call(
        out_middle_kernel,
        (1,),
        [pl.BlockSpec((1, rows, hc), lambda i, core: (0, 0, 0))]
        + [whole_spec(a.shape) for a in received]
        + weights.specs()
        + [whole_spec(x.shape), whole_spec(gain.shape)],
        [whole_spec((rows, width))] * 2,
        [sds((rows, width), F32), sds((rows, width), BF)],
        flops=8 * rows * width * hc,
        nbytes=rows * (8 * width + 8 * hc) + 8 * width * hc,
        prefetch=1,
    )(weights.core, ctx, *received, *weights.arrays(), x, gain)


def norm_back_kernel(nterms, nouts, first_ref, v_ref, gain_ref, *refs):
    terms, outs, sums = refs[:nterms], refs[len(refs) - nouts :], []
    if nouts == 3:
        outs, sums = outs[:2], outs[2:]
    u = sum_terms(terms)
    v = v_ref[...].astype(F32)
    q = lax.rsqrt(jnp.mean(v * v, axis=-1, keepdims=True) + NORM_EPS)
    ug = u * gain_ref[...]
    inner = jnp.mean(ug * v, axis=-1, keepdims=True)
    grad = first_ref[...].astype(F32) + (q * ug - v * (q * q * q * inner))
    for out in outs:
        out[...] = grad.astype(out.dtype)
    for sum_ref in sums:

        @pl.when(pl.program_id(0) == 0)
        def _():
            sum_ref[...] = jnp.zeros_like(sum_ref)

        sum_ref[...] += jnp.sum(u * v * q, axis=0, keepdims=True)


def norm_back(first, v, gain, terms):
    rows, width = v.shape
    tile = min(128, rows)
    blk = pl.BlockSpec((tile, width), lambda i: (i, 0))
    return call(
        functools.partial(norm_back_kernel, len(terms), 3),
        (rows // tile,),
        [blk, blk, whole_spec(gain.shape)] + [blk] * len(terms),
        [blk, blk, pl.BlockSpec((1, width), lambda i: (0, 0))],
        [sds((rows, width), F32), sds((rows, width), BF), sds((1, width), F32)],
        nbytes=rows * width * (12 + 2 * len(terms)),
    )(first, v, gain, *terms)


def norm_back_rows(first, v, gain, terms, group, groups, into):
    rows, width = v.shape
    tile = min(128, rows)
    blk = pl.BlockSpec((tile, width), lambda i: (i, 0))
    spec, shape, old = place(group, groups, rows, tile, width, into)
    return call(
        functools.partial(norm_back_kernel, len(terms), 1),
        (rows // tile,),
        [blk, blk, whole_spec(gain.shape)] + [blk] * len(terms) + [HBM] * len(old),
        spec,
        shape,
        nbytes=rows * width * (12 + 2 * len(terms)),
        aliases={3 + len(terms): 0} if old else None,
    )(first, v, gain, *terms, *old)


def wgrad_rows_kernel(groups, which, nmore, *refs):
    nlhs = groups * (max(which) + 1)
    lhs, rhs, out_ref = refs[:nlhs], refs[nlhs : nlhs + groups * len(which)], refs[-1]
    tile = lhs[0].shape[2]
    left = [a[...].reshape(-1, tile).T for a in lhs]
    for c, w in enumerate(which):
        total = None
        for g in range(groups):
            a = left[w * groups + g]
            term = dot(a, rhs[c * groups + g][...].reshape(a.shape[1], -1))
            total = term if total is None else total + term
        out_ref[0, c * tile : (c + 1) * tile] = total.astype(BF)
    if nmore:
        out_ref[0, len(which) * tile :] = refs[-2][0]


def wgrad_rows(lhs, rhs, which, nd, more=None):
    groups = len(lhs[0])
    nt, rows, width = lhs[0][0].shape
    ds = width // nd
    n = rhs[0][0].shape[2]
    more = [] if more is None else [more]
    height = len(rhs) * ds + sum(a.shape[1] for a in more)
    return call(
        functools.partial(wgrad_rows_kernel, groups, which, len(more)),
        (nd,),
        [pl.BlockSpec((nt, rows, ds), lambda j: (0, 0, j))] * (groups * len(lhs))
        + [whole_spec(a.shape) for r in rhs for a in r]
        + [pl.BlockSpec((1,) + a.shape[1:], lambda j: (j, 0, 0)) for a in more],
        pl.BlockSpec((1, height, n), lambda j: (j, 0, 0)),
        sds((nd, height, n), BF),
        flops=2 * groups * nt * rows * width * n * len(rhs),
        nbytes=2 * groups * nt * rows * (width + n * len(rhs)) + 2 * width * n * len(rhs),
    )(*[a for l in lhs for a in l], *[a for r in rhs for a in r], *more)


def wgrad_cols_kernel(groups, nd, *refs):
    lhs, rhs, out_ref = refs[:groups], refs[groups:-1], refs[-1]
    tile = lhs[0].shape[2]
    ds = out_ref.shape[2]
    left = [a[...].reshape(-1, tile).T for a in lhs]
    total = None
    for g in range(groups):
        term = dot(left[g], rhs[g][...].reshape(left[g].shape[1], -1))
        total = term if total is None else total + term
    for j in range(nd):
        out_ref[j] = total[:, j * ds : (j + 1) * ds].astype(BF)


def wgrad_cols(lhs, rhs, nd):
    groups = len(lhs)
    nt, rows, m = lhs[0].shape
    width = rhs[0].shape[2]
    tile = min(256, m)
    return call(
        functools.partial(wgrad_cols_kernel, groups, nd),
        (m // tile,),
        [pl.BlockSpec((nt, rows, tile), lambda i: (0, 0, i))] * groups
        + [whole_spec(a.shape) for a in rhs],
        pl.BlockSpec((nd, tile, width // nd), lambda i: (0, i, 0)),
        sds((nd, m, width // nd), BF),
        flops=2 * groups * nt * rows * width * m,
        nbytes=2 * groups * nt * rows * (width + m) + 2 * width * m,
    )(*lhs, *rhs)


def doc_starts(segments):
    row_len = segments.shape[-1]
    ids = jnp.arange(row_len, dtype=jnp.int32)
    change = jnp.concatenate(
        [jnp.ones_like(segments[:, :1], dtype=bool), segments[:, 1:] != segments[:, :-1]], axis=1
    )
    return lax.cummax(jnp.where(change, ids[None, :], 0), axis=1)


def tensor_sum(value, nt):
    if nt != 4:
        return lax.psum(value, "tensor")
    value = value + lax.ppermute(value, "tensor", swap_perm(4, 1))
    return value + lax.ppermute(value, "tensor", swap_perm(4, 2))


def slot_order(blocks, index, nt):
    if nt != 4:
        return blocks
    pairs = jnp.stack([blocks[:, 1], blocks[:, 0], blocks[:, 3], blocks[:, 2]], axis=1)
    blocks = jnp.where(index % 2 == 1, pairs, blocks)
    halves = jnp.stack([blocks[:, 2], blocks[:, 3], blocks[:, 0], blocks[:, 1]], axis=1)
    return jnp.where(index // 2 == 1, halves, blocks)


def per_device(nd, nt, groups, layer_input, segments, qkv_w, out_w, gain1, gateup_w, down_w, gain2, grad_out):
    seqs, local, width = layer_input.shape
    per = seqs // groups
    index = lax.axis_index("tensor").astype(jnp.int32)
    blocks = jnp.arange(nt, dtype=jnp.int32)
    slot_of = blocks ^ index if nt == 4 else blocks

    x = [layer_input[g * per : (g + 1) * per].reshape(per * local, width) for g in range(groups)]
    go = [grad_out[g * per : (g + 1) * per].reshape(per * local, width) for g in range(groups)]
    Order.last = None
    x_all = Gather(layer_input.reshape(seqs * local, width), nt)

    gains = lax.all_gather(jnp.stack([gain1, gain2]), "dp", axis=1, tiled=True).astype(F32)
    g1, g2 = gains[:1], gains[1:]
    qkvo_w = jnp.concatenate([qkv_w, out_w.T[None]])
    full_qkvo = lax.all_gather(qkvo_w, "dp", axis=0, tiled=False)
    full_gateup = lax.all_gather(gateup_w, "dp", axis=0, tiled=False)
    full_down = lax.all_gather(down_w, "dp", axis=0, tiled=False)

    start_abs = doc_starts(segments)
    pos_abs = jnp.arange(segments.shape[1], dtype=jnp.int32)[None, :] - start_abs
    start_slot = slot_order(start_abs.reshape(seqs, nt, local), index, nt)
    pos_slot = slot_order(pos_abs.reshape(seqs, nt, local), index, nt)
    inv_freq = ROPE_BASE ** (-jnp.arange(HALF, dtype=F32) * 2.0 / HEAD_DIM)
    angles = pos_slot.astype(F32)[..., None] * inv_freq
    cos, sin = jnp.cos(angles), jnp.sin(angles)
    cos = jnp.concatenate([cos] * 4, axis=-1)
    sin = jnp.concatenate([-sin, sin] * 2, axis=-1)

    def table(t, g):
        t = t[g * per : (g + 1) * per]
        return jnp.swapaxes(t, 0, 1).reshape(nt, per * local, PAIR)

    coss = [table(cos, g) for g in range(groups)]
    sins = [table(sin, g) for g in range(groups)]
    starts = [start_slot[g * per : (g + 1) * per] for g in range(groups)]

    both = range(groups)
    swap_heads = nt == 4 and nd % 4 == 0
    received = {}
    qkv, ctx, lse, mid, low2, g_mid, g_low = ({} for _ in range(7))
    attn_sum, a2_all, ga2, out_sum, ga1 = ({} for _ in range(5))
    sum1, sum2, gm_all, gmf, g_qkv, g_ctx = ({} for _ in range(6))

    def dp_sum(grad):
        return lax.psum_scatter(grad, "dp", scatter_dimension=0, tiled=False)

    def project(g):
        qkv[g] = project_qkv(a1[g], full_qkvo, coss[g], sins[g], nt)

    def attend(g):
        ctx[g], lse[g] = attention_forward(qkv[g], starts[g], slot_of, nt)
        if swap_heads:
            received[g] = exchange_slots(ctx[g])
            return
        attn_sum[g] = Scatter(mm_back([ctx[g]], full_qkvo, [3], nt, 4)[0], nt)

    def middle(g):
        if swap_heads:
            mid[g], low2[g] = out_middle(ctx[g], received[g], head_weights, x[g], g2)
        else:
            attn_sum[g].second()
            mid[g], low2[g] = make_middle(x[g], g2, attn_sum[g].terms)
        a2_all[g] = Gather(low2[g], nt)

    def second_back(g):
        ga2[g] = Scatter(mm_back([gg[g], gu[g]], full_gateup, [0, 1], nt, 2)[0], nt)

    def project_out(g):
        out_sum[g] = Scatter(mm_cols(hid[g], full_down, nt, 2), nt)

    def residual_back(g):
        g_mid[g], g_low[g], sum2[g] = norm_back(go[g], mid[g], g2, ga2[g].terms)
        gm_all[g] = Gather(g_low[g], nt)

    def attention_back_start(g):
        gmf[g], g_ctx[g] = context_back(gm_all[g].pieces, full_qkvo, 3, nt)

    def attention_back(g):
        g_qkv[g] = attention_backward(
            qkv[g], g_ctx[g], starts[g], lse[g], coss[g], sins[g], slot_of, nt
        )

    def input_back(g):
        parts, (sum1[g],) = mm_back(g_qkv[g], full_qkvo, [0, 1, 2], nt, 4, a1[g])
        ga1[g] = Scatter(parts, nt)

    def up_projection(g):
        a2[g], silu[g], slope[g], hid[g] = gate_up(a2_all[g].pieces, full_gateup, nt)

    def hidden_back(g):
        gg[g], gu[g] = gate_back(gof[g], full_down, silu[g], slope[g], nt)

    def finish(g, grad_input):
        return norm_back_rows(g_mid[g], x[g], g1, ga1[g].terms, g, groups, grad_input)

    def by_group(held):
        return [held[g] for g in both]

    def gather_cotangent(g):
        go_all[g] = Gather(link(go[g], flat(x_all.pieces)[-1]), nt)

    a2, silu, slope, hid, gg, gu, go_all, gof = ({} for _ in range(8))
    x_all.second()
    gather_cotangent(1)
    a1 = [assemble(x_all.pieces, nt, 0, groups, g1, coss + sins)]
    if swap_heads:
        head_weights = HeadWeights(full_qkvo, 3, nd)
    gather_cotangent(0)
    project(0)
    a1.append(assemble(x_all.pieces, nt, 1, groups, g1))
    if swap_heads:
        head_weights.second()
    attend(0)
    go_all[1].second()
    project(1)
    middle(0)
    attend(1)
    a2_all[0].second()
    gof[1] = assemble(go_all[1].pieces, nt, 0, 1)
    middle(1)
    go_all[0].second()
    up_projection(0)
    a2_all[1].second()
    gof[0] = assemble(go_all[0].pieces, nt, 0, 1)
    up_projection(1)
    grad_down = dp_sum(wgrad_cols(by_group(hid), by_group(gof), nd))
    hidden_back(0)
    second_back(0)
    hidden_back(1)
    ga2[0].second()
    second_back(1)
    residual_back(0)
    grad_gateup = wgrad_rows([by_group(a2)], [by_group(gg), by_group(gu)], [0, 0], nd)
    ga2[1].second()
    gm_all[0].second()
    grad_gateup = dp_sum(link(grad_gateup, grad_down))
    project_out(0)
    residual_back(1)
    project_out(1)
    attention_back_start(0)
    attention_back(0)
    gm_all[1].second()
    out_sum[0].second()
    input_back(0)
    attention_back_start(1)
    attention_back(1)
    layer_out = layer_out_rows(mid[0], out_sum[0].terms, 0, groups, None)
    input_back(1)
    ds = gain1.shape[0]
    gains = tensor_sum(jnp.concatenate([(sum1[0] + sum1[1]) / g1, sum2[0] + sum2[1]]), nt)
    gains = jnp.swapaxes(gains.reshape(2, nd, ds), 0, 1).astype(BF)
    gains = jnp.pad(gains, ((0, 0), (0, 14), (0, qkv_w.shape[2] - ds)))
    out_sum[1].second()
    grad_qkvo = wgrad_rows(
        [a1, by_group(gmf)],
        [[g_qkv[g][c] for g in both] for c in range(3)] + [by_group(ctx)],
        [0, 0, 0, 1],
        nd,
        gains,
    )
    ga1[0].second()
    ga1[1].second()
    grad_qkvo = dp_sum(link(grad_qkvo, grad_gateup))
    grad_input = finish(0, None)
    layer_out = layer_out_rows(mid[1], out_sum[1].terms, 1, groups, layer_out)
    grad_input = finish(1, grad_input)
    return (
        layer_out.reshape(seqs, local, width),
        grad_input.reshape(seqs, local, width),
        grad_qkvo[: 3 * ds].astype(F32).reshape(3, ds, -1),
        grad_qkvo[3 * ds : 4 * ds].T.astype(F32),
        grad_qkvo[4 * ds, :ds].astype(F32),
        grad_gateup.astype(F32).reshape(2, ds, -1),
        grad_down.astype(F32),
        grad_qkvo[4 * ds + 1, :ds].astype(F32),
    )


def solution(mesh):
    nd, nt = mesh.shape["dp"], mesh.shape["tensor"]
    return jax.shard_map(
        functools.partial(per_device, nd, nt, 2),
        mesh=mesh,
        in_specs=(
            P("dp", "tensor", None),
            P("dp", None),
            P(None, "dp", "tensor"),
            P("tensor", "dp"),
            P("dp"),
            P(None, "dp", "tensor"),
            P("tensor", "dp"),
            P("dp"),
            P("dp", "tensor", None),
        ),
        out_specs=(
            P("dp", "tensor", None),
            P("dp", "tensor", None),
            P(None, "dp", "tensor"),
            P("tensor", "dp"),
            P("dp"),
            P(None, "dp", "tensor"),
            P("tensor", "dp"),
            P("dp"),
        ),
        check_vma=False,
    )
```

```python
import functools

import jax
import jax.numpy as jnp
import numpy as np
from jax import lax
from jax.experimental import pallas as pl
from jax.experimental.pallas import tpu as pltpu
from jax.sharding import PartitionSpec as P

HEAD_DIM = 64
HALF = HEAD_DIM // 2
PAIR = 2 * HEAD_DIM
NORM_EPS = 1e-05
ROPE_BASE = 130000.0
MASKED_SCORE = -1e30
BF = jnp.bfloat16
F32 = jnp.float32
VMEM_SLACK = 8 * 1024 * 1024
VMEM_SMALL = 24 * 1024 * 1024
VMEM_LARGE = 40 * 1024 * 1024
PIN_BYTES = 3 * 1024 * 1024
PIN_BYTES_LARGE = 1024 * 1024
SMALL = 3

NT = (((1,), (1,)), ((), ()))


def dot(a, b):
    return jnp.dot(a, b, preferred_element_type=F32)


def dot_nt(a, b):
    return lax.dot_general(a, b, NT, preferred_element_type=F32)


class Order:
    last = None


HBM = pl.BlockSpec(memory_space=pltpu.HBM)
ANY = pl.BlockSpec(memory_space=pl.ANY)


def is_large(array, least=None):
    return array.size * array.dtype.itemsize >= (least or PIN_BYTES)


def pin(array, least=None):
    return pltpu.with_memory_space_constraint(array, pltpu.HBM) if is_large(array, least) else array


def pinned(shape):
    return pltpu.HBM(shape.shape, shape.dtype) if is_large(shape) else shape


def block_bytes(spec, dtype):
    if spec.block_shape is None:
        return 0
    count = 2 if spec.pipeline_mode is None else spec.pipeline_mode.buffer_count
    return count * int(np.prod([d for d in spec.block_shape if d])) * np.dtype(dtype).itemsize


def call(body, grid, in_specs, out_specs, out_shape, scratch=(), flops=0, nbytes=0, aliases=None, prefetch=0):
    first_extra = prefetch + len(in_specs)
    many = isinstance(out_shape, (list, tuple))
    out_blocks = list(zip(out_specs, out_shape)) if many else [(out_specs, out_shape)]

    def run(*args):
        extra = [] if Order.last is None or any(a is Order.last for a in args) else [pin(Order.last)]

        blocks = list(zip(in_specs, args[prefetch:])) + out_blocks
        vmem = VMEM_SLACK + sum(block_bytes(spec, a.dtype) for spec, a in blocks)
        vmem += sum(int(np.prod(m.shape)) * np.dtype(m.dtype).itemsize for m in scratch)
        least = PIN_BYTES
        if vmem > VMEM_SMALL:
            vmem, least = VMEM_LARGE, PIN_BYTES_LARGE

        args = [pin(a, least) for a in args]

        def ordered_body(*refs):
            body(*refs[:first_extra], *refs[first_extra + len(extra) :])

        outs = pl.pallas_call(
            ordered_body,
            grid_spec=pltpu.PrefetchScalarGridSpec(
                num_scalar_prefetch=prefetch,
                grid=grid,
                in_specs=in_specs + [ANY] * len(extra),
                out_specs=out_specs,
                scratch_shapes=list(scratch),
            ),
            out_shape=[pinned(a) for a in out_shape] if many else pinned(out_shape),
            input_output_aliases=aliases or {},
            cost_estimate=pl.CostEstimate(flops=flops // SMALL, bytes_accessed=nbytes // SMALL, transcendentals=0),
            compiler_params=pltpu.CompilerParams(vmem_limit_bytes=vmem),
        )(*args, *extra)
        Order.last = outs[-1] if isinstance(outs, (list, tuple)) else outs
        return outs

    return run


def link_kernel(value_ref, done_ref, out_ref):
    pass


def link(value, done):
    return call(link_kernel, (1,), [HBM, HBM], HBM, sds(value.shape, value.dtype), aliases={0: 0})(value, done)


def whole_spec(shape, buffers=1):
    zeros = (0,) * len(shape)
    return pl.BlockSpec(shape, lambda *_: zeros, pipeline_mode=pl.Buffered(buffers))


def sds(shape, dtype):
    return jax.ShapeDtypeStruct(shape, dtype)


def swap_perm(count, bit):
    return [(i, i ^ bit) for i in range(count)]


def halves_kernel(y_ref, x_ref, left_ref, right_ref):
    left_ref[...] = y_ref[...]
    right_ref[...] = x_ref[...]


def halves(from_y, from_x):
    rows, width = from_y.shape
    half = width // 2
    tile = min(128, rows)

    def spec(which):
        return pl.BlockSpec((tile, half), lambda i: (i, which))

    return call(
        halves_kernel,
        (rows // tile,),
        [spec(0), spec(1)],
        [spec(0), spec(0)],
        [sds((rows, half), BF)] * 2,
        nbytes=rows * half * 8,
    )(from_y, from_x)


class Gather:
    def __init__(self, block, nt, direct=False):
        self.nt = nt
        if nt != 4:
            full = lax.all_gather(block, "tensor", axis=0, tiled=False)
            self.pieces = [(full[r],) for r in range(nt)]
            return
        self.block = block
        self.from_x = lax.ppermute(block, "tensor", swap_perm(4, 1))
        self.from_y = lax.ppermute(block, "tensor", swap_perm(4, 2))
        if direct:
            diag = lax.ppermute(block, "tensor", swap_perm(4, 3))
            self.pieces = [(block,), (self.from_x,), (self.from_y,), (diag,)]

    def second(self):
        if self.nt != 4:
            return
        left, right = halves(self.from_y, self.from_x)
        diag_x = lax.ppermute(left, "tensor", swap_perm(4, 1))
        diag_y = lax.ppermute(right, "tensor", swap_perm(4, 2))
        self.pieces = [(self.block,), (self.from_x,), (self.from_y,), (diag_x, diag_y)]


def add_halves_kernel(x_ref, for_x_ref, y_ref, for_y_ref, out_x_ref, out_y_ref):
    out_x_ref[...] = (x_ref[...].astype(F32) + for_x_ref[...].astype(F32)).astype(BF)
    out_y_ref[...] = (y_ref[...].astype(F32) + for_y_ref[...].astype(F32)).astype(BF)


def add_halves(to_x, for_x, to_y, for_y):
    rows, width = to_x.shape
    half = width // 2
    tile = min(128, rows)

    def spec(which):
        return pl.BlockSpec((tile, half), lambda i: (i, which))

    return call(
        add_halves_kernel,
        (rows // tile,),
        [spec(1), spec(0), spec(0), spec(0)],
        [spec(1), spec(0)],
        [sds(to_x.shape, BF)] * 2,
        nbytes=rows * half * 12,
        aliases={0: 0, 2: 1},
    )(to_x, for_x, to_y, for_y)


class Scatter:
    def __init__(self, parts, nt):
        self.nt = nt
        if nt != 4:
            full = jnp.stack([p[0] for p in parts])
            self.terms = [lax.psum_scatter(full, "tensor", scatter_dimension=0, tiled=False)]
            return
        (self.own,), (self.to_x,), (self.to_y,), (diag_x, diag_y) = parts
        self.for_y = lax.ppermute(diag_x, "tensor", swap_perm(4, 1))
        self.for_x = lax.ppermute(diag_y, "tensor", swap_perm(4, 2))

    def second(self):
        if self.nt != 4:
            return
        to_x, to_y = add_halves(self.to_x, self.for_x, self.to_y, self.for_y)
        self.terms = [
            self.own,
            lax.ppermute(to_x, "tensor", swap_perm(4, 1)),
            lax.ppermute(to_y, "tensor", swap_perm(4, 2)),
        ]


def piece_shapes(nt, rows, width):
    if nt != 4:
        return [((rows, width),)] * nt
    return [((rows, width),)] * 3 + [((rows, width // 2),) * 2]


def flat(pieces):
    return [a for p in pieces for a in p]


def regroup(items, nt):
    if len(items) == nt:
        return [(a,) for a in items]
    return [(items[0],), (items[1],), (items[2],), (items[3], items[4])]


def fill_from_pieces(refs, full_ref, nt):
    for slot, part in enumerate(regroup(refs, nt)):
        if len(part) == 1:
            full_ref[slot] = part[0][...]
        else:
            half = part[0].shape[1]
            full_ref[slot, :, :half] = part[0][...]
            full_ref[slot, :, half:] = part[1][...]


def out_piece_specs(nt, rows, width, step):
    specs = []
    half_steps = width // step // 2
    for part in piece_shapes(nt, rows, width):
        if len(part) == 1:
            specs.append(pl.BlockSpec((rows, step), lambda j: (0, j)))
        else:
            specs.append(pl.BlockSpec((rows, step), lambda j: (0, jnp.minimum(j, half_steps - 1))))
            specs.append(pl.BlockSpec((rows, step), lambda j: (0, jnp.maximum(j - half_steps, 0))))
    return specs


def store_piece(outs, nt, slot, steps, value):
    part = regroup(outs, nt)[slot]
    if len(part) == 1:
        part[0][...] = value.astype(BF)
    else:
        j = pl.program_id(0)

        @pl.when(j < steps // 2)
        def _():
            part[0][...] = value.astype(BF)

        @pl.when(j >= steps // 2)
        def _():
            part[1][...] = value.astype(BF)


def turn(v):
    lane = lax.broadcasted_iota(jnp.int32, v.shape, 1)
    return jnp.where(lane % HEAD_DIM < HALF, pltpu.roll(v, PAIR - HALF, 1), pltpu.roll(v, HALF, 1))


def rotate(v, cos, sin):
    return v * cos + turn(v) * sin


def unrotate(u, cos, sin):
    return u * cos + turn(u * sin)


def assemble_kernel(nt, count, normed, *refs):
    full_ref = refs[-1]
    fill_from_pieces(refs[:count], full_ref, nt)
    if normed:
        gain = refs[count][...]
        for slot in range(nt):
            x = full_ref[slot].astype(F32)
            scale = lax.rsqrt(jnp.mean(x * x, axis=-1, keepdims=True) + NORM_EPS)
            full_ref[slot] = (x * scale * gain).astype(BF)


def assemble(pieces, nt, group, groups, gain=None, ready=()):
    rows, width = pieces[0][0].shape
    rows //= groups
    tile = min(64, rows)
    first = group * (rows // tile)
    items = flat(pieces)
    extra = [] if gain is None else [gain]
    return call(
        functools.partial(assemble_kernel, nt, len(items), len(extra)),
        (rows // tile,),
        [pl.BlockSpec((tile, a.shape[1]), lambda i: (i + first, 0)) for a in items]
        + [whole_spec(a.shape) for a in extra]
        + [ANY] * len(ready),
        pl.BlockSpec((nt, tile, width), lambda i: (0, i, 0)),
        sds((nt, rows, width), BF),
        nbytes=4 * nt * rows * width,
    )(*items, *extra, *ready)


def qkv_kernel(nt, a1_ref, w_ref, cos_ref, sin_ref, out_ref):
    cols = out_ref.shape[3]
    weight = w_ref[:, 0].reshape(-1, cols)

    @pl.when(pl.program_id(0) < 2)
    def _():
        for slot in range(nt):
            raw = dot(a1_ref[slot], weight)
            cos, sin = cos_ref[slot], sin_ref[slot]
            for p in range(cols // PAIR):
                part = slice(p * PAIR, (p + 1) * PAIR)
                out_ref[0, slot, :, part] = rotate(raw[:, part], cos, sin).astype(BF)

    @pl.when(pl.program_id(0) == 2)
    def _():
        for slot in range(nt):
            out_ref[0, slot] = dot(a1_ref[slot], weight).astype(BF)


def project_qkv(a1, weight, cos, sin, nt):
    nd, _, ds, hc = weight.shape
    _, rows, width = a1.shape
    return call(
        functools.partial(qkv_kernel, nt),
        (3,),
        [
            whole_spec(a1.shape),
            pl.BlockSpec((nd, 1, ds, hc), lambda c: (0, c, 0, 0)),
            whole_spec(cos.shape),
            whole_spec(sin.shape),
        ],
        pl.BlockSpec((1, nt, rows, hc), lambda c: (c, 0, 0, 0)),
        sds((3, nt, rows, hc), BF),
        flops=2 * nt * rows * width * hc * 3,
        nbytes=2 * (nt * rows * width + 3 * width * hc + 3 * nt * rows * hc),
    )(a1, weight, cos, sin)


def allowed_block(start, key_block, query_block, size):
    key_id = lax.broadcasted_iota(jnp.int32, (size, size), 0) + key_block * size
    ok = key_id >= start
    if key_block == query_block:
        ok &= lax.broadcasted_iota(jnp.int32, (size, size), 1) + query_block * size >= key_id
    return ok


def attn_fwd_kernel(nt, slot_ref, q_ref, k_ref, v_ref, start_ref, ctx_ref, lse_ref, vt_ref):
    size = q_ref.shape[1]
    for b in range(nt):
        vt_ref[b] = v_ref[slot_ref[b]].T
    lane = lax.broadcasted_iota(jnp.int32, (size, PAIR), 1)
    for p in range(nt):
        slot = slot_ref[p]
        q = q_ref[slot] * BF(HEAD_DIM**-0.5)
        start = start_ref[0, pl.ds(slot, 1), :]
        outs = []
        for h in range(2):
            qh = jnp.where((lane >= HEAD_DIM) == (h == 1), q, BF(0))
            scores = []
            for b in range(p + 1):
                s = dot_nt(k_ref[slot_ref[b]], qh)
                scores.append(jnp.where(allowed_block(start, b, p, size), s, MASKED_SCORE))
            top = functools.reduce(
                jnp.maximum, [jnp.max(s, axis=0, keepdims=True) for s in scores]
            )
            total = jnp.zeros((1, size), F32)
            acc = jnp.zeros((HEAD_DIM, size), F32)
            for b, s in enumerate(scores):
                e = jnp.exp(s - top)
                total += jnp.sum(e, axis=0, keepdims=True)
                acc += dot(vt_ref[b, h * HEAD_DIM : (h + 1) * HEAD_DIM, :], e.astype(BF))
            outs.append(acc / total)
            lse_ref[0, 0, pl.ds(2 * p + h, 1), :] = top + jnp.log(total)
        ctx_ref[slot] = jnp.concatenate(outs, axis=0).T.astype(BF)


def qkv_specs(nt, size):
    def spec(c):
        return pl.BlockSpec((None, nt, size, PAIR), lambda s, g, _: (c, 0, s, g))

    return [spec(c) for c in range(3)]


def attention_forward(qkv, start, slot_of, nt):
    _, _, rows, hc = qkv.shape
    seqs = start.shape[0]
    size = rows // seqs
    pairs = hc // PAIR
    blk = pl.BlockSpec((nt, size, PAIR), lambda s, g, _: (0, s, g))
    return call(
        functools.partial(attn_fwd_kernel, nt),
        (seqs, pairs),
        qkv_specs(nt, size) + [pl.BlockSpec((1, nt, size), lambda s, g, _: (s, 0, 0))],
        [blk, pl.BlockSpec((1, 1, 2 * nt, size), lambda s, g, _: (s, g, 0, 0))],
        [sds((nt, rows, hc), BF), sds((seqs, pairs, 2 * nt, size), F32)],
        scratch=[pltpu.VMEM((nt, PAIR, size), BF)],
        flops=seqs * pairs * 2 * 4 * (nt * size) ** 2 * 128,
        nbytes=8 * nt * rows * hc,
        prefetch=1,
    )(slot_of, qkv, qkv, qkv, start)


def attn_bwd_kernel(
    nt, slot_ref, q_ref, k_ref, v_ref, go_ref, start_ref, lse_ref, cos_ref, sin_ref,
    gq_ref, gk_ref, gv_ref, kt_ref, dk_ref, dv_ref,
):
    size = q_ref.shape[1]
    scale = HEAD_DIM**-0.5
    for b in range(nt):
        kt_ref[b] = k_ref[slot_ref[b]].T
    dk_ref[...] = jnp.zeros_like(dk_ref)
    dv_ref[...] = jnp.zeros_like(dv_ref)
    lane = lax.broadcasted_iota(jnp.int32, (size, PAIR), 1)
    for p in range(nt):
        slot = slot_ref[p]
        q = q_ref[slot] * BF(scale)
        go = go_ref[slot]
        start = start_ref[0, pl.ds(slot, 1), :]
        outs = []
        for h in range(2):
            mine = (lane >= HEAD_DIM) == (h == 1)
            qh = jnp.where(mine, q, BF(0))
            goh = jnp.where(mine, go, BF(0))
            lse = lse_ref[0, 0, pl.ds(2 * p + h, 1), :]
            probs, grads = [], []
            inner = jnp.zeros((1, size), F32)
            for b in range(p + 1):
                key_slot = slot_ref[b]
                s = dot_nt(k_ref[key_slot], qh)
                s = jnp.where(allowed_block(start, b, p, size), s, MASKED_SCORE)
                e = jnp.exp(s - lse)
                g = dot_nt(v_ref[key_slot], goh)
                inner += jnp.sum(e * g, axis=0, keepdims=True)
                probs.append(e)
                grads.append(g)
            dqt = jnp.zeros((HEAD_DIM, size), F32)
            for b in range(p + 1):
                ds = (probs[b] * (grads[b] - inner)).astype(BF)
                dv_ref[b] += dot(probs[b].astype(BF), goh)
                dk_ref[b] += dot(ds, qh)
                dqt += dot(kt_ref[b, h * HEAD_DIM : (h + 1) * HEAD_DIM, :], ds)
            outs.append(dqt)
        dq = jnp.concatenate(outs, axis=0).T * scale
        gq_ref[slot] = unrotate(dq, cos_ref[slot], sin_ref[slot]).astype(BF)
    for b in range(nt):
        slot = slot_ref[b]
        gk_ref[slot] = unrotate(dk_ref[b], cos_ref[slot], sin_ref[slot]).astype(BF)
        gv_ref[slot] = dv_ref[b].astype(BF)


def attention_backward(qkv, go, start, lse, cos, sin, slot_of, nt):
    _, _, rows, hc = qkv.shape
    seqs = start.shape[0]
    size = rows // seqs
    pairs = hc // PAIR
    blk = pl.BlockSpec((nt, size, PAIR), lambda s, g, _: (0, s, g))
    table = pl.BlockSpec((nt, size, PAIR), lambda s, g, _: (0, s, 0))
    return call(
        functools.partial(attn_bwd_kernel, nt),
        (seqs, pairs),
        qkv_specs(nt, size)
        + [
            blk,
            pl.BlockSpec((1, nt, size), lambda s, g, _: (s, 0, 0)),
            pl.BlockSpec((1, 1, 2 * nt, size), lambda s, g, _: (s, g, 0, 0)),
            table, table,
        ],
        [blk, blk, blk],
        [sds((nt, rows, hc), BF)] * 3,
        scratch=[
            pltpu.VMEM((nt, PAIR, size), BF),
            pltpu.VMEM((nt, size, PAIR), F32),
            pltpu.VMEM((nt, size, PAIR), F32),
        ],
        flops=seqs * pairs * 2 * 10 * (nt * size) ** 2 * 128,
        nbytes=14 * nt * rows * hc,
        prefetch=1,
    )(slot_of, qkv, qkv, qkv, go, start, lse, cos, sin)


def shard_group(nd, count):
    while nd % count or nd // count % 2:
        count //= 2
    return max(count, 1)


def cols_out_kernel(nt, steps, lhs_ref, w_ref, *outs):
    for slot in range(nt):
        lhs = lhs_ref[slot]
        parts = [dot(lhs, w_ref[j]) for j in range(w_ref.shape[0])]
        store_piece(outs, nt, slot, steps, jnp.concatenate(parts, axis=1))


def mm_cols(lhs, weight, nt, group):
    nd, depth, ds = weight.shape
    group = shard_group(nd, group)
    rows = lhs.shape[1]
    width = nd * ds
    shapes = flat(piece_shapes(nt, rows, width))
    outs = call(
        functools.partial(cols_out_kernel, nt, nd // group),
        (nd // group,),
        [whole_spec(lhs.shape), pl.BlockSpec((group, depth, ds), lambda j: (j, 0, 0))],
        out_piece_specs(nt, rows, width, group * ds),
        [sds(s, BF) for s in shapes],
        flops=2 * nt * rows * depth * width,
        nbytes=2 * (nt * rows * (depth + width) + depth * width),
    )(lhs, weight)
    return regroup(outs, nt)


def cols_back_kernel(nt, steps, nlhs, nseen, *refs):
    lhs, w_refs, outs = refs[:nlhs], refs[nlhs : 2 * nlhs], refs[2 * nlhs + nseen :]
    depth = w_refs[0].shape[3]
    weights = [w[:, 0].reshape(-1, depth) for w in w_refs]
    sums = None
    for slot in range(nt):
        total = dot_nt(lhs[0][slot], weights[0])
        for c in range(1, nlhs):
            total += dot_nt(lhs[c][slot], weights[c])
        if nseen:
            part = jnp.sum(total * refs[2 * nlhs][slot].astype(F32), axis=0, keepdims=True)
            sums = part if sums is None else sums + part
        store_piece(outs[: len(outs) - nseen], nt, slot, steps, total)
    if nseen:
        outs[-1][...] = sums


def mm_back(lhs, weight, channels, nt, group, seen=None):
    nd, _, ds, depth = weight.shape
    count = len(lhs)
    group = shard_group(nd, group)
    rows = lhs[0].shape[1]
    width = nd * ds
    shapes = flat(piece_shapes(nt, rows, width))
    step = group * ds
    more = [] if seen is None else [seen]

    def spec(c):
        return pl.BlockSpec((group, 1, ds, depth), lambda j: (j, c, 0, 0))

    outs = call(
        functools.partial(cols_back_kernel, nt, nd // group, count, len(more)),
        (nd // group,),
        [whole_spec(a.shape) for a in lhs]
        + [spec(c) for c in channels]
        + [pl.BlockSpec((nt, rows, step), lambda j: (0, 0, j)) for _ in more],
        out_piece_specs(nt, rows, width, step) + [pl.BlockSpec((1, step), lambda j: (0, j)) for _ in more],
        [sds(s, BF) for s in shapes] + [sds((1, width), F32) for _ in more],
        flops=2 * nt * rows * depth * width * count,
        nbytes=2 * (nt * rows * (depth * count + width) + depth * width * count),
    )(*lhs, *[weight] * count, *more)
    return regroup(outs[: len(shapes)], nt), outs[len(shapes) :]


def gateup_kernel(nt, *refs):
    count = len(flat(piece_shapes(nt, 8, 8)))
    pieces, w_ref, (full_ref, silu_ref, slope_ref, hid_ref) = (
        refs[:count],
        refs[count],
        refs[count + 1 :],
    )

    @pl.when(pl.program_id(0) == 0)
    def _():
        fill_from_pieces(pieces, full_ref, nt)

    cols = hid_ref.shape[2]
    w_gate = w_ref[:, 0].reshape(-1, cols)
    w_up = w_ref[:, 1].reshape(-1, cols)
    for slot in range(nt):
        a2 = full_ref[slot]
        gate = dot(a2, w_gate)
        up = dot(a2, w_up)
        sig = 0.5 + 0.5 * jnp.tanh(0.5 * gate)
        silu = gate * sig
        silu_ref[slot] = silu.astype(BF)
        slope_ref[slot] = (up * (sig + silu - silu * sig)).astype(BF)
        hid_ref[slot] = (silu * up).astype(BF)


def gate_up(pieces, weight, nt):
    nd, _, ds, ff = weight.shape
    rows, width = pieces[0][0].shape
    step = min(512, ff)
    blk = pl.BlockSpec((nt, rows, step), lambda j: (0, 0, j))
    return call(
        functools.partial(gateup_kernel, nt),
        (ff // step,),
        [whole_spec(a.shape) for a in flat(pieces)]
        + [pl.BlockSpec((nd, 2, ds, step), lambda j: (0, 0, 0, j))],
        [whole_spec((nt, rows, width)), blk, blk, blk],
        [sds((nt, rows, width), BF)] + [sds((nt, rows, ff), BF)] * 3,
        flops=4 * nt * rows * width * ff,
        nbytes=2 * (2 * nt * rows * width + 2 * width * ff + 3 * nt * rows * ff),
    )(*flat(pieces), weight)


def gate_back_kernel(nt, full_ref, w_ref, silu_ref, slope_ref, gg_ref, gu_ref):
    weight = jnp.concatenate([w_ref[j] for j in range(w_ref.shape[0])], axis=1)
    for slot in range(nt):
        gh = dot_nt(full_ref[slot], weight)
        gg_ref[slot] = (gh * slope_ref[slot].astype(F32)).astype(BF)
        gu_ref[slot] = (gh * silu_ref[slot].astype(F32)).astype(BF)


def gate_back(full, weight, silu, slope, nt):
    nd, ff, ds = weight.shape
    _, rows, width = full.shape
    step = min(512, ff)
    blk = pl.BlockSpec((nt, rows, step), lambda j: (0, 0, j))
    return call(
        functools.partial(gate_back_kernel, nt),
        (ff // step,),
        [whole_spec(full.shape), pl.BlockSpec((nd, step, ds), lambda j: (0, j, 0)), blk, blk],
        [blk, blk],
        [sds((nt, rows, ff), BF)] * 2,
        flops=2 * nt * rows * width * ff,
        nbytes=2 * (nt * rows * width + width * ff + 4 * nt * rows * ff),
    )(full, weight, silu, slope)


def context_back_kernel(nt, *refs):
    pieces, w_ref, (full_ref, out_ref) = refs[:-3], refs[-3], refs[-2:]

    @pl.when(pl.program_id(0) == 0)
    def _():
        fill_from_pieces(pieces, full_ref, nt)

    weight = w_ref[:, 0].reshape(-1, w_ref.shape[3])
    for slot in range(nt):
        out_ref[slot] = dot(full_ref[slot], weight).astype(BF)


def context_back(pieces, weight, channel, nt):
    nd, _, ds, hc = weight.shape
    rows, width = pieces[0][0].shape
    step = min(256, hc)
    return call(
        functools.partial(context_back_kernel, nt),
        (hc // step,),
        [whole_spec(a.shape) for a in flat(pieces)]
        + [pl.BlockSpec((nd, 1, ds, step), lambda j: (0, channel, 0, j))],
        [whole_spec((nt, rows, width)), pl.BlockSpec((nt, rows, step), lambda j: (0, 0, j))],
        [sds((nt, rows, width), BF), sds((nt, rows, hc), BF)],
        flops=2 * nt * rows * width * hc,
        nbytes=2 * (2 * nt * rows * width + width * hc + nt * rows * hc),
    )(*flat(pieces), weight)


def middle_kernel(nterms, x_ref, gain_ref, *refs):
    terms, (mid_ref, low_ref) = refs[:nterms], refs[nterms:]
    mid = x_ref[...].astype(F32) + sum_terms(terms)
    mid_ref[...] = mid
    scale = lax.rsqrt(jnp.mean(mid * mid, axis=-1, keepdims=True) + NORM_EPS)
    low_ref[...] = (mid * scale * gain_ref[...]).astype(BF)


def make_middle(x, gain, terms):
    rows, width = x.shape
    tile = min(128, rows)
    blk = pl.BlockSpec((tile, width), lambda i: (i, 0))
    return call(
        functools.partial(middle_kernel, len(terms)),
        (rows // tile,),
        [blk, whole_spec(gain.shape)] + [blk] * len(terms),
        [blk, blk],
        [sds((rows, width), F32), sds((rows, width), BF)],
        nbytes=rows * width * (8 + 2 * len(terms)),
    )(x, gain, *terms)


def sum_terms(terms):
    total = terms[0][...].astype(F32)
    for t in terms[1:]:
        total += t[...].astype(F32)
    return total


def layer_out_kernel(nterms, mid_ref, *refs):
    refs[-1][...] = (mid_ref[...] + sum_terms(refs[:nterms])).astype(BF)


def place(group, groups, rows, tile, width, into):
    steps = rows // tile
    spec = pl.BlockSpec((tile, width), lambda i: (i + group * steps, 0))
    return spec, sds((groups * rows, width), BF), [] if into is None else [into]


def layer_out_rows(mid, terms, group, groups, into):
    rows, width = mid.shape
    tile = min(128, rows)
    blk = pl.BlockSpec((tile, width), lambda i: (i, 0))
    spec, shape, old = place(group, groups, rows, tile, width, into)
    return call(
        functools.partial(layer_out_kernel, len(terms)),
        (rows // tile,),
        [blk] * (1 + len(terms)) + [HBM] * len(old),
        spec,
        shape,
        nbytes=rows * width * (6 + 2 * len(terms)),
        aliases={1 + len(terms): 0} if old else None,
    )(mid, *terms, *old)


def norm_back_kernel(nterms, nouts, first_ref, v_ref, gain_ref, *refs):
    terms, outs, sums = refs[:nterms], refs[len(refs) - nouts :], []
    if nouts == 3:
        outs, sums = outs[:2], outs[2:]
    u = sum_terms(terms)
    v = v_ref[...].astype(F32)
    q = lax.rsqrt(jnp.mean(v * v, axis=-1, keepdims=True) + NORM_EPS)
    ug = u * gain_ref[...]
    inner = jnp.mean(ug * v, axis=-1, keepdims=True)
    grad = first_ref[...].astype(F32) + (q * ug - v * (q * q * q * inner))
    for out in outs:
        out[...] = grad.astype(out.dtype)
    for sum_ref in sums:

        @pl.when(pl.program_id(0) == 0)
        def _():
            sum_ref[...] = jnp.zeros_like(sum_ref)

        sum_ref[...] += jnp.sum(u * v * q, axis=0, keepdims=True)


def norm_back(first, v, gain, terms):
    rows, width = v.shape
    tile = min(128, rows)
    blk = pl.BlockSpec((tile, width), lambda i: (i, 0))
    return call(
        functools.partial(norm_back_kernel, len(terms), 3),
        (rows // tile,),
        [blk, blk, whole_spec(gain.shape)] + [blk] * len(terms),
        [blk, blk, pl.BlockSpec((1, width), lambda i: (0, 0))],
        [sds((rows, width), F32), sds((rows, width), BF), sds((1, width), F32)],
        nbytes=rows * width * (12 + 2 * len(terms)),
    )(first, v, gain, *terms)


def norm_back_rows(first, v, gain, terms, group, groups, into):
    rows, width = v.shape
    tile = min(128, rows)
    blk = pl.BlockSpec((tile, width), lambda i: (i, 0))
    spec, shape, old = place(group, groups, rows, tile, width, into)
    return call(
        functools.partial(norm_back_kernel, len(terms), 1),
        (rows // tile,),
        [blk, blk, whole_spec(gain.shape)] + [blk] * len(terms) + [HBM] * len(old),
        spec,
        shape,
        nbytes=rows * width * (12 + 2 * len(terms)),
        aliases={3 + len(terms): 0} if old else None,
    )(first, v, gain, *terms, *old)


def wgrad_rows_kernel(groups, which, nmore, *refs):
    nlhs = groups * (max(which) + 1)
    lhs, rhs, out_ref = refs[:nlhs], refs[nlhs : nlhs + groups * len(which)], refs[-1]
    tile = lhs[0].shape[2]
    left = [a[...].reshape(-1, tile).T for a in lhs]
    for c, w in enumerate(which):
        total = None
        for g in range(groups):
            a = left[w * groups + g]
            term = dot(a, rhs[c * groups + g][...].reshape(a.shape[1], -1))
            total = term if total is None else total + term
        out_ref[0, c * tile : (c + 1) * tile] = total.astype(BF)
    if nmore:
        out_ref[0, len(which) * tile :] = refs[-2][0]


def wgrad_rows(lhs, rhs, which, nd, more=None):
    groups = len(lhs[0])
    nt, rows, width = lhs[0][0].shape
    ds = width // nd
    n = rhs[0][0].shape[2]
    more = [] if more is None else [more]
    height = len(rhs) * ds + sum(a.shape[1] for a in more)
    return call(
        functools.partial(wgrad_rows_kernel, groups, which, len(more)),
        (nd,),
        [pl.BlockSpec((nt, rows, ds), lambda j: (0, 0, j))] * (groups * len(lhs))
        + [whole_spec(a.shape) for r in rhs for a in r]
        + [pl.BlockSpec((1,) + a.shape[1:], lambda j: (j, 0, 0)) for a in more],
        pl.BlockSpec((1, height, n), lambda j: (j, 0, 0)),
        sds((nd, height, n), BF),
        flops=2 * groups * nt * rows * width * n * len(rhs),
        nbytes=2 * groups * nt * rows * (width + n * len(rhs)) + 2 * width * n * len(rhs),
    )(*[a for l in lhs for a in l], *[a for r in rhs for a in r], *more)


def wgrad_cols_kernel(groups, nd, *refs):
    lhs, rhs, out_ref = refs[:groups], refs[groups:-1], refs[-1]
    tile = lhs[0].shape[2]
    ds = out_ref.shape[2]
    left = [a[...].reshape(-1, tile).T for a in lhs]
    total = None
    for g in range(groups):
        term = dot(left[g], rhs[g][...].reshape(left[g].shape[1], -1))
        total = term if total is None else total + term
    for j in range(nd):
        out_ref[j] = total[:, j * ds : (j + 1) * ds].astype(BF)


def wgrad_cols(lhs, rhs, nd):
    groups = len(lhs)
    nt, rows, m = lhs[0].shape
    width = rhs[0].shape[2]
    tile = min(256, m)
    return call(
        functools.partial(wgrad_cols_kernel, groups, nd),
        (m // tile,),
        [pl.BlockSpec((nt, rows, tile), lambda i: (0, 0, i))] * groups
        + [whole_spec(a.shape) for a in rhs],
        pl.BlockSpec((nd, tile, width // nd), lambda i: (0, i, 0)),
        sds((nd, m, width // nd), BF),
        flops=2 * groups * nt * rows * width * m,
        nbytes=2 * groups * nt * rows * (width + m) + 2 * width * m,
    )(*lhs, *rhs)


def doc_starts(segments):
    row_len = segments.shape[-1]
    ids = jnp.arange(row_len, dtype=jnp.int32)
    change = jnp.concatenate(
        [jnp.ones_like(segments[:, :1], dtype=bool), segments[:, 1:] != segments[:, :-1]], axis=1
    )
    return lax.cummax(jnp.where(change, ids[None, :], 0), axis=1)


def tensor_sum(value, nt):
    if nt != 4:
        return lax.psum(value, "tensor")
    value = value + lax.ppermute(value, "tensor", swap_perm(4, 1))
    return value + lax.ppermute(value, "tensor", swap_perm(4, 2))


def slot_order(blocks, index, nt):
    if nt != 4:
        return blocks
    pairs = jnp.stack([blocks[:, 1], blocks[:, 0], blocks[:, 3], blocks[:, 2]], axis=1)
    blocks = jnp.where(index % 2 == 1, pairs, blocks)
    halves = jnp.stack([blocks[:, 2], blocks[:, 3], blocks[:, 0], blocks[:, 1]], axis=1)
    return jnp.where(index // 2 == 1, halves, blocks)


def per_device(nd, nt, groups, layer_input, segments, qkv_w, out_w, gain1, gateup_w, down_w, gain2, grad_out):
    seqs, local, width = layer_input.shape
    per = seqs // groups
    index = lax.axis_index("tensor").astype(jnp.int32)
    blocks = jnp.arange(nt, dtype=jnp.int32)
    slot_of = blocks ^ index if nt == 4 else blocks

    x = [layer_input[g * per : (g + 1) * per].reshape(per * local, width) for g in range(groups)]
    go = [grad_out[g * per : (g + 1) * per].reshape(per * local, width) for g in range(groups)]
    Order.last = None
    x_all = Gather(layer_input.reshape(seqs * local, width), nt)

    gains = lax.all_gather(jnp.stack([gain1, gain2]), "dp", axis=1, tiled=True).astype(F32)
    g1, g2 = gains[:1], gains[1:]
    qkvo_w = jnp.concatenate([qkv_w, out_w.T[None]])
    full_qkvo = lax.all_gather(qkvo_w, "dp", axis=0, tiled=False)
    full_gateup = lax.all_gather(gateup_w, "dp", axis=0, tiled=False)
    full_down = lax.all_gather(down_w, "dp", axis=0, tiled=False)

    start_abs = doc_starts(segments)
    pos_abs = jnp.arange(segments.shape[1], dtype=jnp.int32)[None, :] - start_abs
    start_slot = slot_order(start_abs.reshape(seqs, nt, local), index, nt)
    pos_slot = slot_order(pos_abs.reshape(seqs, nt, local), index, nt)
    inv_freq = ROPE_BASE ** (-jnp.arange(HALF, dtype=F32) * 2.0 / HEAD_DIM)
    angles = pos_slot.astype(F32)[..., None] * inv_freq
    cos, sin = jnp.cos(angles), jnp.sin(angles)
    cos = jnp.concatenate([cos] * 4, axis=-1)
    sin = jnp.concatenate([-sin, sin] * 2, axis=-1)

    def table(t, g):
        t = t[g * per : (g + 1) * per]
        return jnp.swapaxes(t, 0, 1).reshape(nt, per * local, PAIR)

    coss = [table(cos, g) for g in range(groups)]
    sins = [table(sin, g) for g in range(groups)]
    starts = [start_slot[g * per : (g + 1) * per] for g in range(groups)]

    both = range(groups)
    qkv, ctx, lse, mid, low2, g_mid, g_low = ({} for _ in range(7))
    attn_sum, a2_all, ga2, out_sum, ga1 = ({} for _ in range(5))
    sum1, sum2, gm_all, gmf, g_qkv, g_ctx = ({} for _ in range(6))

    def dp_sum(grad):
        return lax.psum_scatter(grad, "dp", scatter_dimension=0, tiled=False)

    def project(g):
        qkv[g] = project_qkv(a1[g], full_qkvo, coss[g], sins[g], nt)

    def attend(g):
        ctx[g], lse[g] = attention_forward(qkv[g], starts[g], slot_of, nt)
        attn_sum[g] = Scatter(mm_back([ctx[g]], full_qkvo, [3], nt, 4)[0], nt)

    def middle(g):
        mid[g], low2[g] = make_middle(x[g], g2, attn_sum[g].terms)
        a2_all[g] = Gather(low2[g], nt)

    def second_back(g):
        ga2[g] = Scatter(mm_back([gg[g], gu[g]], full_gateup, [0, 1], nt, 2)[0], nt)

    def project_out(g):
        out_sum[g] = Scatter(mm_cols(hid[g], full_down, nt, 2), nt)

    def residual_back(g):
        g_mid[g], g_low[g], sum2[g] = norm_back(go[g], mid[g], g2, ga2[g].terms)
        gm_all[g] = Gather(g_low[g], nt)

    def attention_back_start(g):
        gmf[g], g_ctx[g] = context_back(gm_all[g].pieces, full_qkvo, 3, nt)

    def attention_back(g):
        g_qkv[g] = attention_backward(
            qkv[g], g_ctx[g], starts[g], lse[g], coss[g], sins[g], slot_of, nt
        )

    def input_back(g):
        parts, (sum1[g],) = mm_back(g_qkv[g], full_qkvo, [0, 1, 2], nt, 4, a1[g])
        ga1[g] = Scatter(parts, nt)

    def up_projection(g):
        a2[g], silu[g], slope[g], hid[g] = gate_up(a2_all[g].pieces, full_gateup, nt)

    def hidden_back(g):
        gg[g], gu[g] = gate_back(gof[g], full_down, silu[g], slope[g], nt)

    def finish(g, grad_input):
        return norm_back_rows(g_mid[g], x[g], g1, ga1[g].terms, g, groups, grad_input)

    def by_group(held):
        return [held[g] for g in both]

    def gather_cotangent(g):
        go_all[g] = Gather(link(go[g], flat(x_all.pieces)[-1]), nt)

    a2, silu, slope, hid, gg, gu, go_all, gof = ({} for _ in range(8))
    x_all.second()
    gather_cotangent(0)
    gather_cotangent(1)
    a1 = [assemble(x_all.pieces, nt, 0, groups, g1, coss + sins)]
    project(0)
    attend(0)
    go_all[0].second()
    a1.append(assemble(x_all.pieces, nt, 1, groups, g1))
    project(1)
    attn_sum[0].second()
    attend(1)
    middle(0)
    gof[0] = assemble(go_all[0].pieces, nt, 0, 1)
    attn_sum[1].second()
    a2_all[0].second()
    middle(1)
    go_all[1].second()
    up_projection(0)
    a2_all[1].second()
    gof[1] = assemble(go_all[1].pieces, nt, 0, 1)
    up_projection(1)
    hidden_back(0)
    grad_down = dp_sum(wgrad_cols(by_group(hid), by_group(gof), nd))
    second_back(0)
    hidden_back(1)
    ga2[0].second()
    grad_gateup = wgrad_rows([by_group(a2)], [by_group(gg), by_group(gu)], [0, 0], nd)
    residual_back(0)
    grad_gateup = dp_sum(link(grad_gateup, grad_down))
    second_back(1)
    gm_all[0].second()
    project_out(0)
    attention_back_start(0)
    ga2[1].second()
    attention_back(0)
    residual_back(1)
    input_back(0)
    project_out(1)
    gm_all[1].second()
    out_sum[0].second()
    attention_back_start(1)
    attention_back(1)
    input_back(1)
    ds = gain1.shape[0]
    gains = tensor_sum(jnp.concatenate([(sum1[0] + sum1[1]) / g1, sum2[0] + sum2[1]]), nt)
    gains = jnp.swapaxes(gains.reshape(2, nd, ds), 0, 1).astype(BF)
    gains = jnp.pad(gains, ((0, 0), (0, 14), (0, qkv_w.shape[2] - ds)))
    out_sum[1].second()
    layer_out = layer_out_rows(mid[0], out_sum[0].terms, 0, groups, None)
    grad_qkvo = wgrad_rows(
        [a1, by_group(gmf)],
        [[g_qkv[g][c] for g in both] for c in range(3)] + [by_group(ctx)],
        [0, 0, 0, 1],
        nd,
        gains,
    )
    ga1[1].second()
    grad_qkvo = dp_sum(link(grad_qkvo, grad_gateup))
    layer_out = layer_out_rows(mid[1], out_sum[1].terms, 1, groups, layer_out)
    ga1[0].second()
    grad_input = finish(1, None)
    grad_input = finish(0, grad_input)
    return (
        layer_out.reshape(seqs, local, width),
        grad_input.reshape(seqs, local, width),
        grad_qkvo[: 3 * ds].astype(F32).reshape(3, ds, -1),
        grad_qkvo[3 * ds : 4 * ds].T.astype(F32),
        grad_qkvo[4 * ds, :ds].astype(F32),
        grad_gateup.astype(F32).reshape(2, ds, -1),
        grad_down.astype(F32),
        grad_qkvo[4 * ds + 1, :ds].astype(F32),
    )


def solution(mesh):
    nd, nt = mesh.shape["dp"], mesh.shape["tensor"]
    return jax.shard_map(
        functools.partial(per_device, nd, nt, 2),
        mesh=mesh,
        in_specs=(
            P("dp", "tensor", None),
            P("dp", None),
            P(None, "dp", "tensor"),
            P("tensor", "dp"),
            P("dp"),
            P(None, "dp", "tensor"),
            P("tensor", "dp"),
            P("dp"),
            P("dp", "tensor", None),
        ),
        out_specs=(
            P("dp", "tensor", None),
            P("dp", "tensor", None),
            P(None, "dp", "tensor"),
            P("tensor", "dp"),
            P("dp"),
            P(None, "dp", "tensor"),
            P("tensor", "dp"),
            P("dp"),
        ),
        check_vma=False,
    )
```

```python
import functools

import jax
import jax.numpy as jnp
import numpy as np
from jax import lax
from jax.experimental import pallas as pl
from jax.experimental.pallas import tpu as pltpu
from jax.sharding import PartitionSpec as P

HEAD_DIM = 64
HALF = HEAD_DIM // 2
PAIR = 2 * HEAD_DIM
NORM_EPS = 1e-05
ROPE_BASE = 130000.0
MASKED_SCORE = -1e30
BF = jnp.bfloat16
F32 = jnp.float32
VMEM_SLACK = 8 * 1024 * 1024
VMEM_SMALL = 24 * 1024 * 1024
VMEM_LARGE = 40 * 1024 * 1024
PIN_BYTES = 2 * 1024 * 1024
PIN_BYTES_LARGE = 1024 * 1024
SMALL = 3

NT = (((1,), (1,)), ((), ()))


def dot(a, b):
    return jnp.dot(a, b, preferred_element_type=F32)


def dot_nt(a, b):
    return lax.dot_general(a, b, NT, preferred_element_type=F32)


class Order:
    last = None


HBM = pl.BlockSpec(memory_space=pltpu.HBM)
ANY = pl.BlockSpec(memory_space=pl.ANY)


def is_large(array, least=None):
    return array.size * array.dtype.itemsize >= (least or PIN_BYTES)


def pin(array, least=None):
    return pltpu.with_memory_space_constraint(array, pltpu.HBM) if is_large(array, least) else array


def pinned(shape):
    return pltpu.HBM(shape.shape, shape.dtype) if is_large(shape) else shape


def block_bytes(spec, dtype):
    if spec.block_shape is None:
        return 0
    count = 2 if spec.pipeline_mode is None else spec.pipeline_mode.buffer_count
    return count * int(np.prod([d for d in spec.block_shape if d])) * np.dtype(dtype).itemsize


def call(body, grid, in_specs, out_specs, out_shape, scratch=(), flops=0, nbytes=0, aliases=None, prefetch=0):
    first_extra = prefetch + len(in_specs)
    many = isinstance(out_shape, (list, tuple))
    out_blocks = list(zip(out_specs, out_shape)) if many else [(out_specs, out_shape)]

    def run(*args):
        extra = [] if Order.last is None or any(a is Order.last for a in args) else [pin(Order.last)]

        blocks = list(zip(in_specs, args[prefetch:])) + out_blocks
        vmem = VMEM_SLACK + sum(block_bytes(spec, a.dtype) for spec, a in blocks)
        vmem += sum(int(np.prod(m.shape)) * np.dtype(m.dtype).itemsize for m in scratch)
        least = PIN_BYTES
        if vmem > VMEM_SMALL:
            vmem, least = VMEM_LARGE, PIN_BYTES_LARGE

        args = [pin(a, least) for a in args]

        def ordered_body(*refs):
            body(*refs[:first_extra], *refs[first_extra + len(extra) :])

        outs = pl.pallas_call(
            ordered_body,
            grid_spec=pltpu.PrefetchScalarGridSpec(
                num_scalar_prefetch=prefetch,
                grid=grid,
                in_specs=in_specs + [ANY] * len(extra),
                out_specs=out_specs,
                scratch_shapes=list(scratch),
            ),
            out_shape=[pinned(a) for a in out_shape] if many else pinned(out_shape),
            input_output_aliases=aliases or {},
            cost_estimate=pl.CostEstimate(flops=flops // SMALL, bytes_accessed=nbytes // SMALL, transcendentals=0),
            compiler_params=pltpu.CompilerParams(vmem_limit_bytes=vmem),
        )(*args, *extra)
        Order.last = outs[-1] if isinstance(outs, (list, tuple)) else outs
        return outs

    return run


def link_kernel(value_ref, done_ref, out_ref):
    pass


def link(value, done):
    return call(link_kernel, (1,), [HBM, HBM], HBM, sds(value.shape, value.dtype), aliases={0: 0})(value, done)


def whole_spec(shape, buffers=1):
    zeros = (0,) * len(shape)
    return pl.BlockSpec(shape, lambda *_: zeros, pipeline_mode=pl.Buffered(buffers))


def sds(shape, dtype):
    return jax.ShapeDtypeStruct(shape, dtype)


def swap_perm(count, bit):
    return [(i, i ^ bit) for i in range(count)]


def halves_kernel(y_ref, x_ref, left_ref, right_ref):
    left_ref[...] = y_ref[...]
    right_ref[...] = x_ref[...]


def halves(from_y, from_x):
    rows, width = from_y.shape
    half = width // 2
    tile = min(128, rows)

    def spec(which):
        return pl.BlockSpec((tile, half), lambda i: (i, which))

    return call(
        halves_kernel,
        (rows // tile,),
        [spec(0), spec(1)],
        [spec(0), spec(0)],
        [sds((rows, half), BF)] * 2,
        nbytes=rows * half * 8,
    )(from_y, from_x)


class Gather:
    def __init__(self, block, nt, direct=False):
        self.nt = nt
        if nt != 4:
            full = lax.all_gather(block, "tensor", axis=0, tiled=False)
            self.pieces = [(full[r],) for r in range(nt)]
            return
        self.block = block
        self.from_x = lax.ppermute(block, "tensor", swap_perm(4, 1))
        self.from_y = lax.ppermute(block, "tensor", swap_perm(4, 2))
        if direct:
            diag = lax.ppermute(block, "tensor", swap_perm(4, 3))
            self.pieces = [(block,), (self.from_x,), (self.from_y,), (diag,)]

    def second(self):
        if self.nt != 4:
            return
        left, right = halves(self.from_y, self.from_x)
        diag_x = lax.ppermute(left, "tensor", swap_perm(4, 1))
        diag_y = lax.ppermute(right, "tensor", swap_perm(4, 2))
        self.pieces = [(self.block,), (self.from_x,), (self.from_y,), (diag_x, diag_y)]


def add_halves_kernel(x_ref, for_x_ref, y_ref, for_y_ref, out_x_ref, out_y_ref):
    out_x_ref[...] = (x_ref[...].astype(F32) + for_x_ref[...].astype(F32)).astype(BF)
    out_y_ref[...] = (y_ref[...].astype(F32) + for_y_ref[...].astype(F32)).astype(BF)


def add_halves(to_x, for_x, to_y, for_y):
    rows, width = to_x.shape
    half = width // 2
    tile = min(128, rows)

    def spec(which):
        return pl.BlockSpec((tile, half), lambda i: (i, which))

    return call(
        add_halves_kernel,
        (rows // tile,),
        [spec(1), spec(0), spec(0), spec(0)],
        [spec(1), spec(0)],
        [sds(to_x.shape, BF)] * 2,
        nbytes=rows * half * 12,
        aliases={0: 0, 2: 1},
    )(to_x, for_x, to_y, for_y)


class Scatter:
    def __init__(self, parts, nt):
        self.nt = nt
        if nt != 4:
            full = jnp.stack([p[0] for p in parts])
            self.terms = [lax.psum_scatter(full, "tensor", scatter_dimension=0, tiled=False)]
            return
        (self.own,), (self.to_x,), (self.to_y,), (diag_x, diag_y) = parts
        self.for_y = lax.ppermute(diag_x, "tensor", swap_perm(4, 1))
        self.for_x = lax.ppermute(diag_y, "tensor", swap_perm(4, 2))

    def second(self):
        if self.nt != 4:
            return
        to_x, to_y = add_halves(self.to_x, self.for_x, self.to_y, self.for_y)
        self.terms = [
            self.own,
            lax.ppermute(to_x, "tensor", swap_perm(4, 1)),
            lax.ppermute(to_y, "tensor", swap_perm(4, 2)),
        ]


def piece_shapes(nt, rows, width):
    if nt != 4:
        return [((rows, width),)] * nt
    return [((rows, width),)] * 3 + [((rows, width // 2),) * 2]


def flat(pieces):
    return [a for p in pieces for a in p]


def regroup(items, nt):
    if len(items) == nt:
        return [(a,) for a in items]
    return [(items[0],), (items[1],), (items[2],), (items[3], items[4])]


def fill_from_pieces(refs, full_ref, nt):
    for slot, part in enumerate(regroup(refs, nt)):
        if len(part) == 1:
            full_ref[slot] = part[0][...]
        else:
            half = part[0].shape[1]
            full_ref[slot, :, :half] = part[0][...]
            full_ref[slot, :, half:] = part[1][...]


def out_piece_specs(nt, rows, width, step):
    specs = []
    half_steps = width // step // 2
    for part in piece_shapes(nt, rows, width):
        if len(part) == 1:
            specs.append(pl.BlockSpec((rows, step), lambda j: (0, j)))
        else:
            specs.append(pl.BlockSpec((rows, step), lambda j: (0, jnp.minimum(j, half_steps - 1))))
            specs.append(pl.BlockSpec((rows, step), lambda j: (0, jnp.maximum(j - half_steps, 0))))
    return specs


def store_piece(outs, nt, slot, steps, value):
    part = regroup(outs, nt)[slot]
    if len(part) == 1:
        part[0][...] = value.astype(BF)
    else:
        j = pl.program_id(0)

        @pl.when(j < steps // 2)
        def _():
            part[0][...] = value.astype(BF)

        @pl.when(j >= steps // 2)
        def _():
            part[1][...] = value.astype(BF)


def turn(v):
    lane = lax.broadcasted_iota(jnp.int32, v.shape, 1)
    return jnp.where(lane % HEAD_DIM < HALF, pltpu.roll(v, PAIR - HALF, 1), pltpu.roll(v, HALF, 1))


def rotate(v, cos, sin):
    return v * cos + turn(v) * sin


def unrotate(u, cos, sin):
    return u * cos + turn(u * sin)


def assemble_kernel(nt, count, normed, *refs):
    full_ref = refs[-1]
    fill_from_pieces(refs[:count], full_ref, nt)
    if normed:
        gain = refs[count][...]
        for slot in range(nt):
            x = full_ref[slot].astype(F32)
            scale = lax.rsqrt(jnp.mean(x * x, axis=-1, keepdims=True) + NORM_EPS)
            full_ref[slot] = (x * scale * gain).astype(BF)


def assemble(pieces, nt, group, groups, gain=None, ready=()):
    rows, width = pieces[0][0].shape
    rows //= groups
    tile = min(64, rows)
    first = group * (rows // tile)
    items = flat(pieces)
    extra = [] if gain is None else [gain]
    return call(
        functools.partial(assemble_kernel, nt, len(items), len(extra)),
        (rows // tile,),
        [pl.BlockSpec((tile, a.shape[1]), lambda i: (i + first, 0)) for a in items]
        + [whole_spec(a.shape) for a in extra]
        + [ANY] * len(ready),
        pl.BlockSpec((nt, tile, width), lambda i: (0, i, 0)),
        sds((nt, rows, width), BF),
        nbytes=4 * nt * rows * width,
    )(*items, *extra, *ready)


def qkv_kernel(nt, a1_ref, w_ref, cos_ref, sin_ref, out_ref):
    cols = out_ref.shape[3]
    weight = w_ref[:, 0].reshape(-1, cols)

    @pl.when(pl.program_id(0) < 2)
    def _():
        for slot in range(nt):
            raw = dot(a1_ref[slot], weight)
            cos, sin = cos_ref[slot], sin_ref[slot]
            for p in range(cols // PAIR):
                part = slice(p * PAIR, (p + 1) * PAIR)
                out_ref[0, slot, :, part] = rotate(raw[:, part], cos, sin).astype(BF)

    @pl.when(pl.program_id(0) == 2)
    def _():
        for slot in range(nt):
            out_ref[0, slot] = dot(a1_ref[slot], weight).astype(BF)


def project_qkv(a1, weight, cos, sin, nt):
    nd, _, ds, hc = weight.shape
    _, rows, width = a1.shape
    return call(
        functools.partial(qkv_kernel, nt),
        (3,),
        [
            whole_spec(a1.shape),
            pl.BlockSpec((nd, 1, ds, hc), lambda c: (0, c, 0, 0)),
            whole_spec(cos.shape),
            whole_spec(sin.shape),
        ],
        pl.BlockSpec((1, nt, rows, hc), lambda c: (c, 0, 0, 0)),
        sds((3, nt, rows, hc), BF),
        flops=2 * nt * rows * width * hc * 3,
        nbytes=2 * (nt * rows * width + 3 * width * hc + 3 * nt * rows * hc),
    )(a1, weight, cos, sin)


def allowed_block(start, key_block, query_block, size):
    key_id = lax.broadcasted_iota(jnp.int32, (size, size), 0) + key_block * size
    ok = key_id >= start
    if key_block == query_block:
        ok &= lax.broadcasted_iota(jnp.int32, (size, size), 1) + query_block * size >= key_id
    return ok


def attn_fwd_kernel(nt, slot_ref, q_ref, k_ref, v_ref, start_ref, ctx_ref, lse_ref, vt_ref):
    size = q_ref.shape[1]
    for b in range(nt):
        vt_ref[b] = v_ref[slot_ref[b]].T
    lane = lax.broadcasted_iota(jnp.int32, (size, PAIR), 1)
    for p in range(nt):
        slot = slot_ref[p]
        q = q_ref[slot] * BF(HEAD_DIM**-0.5)
        start = start_ref[0, pl.ds(slot, 1), :]
        outs = []
        for h in range(2):
            qh = jnp.where((lane >= HEAD_DIM) == (h == 1), q, BF(0))
            scores = []
            for b in range(p + 1):
                s = dot_nt(k_ref[slot_ref[b]], qh)
                scores.append(jnp.where(allowed_block(start, b, p, size), s, MASKED_SCORE))
            top = functools.reduce(
                jnp.maximum, [jnp.max(s, axis=0, keepdims=True) for s in scores]
            )
            total = jnp.zeros((1, size), F32)
            acc = jnp.zeros((HEAD_DIM, size), F32)
            for b, s in enumerate(scores):
                e = jnp.exp(s - top)
                total += jnp.sum(e, axis=0, keepdims=True)
                acc += dot(vt_ref[b, h * HEAD_DIM : (h + 1) * HEAD_DIM, :], e.astype(BF))
            outs.append(acc / total)
            lse_ref[0, 0, pl.ds(2 * p + h, 1), :] = top + jnp.log(total)
        ctx_ref[slot] = jnp.concatenate(outs, axis=0).T.astype(BF)


def qkv_specs(nt, size):
    def spec(c):
        return pl.BlockSpec((None, nt, size, PAIR), lambda s, g, _: (c, 0, s, g))

    return [spec(c) for c in range(3)]


def attention_forward(qkv, start, slot_of, nt):
    _, _, rows, hc = qkv.shape
    seqs = start.shape[0]
    size = rows // seqs
    pairs = hc // PAIR
    blk = pl.BlockSpec((nt, size, PAIR), lambda s, g, _: (0, s, g))
    return call(
        functools.partial(attn_fwd_kernel, nt),
        (seqs, pairs),
        qkv_specs(nt, size) + [pl.BlockSpec((1, nt, size), lambda s, g, _: (s, 0, 0))],
        [blk, pl.BlockSpec((1, 1, 2 * nt, size), lambda s, g, _: (s, g, 0, 0))],
        [sds((nt, rows, hc), BF), sds((seqs, pairs, 2 * nt, size), F32)],
        scratch=[pltpu.VMEM((nt, PAIR, size), BF)],
        flops=seqs * pairs * 2 * 4 * (nt * size) ** 2 * 128,
        nbytes=8 * nt * rows * hc,
        prefetch=1,
    )(slot_of, qkv, qkv, qkv, start)


def attn_bwd_kernel(
    nt, slot_ref, q_ref, k_ref, v_ref, go_ref, start_ref, lse_ref, cos_ref, sin_ref,
    gq_ref, gk_ref, gv_ref, kt_ref, dk_ref, dv_ref,
):
    size = q_ref.shape[1]
    scale = HEAD_DIM**-0.5
    for b in range(nt):
        kt_ref[b] = k_ref[slot_ref[b]].T
    dk_ref[...] = jnp.zeros_like(dk_ref)
    dv_ref[...] = jnp.zeros_like(dv_ref)
    lane = lax.broadcasted_iota(jnp.int32, (size, PAIR), 1)
    for p in range(nt):
        slot = slot_ref[p]
        q = q_ref[slot] * BF(scale)
        go = go_ref[slot]
        start = start_ref[0, pl.ds(slot, 1), :]
        outs = []
        for h in range(2):
            mine = (lane >= HEAD_DIM) == (h == 1)
            qh = jnp.where(mine, q, BF(0))
            goh = jnp.where(mine, go, BF(0))
            lse = lse_ref[0, 0, pl.ds(2 * p + h, 1), :]
            probs, grads = [], []
            inner = jnp.zeros((1, size), F32)
            for b in range(p + 1):
                key_slot = slot_ref[b]
                s = dot_nt(k_ref[key_slot], qh)
                s = jnp.where(allowed_block(start, b, p, size), s, MASKED_SCORE)
                e = jnp.exp(s - lse)
                g = dot_nt(v_ref[key_slot], goh)
                inner += jnp.sum(e * g, axis=0, keepdims=True)
                probs.append(e)
                grads.append(g)
            dqt = jnp.zeros((HEAD_DIM, size), F32)
            for b in range(p + 1):
                ds = (probs[b] * (grads[b] - inner)).astype(BF)
                dv_ref[b] += dot(probs[b].astype(BF), goh)
                dk_ref[b] += dot(ds, qh)
                dqt += dot(kt_ref[b, h * HEAD_DIM : (h + 1) * HEAD_DIM, :], ds)
            outs.append(dqt)
        dq = jnp.concatenate(outs, axis=0).T * scale
        gq_ref[slot] = unrotate(dq, cos_ref[slot], sin_ref[slot]).astype(BF)
    for b in range(nt):
        slot = slot_ref[b]
        gk_ref[slot] = unrotate(dk_ref[b], cos_ref[slot], sin_ref[slot]).astype(BF)
        gv_ref[slot] = dv_ref[b].astype(BF)


def attention_backward(qkv, go, start, lse, cos, sin, slot_of, nt):
    _, _, rows, hc = qkv.shape
    seqs = start.shape[0]
    size = rows // seqs
    pairs = hc // PAIR
    blk = pl.BlockSpec((nt, size, PAIR), lambda s, g, _: (0, s, g))
    table = pl.BlockSpec((nt, size, PAIR), lambda s, g, _: (0, s, 0))
    return call(
        functools.partial(attn_bwd_kernel, nt),
        (seqs, pairs),
        qkv_specs(nt, size)
        + [
            blk,
            pl.BlockSpec((1, nt, size), lambda s, g, _: (s, 0, 0)),
            pl.BlockSpec((1, 1, 2 * nt, size), lambda s, g, _: (s, g, 0, 0)),
            table, table,
        ],
        [blk, blk, blk],
        [sds((nt, rows, hc), BF)] * 3,
        scratch=[
            pltpu.VMEM((nt, PAIR, size), BF),
            pltpu.VMEM((nt, size, PAIR), F32),
            pltpu.VMEM((nt, size, PAIR), F32),
        ],
        flops=seqs * pairs * 2 * 10 * (nt * size) ** 2 * 128,
        nbytes=14 * nt * rows * hc,
        prefetch=1,
    )(slot_of, qkv, qkv, qkv, go, start, lse, cos, sin)


def shard_group(nd, count):
    while nd % count or nd // count % 2:
        count //= 2
    return max(count, 1)


def cols_out_kernel(nt, steps, lhs_ref, w_ref, *outs):
    for slot in range(nt):
        lhs = lhs_ref[slot]
        parts = [dot(lhs, w_ref[j]) for j in range(w_ref.shape[0])]
        store_piece(outs, nt, slot, steps, jnp.concatenate(parts, axis=1))


def mm_cols(lhs, weight, nt, group):
    nd, depth, ds = weight.shape
    group = shard_group(nd, group)
    rows = lhs.shape[1]
    width = nd * ds
    shapes = flat(piece_shapes(nt, rows, width))
    outs = call(
        functools.partial(cols_out_kernel, nt, nd // group),
        (nd // group,),
        [whole_spec(lhs.shape), pl.BlockSpec((group, depth, ds), lambda j: (j, 0, 0))],
        out_piece_specs(nt, rows, width, group * ds),
        [sds(s, BF) for s in shapes],
        flops=2 * nt * rows * depth * width,
        nbytes=2 * (nt * rows * (depth + width) + depth * width),
    )(lhs, weight)
    return regroup(outs, nt)


def cols_back_kernel(nt, steps, nlhs, nseen, *refs):
    lhs, w_refs, outs = refs[:nlhs], refs[nlhs : 2 * nlhs], refs[2 * nlhs + nseen :]
    depth = w_refs[0].shape[3]
    weights = [w[:, 0].reshape(-1, depth) for w in w_refs]
    sums = None
    for slot in range(nt):
        total = dot_nt(lhs[0][slot], weights[0])
        for c in range(1, nlhs):
            total += dot_nt(lhs[c][slot], weights[c])
        if nseen:
            part = jnp.sum(total * refs[2 * nlhs][slot].astype(F32), axis=0, keepdims=True)
            sums = part if sums is None else sums + part
        store_piece(outs[: len(outs) - nseen], nt, slot, steps, total)
    if nseen:
        outs[-1][...] = sums


def mm_back(lhs, weight, channels, nt, group, seen=None):
    nd, _, ds, depth = weight.shape
    count = len(lhs)
    group = shard_group(nd, group)
    rows = lhs[0].shape[1]
    width = nd * ds
    shapes = flat(piece_shapes(nt, rows, width))
    step = group * ds
    more = [] if seen is None else [seen]

    def spec(c):
        return pl.BlockSpec((group, 1, ds, depth), lambda j: (j, c, 0, 0))

    outs = call(
        functools.partial(cols_back_kernel, nt, nd // group, count, len(more)),
        (nd // group,),
        [whole_spec(a.shape) for a in lhs]
        + [spec(c) for c in channels]
        + [pl.BlockSpec((nt, rows, step), lambda j: (0, 0, j)) for _ in more],
        out_piece_specs(nt, rows, width, step) + [pl.BlockSpec((1, step), lambda j: (0, j)) for _ in more],
        [sds(s, BF) for s in shapes] + [sds((1, width), F32) for _ in more],
        flops=2 * nt * rows * depth * width * count,
        nbytes=2 * (nt * rows * (depth * count + width) + depth * width * count),
    )(*lhs, *[weight] * count, *more)
    return regroup(outs[: len(shapes)], nt), outs[len(shapes) :]


def gateup_kernel(nt, *refs):
    count = len(flat(piece_shapes(nt, 8, 8)))
    pieces, w_ref, (full_ref, silu_ref, slope_ref, hid_ref) = (
        refs[:count],
        refs[count],
        refs[count + 1 :],
    )

    @pl.when(pl.program_id(0) == 0)
    def _():
        fill_from_pieces(pieces, full_ref, nt)

    cols = hid_ref.shape[2]
    w_gate = w_ref[:, 0].reshape(-1, cols)
    w_up = w_ref[:, 1].reshape(-1, cols)
    for slot in range(nt):
        a2 = full_ref[slot]
        gate = dot(a2, w_gate)
        up = dot(a2, w_up)
        sig = 0.5 + 0.5 * jnp.tanh(0.5 * gate)
        silu = gate * sig
        silu_ref[slot] = silu.astype(BF)
        slope_ref[slot] = (up * (sig + silu - silu * sig)).astype(BF)
        hid_ref[slot] = (silu * up).astype(BF)


def gate_up(pieces, weight, nt):
    nd, _, ds, ff = weight.shape
    rows, width = pieces[0][0].shape
    step = min(512, ff)
    blk = pl.BlockSpec((nt, rows, step), lambda j: (0, 0, j))
    return call(
        functools.partial(gateup_kernel, nt),
        (ff // step,),
        [whole_spec(a.shape) for a in flat(pieces)]
        + [pl.BlockSpec((nd, 2, ds, step), lambda j: (0, 0, 0, j))],
        [whole_spec((nt, rows, width)), blk, blk, blk],
        [sds((nt, rows, width), BF)] + [sds((nt, rows, ff), BF)] * 3,
        flops=4 * nt * rows * width * ff,
        nbytes=2 * (2 * nt * rows * width + 2 * width * ff + 3 * nt * rows * ff),
    )(*flat(pieces), weight)


def gate_back_kernel(nt, full_ref, w_ref, silu_ref, slope_ref, gg_ref, gu_ref):
    weight = jnp.concatenate([w_ref[j] for j in range(w_ref.shape[0])], axis=1)
    for slot in range(nt):
        gh = dot_nt(full_ref[slot], weight)
        gg_ref[slot] = (gh * slope_ref[slot].astype(F32)).astype(BF)
        gu_ref[slot] = (gh * silu_ref[slot].astype(F32)).astype(BF)


def gate_back(full, weight, silu, slope, nt):
    nd, ff, ds = weight.shape
    _, rows, width = full.shape
    step = min(512, ff)
    blk = pl.BlockSpec((nt, rows, step), lambda j: (0, 0, j))
    return call(
        functools.partial(gate_back_kernel, nt),
        (ff // step,),
        [whole_spec(full.shape), pl.BlockSpec((nd, step, ds), lambda j: (0, j, 0)), blk, blk],
        [blk, blk],
        [sds((nt, rows, ff), BF)] * 2,
        flops=2 * nt * rows * width * ff,
        nbytes=2 * (nt * rows * width + width * ff + 4 * nt * rows * ff),
    )(full, weight, silu, slope)


def context_back_kernel(nt, *refs):
    pieces, w_ref, (full_ref, out_ref) = refs[:-3], refs[-3], refs[-2:]

    @pl.when(pl.program_id(0) == 0)
    def _():
        fill_from_pieces(pieces, full_ref, nt)

    weight = w_ref[:, 0].reshape(-1, w_ref.shape[3])
    for slot in range(nt):
        out_ref[slot] = dot(full_ref[slot], weight).astype(BF)


def context_back(pieces, weight, channel, nt):
    nd, _, ds, hc = weight.shape
    rows, width = pieces[0][0].shape
    step = min(256, hc)
    return call(
        functools.partial(context_back_kernel, nt),
        (hc // step,),
        [whole_spec(a.shape) for a in flat(pieces)]
        + [pl.BlockSpec((nd, 1, ds, step), lambda j: (0, channel, 0, j))],
        [whole_spec((nt, rows, width)), pl.BlockSpec((nt, rows, step), lambda j: (0, 0, j))],
        [sds((nt, rows, width), BF), sds((nt, rows, hc), BF)],
        flops=2 * nt * rows * width * hc,
        nbytes=2 * (2 * nt * rows * width + width * hc + nt * rows * hc),
    )(*flat(pieces), weight)


def middle_kernel(nterms, x_ref, gain_ref, *refs):
    terms, (mid_ref, low_ref) = refs[:nterms], refs[nterms:]
    mid = x_ref[...].astype(F32) + sum_terms(terms)
    mid_ref[...] = mid
    scale = lax.rsqrt(jnp.mean(mid * mid, axis=-1, keepdims=True) + NORM_EPS)
    low_ref[...] = (mid * scale * gain_ref[...]).astype(BF)


def make_middle(x, gain, terms):
    rows, width = x.shape
    tile = min(128, rows)
    blk = pl.BlockSpec((tile, width), lambda i: (i, 0))
    return call(
        functools.partial(middle_kernel, len(terms)),
        (rows // tile,),
        [blk, whole_spec(gain.shape)] + [blk] * len(terms),
        [blk, blk],
        [sds((rows, width), F32), sds((rows, width), BF)],
        nbytes=rows * width * (8 + 2 * len(terms)),
    )(x, gain, *terms)


def sum_terms(terms):
    total = terms[0][...].astype(F32)
    for t in terms[1:]:
        total += t[...].astype(F32)
    return total


def layer_out_kernel(nterms, mid_ref, *refs):
    refs[-1][...] = (mid_ref[...] + sum_terms(refs[:nterms])).astype(BF)


def place(group, groups, rows, tile, width, into):
    steps = rows // tile
    spec = pl.BlockSpec((tile, width), lambda i: (i + group * steps, 0))
    return spec, sds((groups * rows, width), BF), [] if into is None else [into]


def layer_out_rows(mid, terms, group, groups, into):
    rows, width = mid.shape
    tile = min(128, rows)
    blk = pl.BlockSpec((tile, width), lambda i: (i, 0))
    spec, shape, old = place(group, groups, rows, tile, width, into)
    return call(
        functools.partial(layer_out_kernel, len(terms)),
        (rows // tile,),
        [blk] * (1 + len(terms)) + [HBM] * len(old),
        spec,
        shape,
        nbytes=rows * width * (6 + 2 * len(terms)),
        aliases={1 + len(terms): 0} if old else None,
    )(mid, *terms, *old)


def norm_back_kernel(nterms, nouts, first_ref, v_ref, gain_ref, *refs):
    terms, outs, sums = refs[:nterms], refs[len(refs) - nouts :], []
    if nouts == 3:
        outs, sums = outs[:2], outs[2:]
    u = sum_terms(terms)
    v = v_ref[...].astype(F32)
    q = lax.rsqrt(jnp.mean(v * v, axis=-1, keepdims=True) + NORM_EPS)
    ug = u * gain_ref[...]
    inner = jnp.mean(ug * v, axis=-1, keepdims=True)
    grad = first_ref[...].astype(F32) + (q * ug - v * (q * q * q * inner))
    for out in outs:
        out[...] = grad.astype(out.dtype)
    for sum_ref in sums:

        @pl.when(pl.program_id(0) == 0)
        def _():
            sum_ref[...] = jnp.zeros_like(sum_ref)

        sum_ref[...] += jnp.sum(u * v * q, axis=0, keepdims=True)


def norm_back(first, v, gain, terms):
    rows, width = v.shape
    tile = min(128, rows)
    blk = pl.BlockSpec((tile, width), lambda i: (i, 0))
    return call(
        functools.partial(norm_back_kernel, len(terms), 3),
        (rows // tile,),
        [blk, blk, whole_spec(gain.shape)] + [blk] * len(terms),
        [blk, blk, pl.BlockSpec((1, width), lambda i: (0, 0))],
        [sds((rows, width), F32), sds((rows, width), BF), sds((1, width), F32)],
        nbytes=rows * width * (12 + 2 * len(terms)),
    )(first, v, gain, *terms)


def norm_back_rows(first, v, gain, terms, group, groups, into):
    rows, width = v.shape
    tile = min(128, rows)
    blk = pl.BlockSpec((tile, width), lambda i: (i, 0))
    spec, shape, old = place(group, groups, rows, tile, width, into)
    return call(
        functools.partial(norm_back_kernel, len(terms), 1),
        (rows // tile,),
        [blk, blk, whole_spec(gain.shape)] + [blk] * len(terms) + [HBM] * len(old),
        spec,
        shape,
        nbytes=rows * width * (12 + 2 * len(terms)),
        aliases={3 + len(terms): 0} if old else None,
    )(first, v, gain, *terms, *old)


def wgrad_rows_kernel(groups, which, nmore, *refs):
    nlhs = groups * (max(which) + 1)
    lhs, rhs, out_ref = refs[:nlhs], refs[nlhs : nlhs + groups * len(which)], refs[-1]
    tile = lhs[0].shape[2]
    left = [a[...].reshape(-1, tile).T for a in lhs]
    for c, w in enumerate(which):
        total = None
        for g in range(groups):
            a = left[w * groups + g]
            term = dot(a, rhs[c * groups + g][...].reshape(a.shape[1], -1))
            total = term if total is None else total + term
        out_ref[0, c * tile : (c + 1) * tile] = total.astype(BF)
    if nmore:
        out_ref[0, len(which) * tile :] = refs[-2][0]


def wgrad_rows(lhs, rhs, which, nd, more=None):
    groups = len(lhs[0])
    nt, rows, width = lhs[0][0].shape
    ds = width // nd
    n = rhs[0][0].shape[2]
    more = [] if more is None else [more]
    height = len(rhs) * ds + sum(a.shape[1] for a in more)
    return call(
        functools.partial(wgrad_rows_kernel, groups, which, len(more)),
        (nd,),
        [pl.BlockSpec((nt, rows, ds), lambda j: (0, 0, j))] * (groups * len(lhs))
        + [whole_spec(a.shape) for r in rhs for a in r]
        + [pl.BlockSpec((1,) + a.shape[1:], lambda j: (j, 0, 0)) for a in more],
        pl.BlockSpec((1, height, n), lambda j: (j, 0, 0)),
        sds((nd, height, n), BF),
        flops=2 * groups * nt * rows * width * n * len(rhs),
        nbytes=2 * groups * nt * rows * (width + n * len(rhs)) + 2 * width * n * len(rhs),
    )(*[a for l in lhs for a in l], *[a for r in rhs for a in r], *more)


def wgrad_cols_kernel(groups, nd, *refs):
    lhs, rhs, out_ref = refs[:groups], refs[groups:-1], refs[-1]
    tile = lhs[0].shape[2]
    ds = out_ref.shape[2]
    left = [a[...].reshape(-1, tile).T for a in lhs]
    total = None
    for g in range(groups):
        term = dot(left[g], rhs[g][...].reshape(left[g].shape[1], -1))
        total = term if total is None else total + term
    for j in range(nd):
        out_ref[j] = total[:, j * ds : (j + 1) * ds].astype(BF)


def wgrad_cols(lhs, rhs, nd):
    groups = len(lhs)
    nt, rows, m = lhs[0].shape
    width = rhs[0].shape[2]
    tile = min(256, m)
    return call(
        functools.partial(wgrad_cols_kernel, groups, nd),
        (m // tile,),
        [pl.BlockSpec((nt, rows, tile), lambda i: (0, 0, i))] * groups
        + [whole_spec(a.shape) for a in rhs],
        pl.BlockSpec((nd, tile, width // nd), lambda i: (0, i, 0)),
        sds((nd, m, width // nd), BF),
        flops=2 * groups * nt * rows * width * m,
        nbytes=2 * groups * nt * rows * (width + m) + 2 * width * m,
    )(*lhs, *rhs)


def doc_starts(segments):
    row_len = segments.shape[-1]
    ids = jnp.arange(row_len, dtype=jnp.int32)
    change = jnp.concatenate(
        [jnp.ones_like(segments[:, :1], dtype=bool), segments[:, 1:] != segments[:, :-1]], axis=1
    )
    return lax.cummax(jnp.where(change, ids[None, :], 0), axis=1)


def tensor_sum(value, nt):
    if nt != 4:
        return lax.psum(value, "tensor")
    value = value + lax.ppermute(value, "tensor", swap_perm(4, 1))
    return value + lax.ppermute(value, "tensor", swap_perm(4, 2))


def slot_order(blocks, index, nt):
    if nt != 4:
        return blocks
    pairs = jnp.stack([blocks[:, 1], blocks[:, 0], blocks[:, 3], blocks[:, 2]], axis=1)
    blocks = jnp.where(index % 2 == 1, pairs, blocks)
    halves = jnp.stack([blocks[:, 2], blocks[:, 3], blocks[:, 0], blocks[:, 1]], axis=1)
    return jnp.where(index // 2 == 1, halves, blocks)


def per_device(nd, nt, groups, layer_input, segments, qkv_w, out_w, gain1, gateup_w, down_w, gain2, grad_out):
    seqs, local, width = layer_input.shape
    per = seqs // groups
    index = lax.axis_index("tensor").astype(jnp.int32)
    blocks = jnp.arange(nt, dtype=jnp.int32)
    slot_of = blocks ^ index if nt == 4 else blocks

    x = [layer_input[g * per : (g + 1) * per].reshape(per * local, width) for g in range(groups)]
    go = [grad_out[g * per : (g + 1) * per].reshape(per * local, width) for g in range(groups)]
    Order.last = None
    x_all = Gather(layer_input.reshape(seqs * local, width), nt)

    gains = lax.all_gather(jnp.stack([gain1, gain2]), "dp", axis=1, tiled=True).astype(F32)
    g1, g2 = gains[:1], gains[1:]
    qkvo_w = jnp.concatenate([qkv_w, out_w.T[None]])
    full_qkvo = lax.all_gather(qkvo_w, "dp", axis=0, tiled=False)
    full_gateup = lax.all_gather(gateup_w, "dp", axis=0, tiled=False)
    full_down = lax.all_gather(down_w, "dp", axis=0, tiled=False)

    start_abs = doc_starts(segments)
    pos_abs = jnp.arange(segments.shape[1], dtype=jnp.int32)[None, :] - start_abs
    start_slot = slot_order(start_abs.reshape(seqs, nt, local), index, nt)
    pos_slot = slot_order(pos_abs.reshape(seqs, nt, local), index, nt)
    inv_freq = ROPE_BASE ** (-jnp.arange(HALF, dtype=F32) * 2.0 / HEAD_DIM)
    angles = pos_slot.astype(F32)[..., None] * inv_freq
    cos, sin = jnp.cos(angles), jnp.sin(angles)
    cos = jnp.concatenate([cos] * 4, axis=-1)
    sin = jnp.concatenate([-sin, sin] * 2, axis=-1)

    def table(t, g):
        t = t[g * per : (g + 1) * per]
        return jnp.swapaxes(t, 0, 1).reshape(nt, per * local, PAIR)

    coss = [table(cos, g) for g in range(groups)]
    sins = [table(sin, g) for g in range(groups)]
    starts = [start_slot[g * per : (g + 1) * per] for g in range(groups)]

    both = range(groups)
    qkv, ctx, lse, mid, low2, g_mid, g_low = ({} for _ in range(7))
    attn_sum, a2_all, ga2, out_sum, ga1 = ({} for _ in range(5))
    sum1, sum2, gm_all, gmf, g_qkv, g_ctx = ({} for _ in range(6))

    def dp_sum(grad):
        return lax.psum_scatter(grad, "dp", scatter_dimension=0, tiled=False)

    def project(g):
        qkv[g] = project_qkv(a1[g], full_qkvo, coss[g], sins[g], nt)

    def attend(g):
        ctx[g], lse[g] = attention_forward(qkv[g], starts[g], slot_of, nt)
        attn_sum[g] = Scatter(mm_back([ctx[g]], full_qkvo, [3], nt, 4)[0], nt)

    def middle(g):
        mid[g], low2[g] = make_middle(x[g], g2, attn_sum[g].terms)
        a2_all[g] = Gather(low2[g], nt)

    def second_back(g):
        ga2[g] = Scatter(mm_back([gg[g], gu[g]], full_gateup, [0, 1], nt, 2)[0], nt)

    def project_out(g):
        out_sum[g] = Scatter(mm_cols(hid[g], full_down, nt, 2), nt)

    def residual_back(g):
        g_mid[g], g_low[g], sum2[g] = norm_back(go[g], mid[g], g2, ga2[g].terms)
        gm_all[g] = Gather(g_low[g], nt)

    def attention_back_start(g):
        gmf[g], g_ctx[g] = context_back(gm_all[g].pieces, full_qkvo, 3, nt)

    def attention_back(g):
        g_qkv[g] = attention_backward(
            qkv[g], g_ctx[g], starts[g], lse[g], coss[g], sins[g], slot_of, nt
        )

    def input_back(g):
        parts, (sum1[g],) = mm_back(g_qkv[g], full_qkvo, [0, 1, 2], nt, 4, a1[g])
        ga1[g] = Scatter(parts, nt)

    def up_projection(g):
        a2[g], silu[g], slope[g], hid[g] = gate_up(a2_all[g].pieces, full_gateup, nt)

    def hidden_back(g):
        gg[g], gu[g] = gate_back(gof[g], full_down, silu[g], slope[g], nt)

    def finish(g, grad_input):
        return norm_back_rows(g_mid[g], x[g], g1, ga1[g].terms, g, groups, grad_input)

    def by_group(held):
        return [held[g] for g in both]

    def gather_cotangent(g):
        go_all[g] = Gather(link(go[g], flat(x_all.pieces)[-1]), nt)

    a2, silu, slope, hid, gg, gu, go_all, gof = ({} for _ in range(8))
    x_all.second()
    gather_cotangent(0)
    gather_cotangent(1)
    a1 = [assemble(x_all.pieces, nt, 0, groups, g1, coss + sins)]
    project(0)
    attend(0)
    go_all[0].second()
    a1.append(assemble(x_all.pieces, nt, 1, groups, g1))
    project(1)
    attn_sum[0].second()
    attend(1)
    middle(0)
    gof[0] = assemble(go_all[0].pieces, nt, 0, 1)
    attn_sum[1].second()
    a2_all[0].second()
    middle(1)
    go_all[1].second()
    up_projection(0)
    a2_all[1].second()
    gof[1] = assemble(go_all[1].pieces, nt, 0, 1)
    up_projection(1)
    hidden_back(0)
    grad_down = dp_sum(wgrad_cols(by_group(hid), by_group(gof), nd))
    second_back(0)
    hidden_back(1)
    ga2[0].second()
    grad_gateup = wgrad_rows([by_group(a2)], [by_group(gg), by_group(gu)], [0, 0], nd)
    residual_back(0)
    grad_gateup = dp_sum(link(grad_gateup, grad_down))
    second_back(1)
    gm_all[0].second()
    project_out(0)
    attention_back_start(0)
    ga2[1].second()
    attention_back(0)
    residual_back(1)
    input_back(0)
    gm_all[1].second()
    out_sum[0].second()
    attention_back_start(1)
    attention_back(1)
    input_back(1)
    ds = gain1.shape[0]
    gains = tensor_sum(jnp.concatenate([(sum1[0] + sum1[1]) / g1, sum2[0] + sum2[1]]), nt)
    gains = jnp.swapaxes(gains.reshape(2, nd, ds), 0, 1).astype(BF)
    gains = jnp.pad(gains, ((0, 0), (0, 14), (0, qkv_w.shape[2] - ds)))
    project_out(1)
    layer_out = layer_out_rows(mid[0], out_sum[0].terms, 0, groups, None)
    grad_qkvo = wgrad_rows(
        [a1, by_group(gmf)],
        [[g_qkv[g][c] for g in both] for c in range(3)] + [by_group(ctx)],
        [0, 0, 0, 1],
        nd,
        gains,
    )
    ga1[1].second()
    out_sum[1].second()
    grad_qkvo = dp_sum(link(grad_qkvo, grad_gateup))
    layer_out = layer_out_rows(mid[1], out_sum[1].terms, 1, groups, layer_out)
    ga1[0].second()
    grad_input = finish(1, None)
    grad_input = finish(0, grad_input)
    return (
        layer_out.reshape(seqs, local, width),
        grad_input.reshape(seqs, local, width),
        grad_qkvo[: 3 * ds].astype(F32).reshape(3, ds, -1),
        grad_qkvo[3 * ds : 4 * ds].T.astype(F32),
        grad_qkvo[4 * ds, :ds].astype(F32),
        grad_gateup.astype(F32).reshape(2, ds, -1),
        grad_down.astype(F32),
        grad_qkvo[4 * ds + 1, :ds].astype(F32),
    )


def solution(mesh):
    nd, nt = mesh.shape["dp"], mesh.shape["tensor"]
    return jax.shard_map(
        functools.partial(per_device, nd, nt, 2),
        mesh=mesh,
        in_specs=(
            P("dp", "tensor", None),
            P("dp", None),
            P(None, "dp", "tensor"),
            P("tensor", "dp"),
            P("dp"),
            P(None, "dp", "tensor"),
            P("tensor", "dp"),
            P("dp"),
            P("dp", "tensor", None),
        ),
        out_specs=(
            P("dp", "tensor", None),
            P("dp", "tensor", None),
            P(None, "dp", "tensor"),
            P("tensor", "dp"),
            P("dp"),
            P(None, "dp", "tensor"),
            P("tensor", "dp"),
            P("dp"),
        ),
        check_vma=False,
    )
```

```python
import functools

import jax
import jax.numpy as jnp
import numpy as np
from jax import lax
from jax.experimental import pallas as pl
from jax.experimental.pallas import tpu as pltpu
from jax.sharding import PartitionSpec as P

HEAD_DIM = 64
HALF = HEAD_DIM // 2
PAIR = 2 * HEAD_DIM
NORM_EPS = 1e-05
ROPE_BASE = 130000.0
MASKED_SCORE = -1e30
BF = jnp.bfloat16
F32 = jnp.float32
VMEM_SLACK = 8 * 1024 * 1024
VMEM_SMALL = 24 * 1024 * 1024
VMEM_LARGE = 40 * 1024 * 1024
PIN_BYTES = 2 * 1024 * 1024
PIN_BYTES_LARGE = 1024 * 1024
SMALL = 3

NT = (((1,), (1,)), ((), ()))


def dot(a, b):
    return jnp.dot(a, b, preferred_element_type=F32)


def dot_nt(a, b):
    return lax.dot_general(a, b, NT, preferred_element_type=F32)


class Order:
    last = None


HBM = pl.BlockSpec(memory_space=pltpu.HBM)
ANY = pl.BlockSpec(memory_space=pl.ANY)


def is_large(array, least=None):
    return array.size * array.dtype.itemsize >= (least or PIN_BYTES)


def pin(array, least=None):
    return pltpu.with_memory_space_constraint(array, pltpu.HBM) if is_large(array, least) else array


def pinned(shape):
    return pltpu.HBM(shape.shape, shape.dtype) if is_large(shape) else shape


def block_bytes(spec, dtype):
    if spec.block_shape is None:
        return 0
    count = 2 if spec.pipeline_mode is None else spec.pipeline_mode.buffer_count
    return count * int(np.prod([d for d in spec.block_shape if d])) * np.dtype(dtype).itemsize


def call(body, grid, in_specs, out_specs, out_shape, scratch=(), flops=0, nbytes=0, aliases=None, prefetch=0):
    first_extra = prefetch + len(in_specs)
    many = isinstance(out_shape, (list, tuple))
    out_blocks = list(zip(out_specs, out_shape)) if many else [(out_specs, out_shape)]

    def run(*args):
        extra = [] if Order.last is None or any(a is Order.last for a in args) else [pin(Order.last)]

        blocks = list(zip(in_specs, args[prefetch:])) + out_blocks
        vmem = VMEM_SLACK + sum(block_bytes(spec, a.dtype) for spec, a in blocks)
        vmem += sum(int(np.prod(m.shape)) * np.dtype(m.dtype).itemsize for m in scratch)
        least = PIN_BYTES
        if vmem > VMEM_SMALL:
            vmem, least = VMEM_LARGE, PIN_BYTES_LARGE

        args = [pin(a, least) for a in args]

        def ordered_body(*refs):
            body(*refs[:first_extra], *refs[first_extra + len(extra) :])

        outs = pl.pallas_call(
            ordered_body,
            grid_spec=pltpu.PrefetchScalarGridSpec(
                num_scalar_prefetch=prefetch,
                grid=grid,
                in_specs=in_specs + [ANY] * len(extra),
                out_specs=out_specs,
                scratch_shapes=list(scratch),
            ),
            out_shape=[pinned(a) for a in out_shape] if many else pinned(out_shape),
            input_output_aliases=aliases or {},
            cost_estimate=pl.CostEstimate(flops=flops // SMALL, bytes_accessed=nbytes // SMALL, transcendentals=0),
            compiler_params=pltpu.CompilerParams(vmem_limit_bytes=vmem),
        )(*args, *extra)
        Order.last = outs[-1] if isinstance(outs, (list, tuple)) else outs
        return outs

    return run


def link_kernel(value_ref, done_ref, out_ref):
    pass


def link(value, done):
    return call(link_kernel, (1,), [HBM, HBM], HBM, sds(value.shape, value.dtype), aliases={0: 0})(value, done)


def whole_spec(shape, buffers=1):
    zeros = (0,) * len(shape)
    return pl.BlockSpec(shape, lambda *_: zeros, pipeline_mode=pl.Buffered(buffers))


def sds(shape, dtype):
    return jax.ShapeDtypeStruct(shape, dtype)


def swap_perm(count, bit):
    return [(i, i ^ bit) for i in range(count)]


def halves_kernel(y_ref, x_ref, left_ref, right_ref):
    left_ref[...] = y_ref[...]
    right_ref[...] = x_ref[...]


def halves(from_y, from_x):
    rows, width = from_y.shape
    half = width // 2
    tile = min(128, rows)

    def spec(which):
        return pl.BlockSpec((tile, half), lambda i: (i, which))

    return call(
        halves_kernel,
        (rows // tile,),
        [spec(0), spec(1)],
        [spec(0), spec(0)],
        [sds((rows, half), BF)] * 2,
        nbytes=rows * half * 8,
    )(from_y, from_x)


class Gather:
    def __init__(self, block, nt, direct=False):
        self.nt = nt
        if nt != 4:
            full = lax.all_gather(block, "tensor", axis=0, tiled=False)
            self.pieces = [(full[r],) for r in range(nt)]
            return
        self.block = block
        self.from_x = lax.ppermute(block, "tensor", swap_perm(4, 1))
        self.from_y = lax.ppermute(block, "tensor", swap_perm(4, 2))
        if direct:
            diag = lax.ppermute(block, "tensor", swap_perm(4, 3))
            self.pieces = [(block,), (self.from_x,), (self.from_y,), (diag,)]

    def second(self):
        if self.nt != 4:
            return
        left, right = halves(self.from_y, self.from_x)
        diag_x = lax.ppermute(left, "tensor", swap_perm(4, 1))
        diag_y = lax.ppermute(right, "tensor", swap_perm(4, 2))
        self.pieces = [(self.block,), (self.from_x,), (self.from_y,), (diag_x, diag_y)]


def add_halves_kernel(x_ref, for_x_ref, y_ref, for_y_ref, out_x_ref, out_y_ref):
    out_x_ref[...] = (x_ref[...].astype(F32) + for_x_ref[...].astype(F32)).astype(BF)
    out_y_ref[...] = (y_ref[...].astype(F32) + for_y_ref[...].astype(F32)).astype(BF)


def add_halves(to_x, for_x, to_y, for_y):
    rows, width = to_x.shape
    half = width // 2
    tile = min(128, rows)

    def spec(which):
        return pl.BlockSpec((tile, half), lambda i: (i, which))

    return call(
        add_halves_kernel,
        (rows // tile,),
        [spec(1), spec(0), spec(0), spec(0)],
        [spec(1), spec(0)],
        [sds(to_x.shape, BF)] * 2,
        nbytes=rows * half * 12,
        aliases={0: 0, 2: 1},
    )(to_x, for_x, to_y, for_y)


class Scatter:
    def __init__(self, parts, nt):
        self.nt = nt
        if nt != 4:
            full = jnp.stack([p[0] for p in parts])
            self.terms = [lax.psum_scatter(full, "tensor", scatter_dimension=0, tiled=False)]
            return
        (self.own,), (self.to_x,), (self.to_y,), (diag_x, diag_y) = parts
        self.for_y = lax.ppermute(diag_x, "tensor", swap_perm(4, 1))
        self.for_x = lax.ppermute(diag_y, "tensor", swap_perm(4, 2))

    def second(self):
        if self.nt != 4:
            return
        to_x, to_y = add_halves(self.to_x, self.for_x, self.to_y, self.for_y)
        self.terms = [
            self.own,
            lax.ppermute(to_x, "tensor", swap_perm(4, 1)),
            lax.ppermute(to_y, "tensor", swap_perm(4, 2)),
        ]


def piece_shapes(nt, rows, width):
    if nt != 4:
        return [((rows, width),)] * nt
    return [((rows, width),)] * 3 + [((rows, width // 2),) * 2]


def flat(pieces):
    return [a for p in pieces for a in p]


def regroup(items, nt):
    if len(items) == nt:
        return [(a,) for a in items]
    return [(items[0],), (items[1],), (items[2],), (items[3], items[4])]


def fill_from_pieces(refs, full_ref, nt):
    for slot, part in enumerate(regroup(refs, nt)):
        if len(part) == 1:
            full_ref[slot] = part[0][...]
        else:
            half = part[0].shape[1]
            full_ref[slot, :, :half] = part[0][...]
            full_ref[slot, :, half:] = part[1][...]


def out_piece_specs(nt, rows, width, step):
    specs = []
    half_steps = width // step // 2
    for part in piece_shapes(nt, rows, width):
        if len(part) == 1:
            specs.append(pl.BlockSpec((rows, step), lambda j: (0, j)))
        else:
            specs.append(pl.BlockSpec((rows, step), lambda j: (0, jnp.minimum(j, half_steps - 1))))
            specs.append(pl.BlockSpec((rows, step), lambda j: (0, jnp.maximum(j - half_steps, 0))))
    return specs


def store_piece(outs, nt, slot, steps, value):
    part = regroup(outs, nt)[slot]
    if len(part) == 1:
        part[0][...] = value.astype(BF)
    else:
        j = pl.program_id(0)

        @pl.when(j < steps // 2)
        def _():
            part[0][...] = value.astype(BF)

        @pl.when(j >= steps // 2)
        def _():
            part[1][...] = value.astype(BF)


def turn(v):
    lane = lax.broadcasted_iota(jnp.int32, v.shape, 1)
    return jnp.where(lane % HEAD_DIM < HALF, pltpu.roll(v, PAIR - HALF, 1), pltpu.roll(v, HALF, 1))


def rotate(v, cos, sin):
    return v * cos + turn(v) * sin


def unrotate(u, cos, sin):
    return u * cos + turn(u * sin)


def assemble_kernel(nt, count, normed, *refs):
    full_ref = refs[-1]
    fill_from_pieces(refs[:count], full_ref, nt)
    if normed:
        gain = refs[count][...]
        for slot in range(nt):
            x = full_ref[slot].astype(F32)
            scale = lax.rsqrt(jnp.mean(x * x, axis=-1, keepdims=True) + NORM_EPS)
            full_ref[slot] = (x * scale * gain).astype(BF)


def assemble(pieces, nt, group, groups, gain=None, ready=()):
    rows, width = pieces[0][0].shape
    rows //= groups
    tile = min(64, rows)
    first = group * (rows // tile)
    items = flat(pieces)
    extra = [] if gain is None else [gain]
    return call(
        functools.partial(assemble_kernel, nt, len(items), len(extra)),
        (rows // tile,),
        [pl.BlockSpec((tile, a.shape[1]), lambda i: (i + first, 0)) for a in items]
        + [whole_spec(a.shape) for a in extra]
        + [ANY] * len(ready),
        pl.BlockSpec((nt, tile, width), lambda i: (0, i, 0)),
        sds((nt, rows, width), BF),
        nbytes=4 * nt * rows * width,
    )(*items, *extra, *ready)


def qkv_kernel(nt, a1_ref, w_ref, cos_ref, sin_ref, out_ref):
    cols = out_ref.shape[3]
    weight = w_ref[:, 0].reshape(-1, cols)

    @pl.when(pl.program_id(0) < 2)
    def _():
        for slot in range(nt):
            raw = dot(a1_ref[slot], weight)
            cos, sin = cos_ref[slot], sin_ref[slot]
            for p in range(cols // PAIR):
                part = slice(p * PAIR, (p + 1) * PAIR)
                out_ref[0, slot, :, part] = rotate(raw[:, part], cos, sin).astype(BF)

    @pl.when(pl.program_id(0) == 2)
    def _():
        for slot in range(nt):
            out_ref[0, slot] = dot(a1_ref[slot], weight).astype(BF)


def project_qkv(a1, weight, cos, sin, nt):
    nd, _, ds, hc = weight.shape
    _, rows, width = a1.shape
    return call(
        functools.partial(qkv_kernel, nt),
        (3,),
        [
            whole_spec(a1.shape),
            pl.BlockSpec((nd, 1, ds, hc), lambda c: (0, c, 0, 0)),
            whole_spec(cos.shape),
            whole_spec(sin.shape),
        ],
        pl.BlockSpec((1, nt, rows, hc), lambda c: (c, 0, 0, 0)),
        sds((3, nt, rows, hc), BF),
        flops=2 * nt * rows * width * hc * 3,
        nbytes=2 * (nt * rows * width + 3 * width * hc + 3 * nt * rows * hc),
    )(a1, weight, cos, sin)


def allowed_block(start, key_block, query_block, size):
    key_id = lax.broadcasted_iota(jnp.int32, (size, size), 0) + key_block * size
    ok = key_id >= start
    if key_block == query_block:
        ok &= lax.broadcasted_iota(jnp.int32, (size, size), 1) + query_block * size >= key_id
    return ok


def attn_fwd_kernel(nt, slot_ref, q_ref, k_ref, v_ref, start_ref, ctx_ref, lse_ref, vt_ref):
    size = q_ref.shape[1]
    for b in range(nt):
        vt_ref[b] = v_ref[slot_ref[b]].T
    lane = lax.broadcasted_iota(jnp.int32, (size, PAIR), 1)
    for p in range(nt):
        slot = slot_ref[p]
        q = q_ref[slot] * BF(HEAD_DIM**-0.5)
        start = start_ref[0, pl.ds(slot, 1), :]
        outs = []
        for h in range(2):
            qh = jnp.where((lane >= HEAD_DIM) == (h == 1), q, BF(0))
            scores = []
            for b in range(p + 1):
                s = dot_nt(k_ref[slot_ref[b]], qh)
                scores.append(jnp.where(allowed_block(start, b, p, size), s, MASKED_SCORE))
            top = functools.reduce(
                jnp.maximum, [jnp.max(s, axis=0, keepdims=True) for s in scores]
            )
            total = jnp.zeros((1, size), F32)
            acc = jnp.zeros((HEAD_DIM, size), F32)
            for b, s in enumerate(scores):
                e = jnp.exp(s - top)
                total += jnp.sum(e, axis=0, keepdims=True)
                acc += dot(vt_ref[b, h * HEAD_DIM : (h + 1) * HEAD_DIM, :], e.astype(BF))
            outs.append(acc / total)
            lse_ref[0, 0, pl.ds(2 * p + h, 1), :] = top + jnp.log(total)
        ctx_ref[slot] = jnp.concatenate(outs, axis=0).T.astype(BF)


def qkv_specs(nt, size):
    def spec(c):
        return pl.BlockSpec((None, nt, size, PAIR), lambda s, g, _: (c, 0, s, g))

    return [spec(c) for c in range(3)]


def attention_forward(qkv, start, slot_of, nt):
    _, _, rows, hc = qkv.shape
    seqs = start.shape[0]
    size = rows // seqs
    pairs = hc // PAIR
    blk = pl.BlockSpec((nt, size, PAIR), lambda s, g, _: (0, s, g))
    return call(
        functools.partial(attn_fwd_kernel, nt),
        (seqs, pairs),
        qkv_specs(nt, size) + [pl.BlockSpec((1, nt, size), lambda s, g, _: (s, 0, 0))],
        [blk, pl.BlockSpec((1, 1, 2 * nt, size), lambda s, g, _: (s, g, 0, 0))],
        [sds((nt, rows, hc), BF), sds((seqs, pairs, 2 * nt, size), F32)],
        scratch=[pltpu.VMEM((nt, PAIR, size), BF)],
        flops=seqs * pairs * 2 * 4 * (nt * size) ** 2 * 128,
        nbytes=8 * nt * rows * hc,
        prefetch=1,
    )(slot_of, qkv, qkv, qkv, start)


def attn_bwd_kernel(
    nt, slot_ref, q_ref, k_ref, v_ref, go_ref, start_ref, lse_ref, cos_ref, sin_ref,
    gq_ref, gk_ref, gv_ref, kt_ref, dk_ref, dv_ref,
):
    size = q_ref.shape[1]
    scale = HEAD_DIM**-0.5
    for b in range(nt):
        kt_ref[b] = k_ref[slot_ref[b]].T
    dk_ref[...] = jnp.zeros_like(dk_ref)
    dv_ref[...] = jnp.zeros_like(dv_ref)
    lane = lax.broadcasted_iota(jnp.int32, (size, PAIR), 1)
    for p in range(nt):
        slot = slot_ref[p]
        q = q_ref[slot] * BF(scale)
        go = go_ref[slot]
        start = start_ref[0, pl.ds(slot, 1), :]
        outs = []
        for h in range(2):
            mine = (lane >= HEAD_DIM) == (h == 1)
            qh = jnp.where(mine, q, BF(0))
            goh = jnp.where(mine, go, BF(0))
            lse = lse_ref[0, 0, pl.ds(2 * p + h, 1), :]
            probs, grads = [], []
            inner = jnp.zeros((1, size), F32)
            for b in range(p + 1):
                key_slot = slot_ref[b]
                s = dot_nt(k_ref[key_slot], qh)
                s = jnp.where(allowed_block(start, b, p, size), s, MASKED_SCORE)
                e = jnp.exp(s - lse)
                g = dot_nt(v_ref[key_slot], goh)
                inner += jnp.sum(e * g, axis=0, keepdims=True)
                probs.append(e)
                grads.append(g)
            dqt = jnp.zeros((HEAD_DIM, size), F32)
            for b in range(p + 1):
                ds = (probs[b] * (grads[b] - inner)).astype(BF)
                dv_ref[b] += dot(probs[b].astype(BF), goh)
                dk_ref[b] += dot(ds, qh)
                dqt += dot(kt_ref[b, h * HEAD_DIM : (h + 1) * HEAD_DIM, :], ds)
            outs.append(dqt)
        dq = jnp.concatenate(outs, axis=0).T * scale
        gq_ref[slot] = unrotate(dq, cos_ref[slot], sin_ref[slot]).astype(BF)
    for b in range(nt):
        slot = slot_ref[b]
        gk_ref[slot] = unrotate(dk_ref[b], cos_ref[slot], sin_ref[slot]).astype(BF)
        gv_ref[slot] = dv_ref[b].astype(BF)


def attention_backward(qkv, go, start, lse, cos, sin, slot_of, nt):
    _, _, rows, hc = qkv.shape
    seqs = start.shape[0]
    size = rows // seqs
    pairs = hc // PAIR
    blk = pl.BlockSpec((nt, size, PAIR), lambda s, g, _: (0, s, g))
    table = pl.BlockSpec((nt, size, PAIR), lambda s, g, _: (0, s, 0))
    return call(
        functools.partial(attn_bwd_kernel, nt),
        (seqs, pairs),
        qkv_specs(nt, size)
        + [
            blk,
            pl.BlockSpec((1, nt, size), lambda s, g, _: (s, 0, 0)),
            pl.BlockSpec((1, 1, 2 * nt, size), lambda s, g, _: (s, g, 0, 0)),
            table, table,
        ],
        [blk, blk, blk],
        [sds((nt, rows, hc), BF)] * 3,
        scratch=[
            pltpu.VMEM((nt, PAIR, size), BF),
            pltpu.VMEM((nt, size, PAIR), F32),
            pltpu.VMEM((nt, size, PAIR), F32),
        ],
        flops=seqs * pairs * 2 * 10 * (nt * size) ** 2 * 128,
        nbytes=14 * nt * rows * hc,
        prefetch=1,
    )(slot_of, qkv, qkv, qkv, go, start, lse, cos, sin)


def shard_group(nd, count):
    while nd % count or nd // count % 2:
        count //= 2
    return max(count, 1)


def cols_out_kernel(nt, steps, lhs_ref, w_ref, *outs):
    for slot in range(nt):
        lhs = lhs_ref[slot]
        parts = [dot(lhs, w_ref[j]) for j in range(w_ref.shape[0])]
        store_piece(outs, nt, slot, steps, jnp.concatenate(parts, axis=1))


def mm_cols(lhs, weight, nt, group):
    nd, depth, ds = weight.shape
    group = shard_group(nd, group)
    rows = lhs.shape[1]
    width = nd * ds
    shapes = flat(piece_shapes(nt, rows, width))
    outs = call(
        functools.partial(cols_out_kernel, nt, nd // group),
        (nd // group,),
        [whole_spec(lhs.shape), pl.BlockSpec((group, depth, ds), lambda j: (j, 0, 0))],
        out_piece_specs(nt, rows, width, group * ds),
        [sds(s, BF) for s in shapes],
        flops=2 * nt * rows * depth * width,
        nbytes=2 * (nt * rows * (depth + width) + depth * width),
    )(lhs, weight)
    return regroup(outs, nt)


def cols_back_kernel(nt, steps, nlhs, nseen, *refs):
    lhs, w_refs, outs = refs[:nlhs], refs[nlhs : 2 * nlhs], refs[2 * nlhs + nseen :]
    depth = w_refs[0].shape[3]
    weights = [w[:, 0].reshape(-1, depth) for w in w_refs]
    sums = None
    for slot in range(nt):
        total = dot_nt(lhs[0][slot], weights[0])
        for c in range(1, nlhs):
            total += dot_nt(lhs[c][slot], weights[c])
        if nseen:
            part = jnp.sum(total * refs[2 * nlhs][slot].astype(F32), axis=0, keepdims=True)
            sums = part if sums is None else sums + part
        store_piece(outs[: len(outs) - nseen], nt, slot, steps, total)
    if nseen:
        outs[-1][...] = sums


def mm_back(lhs, weight, channels, nt, group, seen=None):
    nd, _, ds, depth = weight.shape
    count = len(lhs)
    group = shard_group(nd, group)
    rows = lhs[0].shape[1]
    width = nd * ds
    shapes = flat(piece_shapes(nt, rows, width))
    step = group * ds
    more = [] if seen is None else [seen]

    def spec(c):
        return pl.BlockSpec((group, 1, ds, depth), lambda j: (j, c, 0, 0))

    outs = call(
        functools.partial(cols_back_kernel, nt, nd // group, count, len(more)),
        (nd // group,),
        [whole_spec(a.shape) for a in lhs]
        + [spec(c) for c in channels]
        + [pl.BlockSpec((nt, rows, step), lambda j: (0, 0, j)) for _ in more],
        out_piece_specs(nt, rows, width, step) + [pl.BlockSpec((1, step), lambda j: (0, j)) for _ in more],
        [sds(s, BF) for s in shapes] + [sds((1, width), F32) for _ in more],
        flops=2 * nt * rows * depth * width * count,
        nbytes=2 * (nt * rows * (depth * count + width) + depth * width * count),
    )(*lhs, *[weight] * count, *more)
    return regroup(outs[: len(shapes)], nt), outs[len(shapes) :]


def gateup_kernel(nt, *refs):
    count = len(flat(piece_shapes(nt, 8, 8)))
    pieces, w_ref, (full_ref, silu_ref, slope_ref, hid_ref) = (
        refs[:count],
        refs[count],
        refs[count + 1 :],
    )

    @pl.when(pl.program_id(0) == 0)
    def _():
        fill_from_pieces(pieces, full_ref, nt)

    cols = hid_ref.shape[2]
    w_gate = w_ref[:, 0].reshape(-1, cols)
    w_up = w_ref[:, 1].reshape(-1, cols)
    for slot in range(nt):
        a2 = full_ref[slot]
        gate = dot(a2, w_gate)
        up = dot(a2, w_up)
        sig = 0.5 + 0.5 * jnp.tanh(0.5 * gate)
        silu = gate * sig
        silu_ref[slot] = silu.astype(BF)
        slope_ref[slot] = (up * (sig + silu - silu * sig)).astype(BF)
        hid_ref[slot] = (silu * up).astype(BF)


def gate_up(pieces, weight, nt):
    nd, _, ds, ff = weight.shape
    rows, width = pieces[0][0].shape
    step = min(512, ff)
    blk = pl.BlockSpec((nt, rows, step), lambda j: (0, 0, j))
    return call(
        functools.partial(gateup_kernel, nt),
        (ff // step,),
        [whole_spec(a.shape) for a in flat(pieces)]
        + [pl.BlockSpec((nd, 2, ds, step), lambda j: (0, 0, 0, j))],
        [whole_spec((nt, rows, width)), blk, blk, blk],
        [sds((nt, rows, width), BF)] + [sds((nt, rows, ff), BF)] * 3,
        flops=4 * nt * rows * width * ff,
        nbytes=2 * (2 * nt * rows * width + 2 * width * ff + 3 * nt * rows * ff),
    )(*flat(pieces), weight)


def gate_back_kernel(nt, full_ref, w_ref, silu_ref, slope_ref, gg_ref, gu_ref):
    weight = jnp.concatenate([w_ref[j] for j in range(w_ref.shape[0])], axis=1)
    for slot in range(nt):
        gh = dot_nt(full_ref[slot], weight)
        gg_ref[slot] = (gh * slope_ref[slot].astype(F32)).astype(BF)
        gu_ref[slot] = (gh * silu_ref[slot].astype(F32)).astype(BF)


def gate_back(full, weight, silu, slope, nt):
    nd, ff, ds = weight.shape
    _, rows, width = full.shape
    step = min(512, ff)
    blk = pl.BlockSpec((nt, rows, step), lambda j: (0, 0, j))
    return call(
        functools.partial(gate_back_kernel, nt),
        (ff // step,),
        [whole_spec(full.shape), pl.BlockSpec((nd, step, ds), lambda j: (0, j, 0)), blk, blk],
        [blk, blk],
        [sds((nt, rows, ff), BF)] * 2,
        flops=2 * nt * rows * width * ff,
        nbytes=2 * (nt * rows * width + width * ff + 4 * nt * rows * ff),
    )(full, weight, silu, slope)


def context_back_kernel(nt, *refs):
    pieces, w_ref, (full_ref, out_ref) = refs[:-3], refs[-3], refs[-2:]

    @pl.when(pl.program_id(0) == 0)
    def _():
        fill_from_pieces(pieces, full_ref, nt)

    weight = w_ref[:, 0].reshape(-1, w_ref.shape[3])
    for slot in range(nt):
        out_ref[slot] = dot(full_ref[slot], weight).astype(BF)


def context_back(pieces, weight, channel, nt):
    nd, _, ds, hc = weight.shape
    rows, width = pieces[0][0].shape
    step = min(256, hc)
    return call(
        functools.partial(context_back_kernel, nt),
        (hc // step,),
        [whole_spec(a.shape) for a in flat(pieces)]
        + [pl.BlockSpec((nd, 1, ds, step), lambda j: (0, channel, 0, j))],
        [whole_spec((nt, rows, width)), pl.BlockSpec((nt, rows, step), lambda j: (0, 0, j))],
        [sds((nt, rows, width), BF), sds((nt, rows, hc), BF)],
        flops=2 * nt * rows * width * hc,
        nbytes=2 * (2 * nt * rows * width + width * hc + nt * rows * hc),
    )(*flat(pieces), weight)


def middle_kernel(nterms, x_ref, gain_ref, *refs):
    terms, (mid_ref, low_ref) = refs[:nterms], refs[nterms:]
    mid = x_ref[...].astype(F32) + sum_terms(terms)
    mid_ref[...] = mid
    scale = lax.rsqrt(jnp.mean(mid * mid, axis=-1, keepdims=True) + NORM_EPS)
    low_ref[...] = (mid * scale * gain_ref[...]).astype(BF)


def make_middle(x, gain, terms):
    rows, width = x.shape
    tile = min(128, rows)
    blk = pl.BlockSpec((tile, width), lambda i: (i, 0))
    return call(
        functools.partial(middle_kernel, len(terms)),
        (rows // tile,),
        [blk, whole_spec(gain.shape)] + [blk] * len(terms),
        [blk, blk],
        [sds((rows, width), F32), sds((rows, width), BF)],
        nbytes=rows * width * (8 + 2 * len(terms)),
    )(x, gain, *terms)


def sum_terms(terms):
    total = terms[0][...].astype(F32)
    for t in terms[1:]:
        total += t[...].astype(F32)
    return total


def layer_out_kernel(nterms, mid_ref, *refs):
    refs[-1][...] = (mid_ref[...] + sum_terms(refs[:nterms])).astype(BF)


def place(group, groups, rows, tile, width, into):
    steps = rows // tile
    spec = pl.BlockSpec((tile, width), lambda i: (i + group * steps, 0))
    return spec, sds((groups * rows, width), BF), [] if into is None else [into]


def layer_out_rows(mid, terms, group, groups, into):
    rows, width = mid.shape
    tile = min(128, rows)
    blk = pl.BlockSpec((tile, width), lambda i: (i, 0))
    spec, shape, old = place(group, groups, rows, tile, width, into)
    return call(
        functools.partial(layer_out_kernel, len(terms)),
        (rows // tile,),
        [blk] * (1 + len(terms)) + [HBM] * len(old),
        spec,
        shape,
        nbytes=rows * width * (6 + 2 * len(terms)),
        aliases={1 + len(terms): 0} if old else None,
    )(mid, *terms, *old)


def norm_back_kernel(nterms, nouts, first_ref, v_ref, gain_ref, *refs):
    terms, outs, sums = refs[:nterms], refs[len(refs) - nouts :], []
    if nouts == 3:
        outs, sums = outs[:2], outs[2:]
    u = sum_terms(terms)
    v = v_ref[...].astype(F32)
    q = lax.rsqrt(jnp.mean(v * v, axis=-1, keepdims=True) + NORM_EPS)
    ug = u * gain_ref[...]
    inner = jnp.mean(ug * v, axis=-1, keepdims=True)
    grad = first_ref[...].astype(F32) + (q * ug - v * (q * q * q * inner))
    for out in outs:
        out[...] = grad.astype(out.dtype)
    for sum_ref in sums:

        @pl.when(pl.program_id(0) == 0)
        def _():
            sum_ref[...] = jnp.zeros_like(sum_ref)

        sum_ref[...] += jnp.sum(u * v * q, axis=0, keepdims=True)


def norm_back(first, v, gain, terms):
    rows, width = v.shape
    tile = min(128, rows)
    blk = pl.BlockSpec((tile, width), lambda i: (i, 0))
    return call(
        functools.partial(norm_back_kernel, len(terms), 3),
        (rows // tile,),
        [blk, blk, whole_spec(gain.shape)] + [blk] * len(terms),
        [blk, blk, pl.BlockSpec((1, width), lambda i: (0, 0))],
        [sds((rows, width), F32), sds((rows, width), BF), sds((1, width), F32)],
        nbytes=rows * width * (12 + 2 * len(terms)),
    )(first, v, gain, *terms)


def norm_back_rows(first, v, gain, terms, group, groups, into):
    rows, width = v.shape
    tile = min(128, rows)
    blk = pl.BlockSpec((tile, width), lambda i: (i, 0))
    spec, shape, old = place(group, groups, rows, tile, width, into)
    return call(
        functools.partial(norm_back_kernel, len(terms), 1),
        (rows // tile,),
        [blk, blk, whole_spec(gain.shape)] + [blk] * len(terms) + [HBM] * len(old),
        spec,
        shape,
        nbytes=rows * width * (12 + 2 * len(terms)),
        aliases={3 + len(terms): 0} if old else None,
    )(first, v, gain, *terms, *old)


def wgrad_rows_kernel(groups, which, nmore, *refs):
    nlhs = groups * (max(which) + 1)
    lhs, rhs, out_ref = refs[:nlhs], refs[nlhs : nlhs + groups * len(which)], refs[-1]
    tile = lhs[0].shape[2]
    left = [a[...].reshape(-1, tile).T for a in lhs]
    for c, w in enumerate(which):
        total = None
        for g in range(groups):
            a = left[w * groups + g]
            term = dot(a, rhs[c * groups + g][...].reshape(a.shape[1], -1))
            total = term if total is None else total + term
        out_ref[0, c * tile : (c + 1) * tile] = total.astype(BF)
    if nmore:
        out_ref[0, len(which) * tile :] = refs[-2][0]


def wgrad_rows(lhs, rhs, which, nd, more=None):
    groups = len(lhs[0])
    nt, rows, width = lhs[0][0].shape
    ds = width // nd
    n = rhs[0][0].shape[2]
    more = [] if more is None else [more]
    height = len(rhs) * ds + sum(a.shape[1] for a in more)
    return call(
        functools.partial(wgrad_rows_kernel, groups, which, len(more)),
        (nd,),
        [pl.BlockSpec((nt, rows, ds), lambda j: (0, 0, j))] * (groups * len(lhs))
        + [whole_spec(a.shape) for r in rhs for a in r]
        + [pl.BlockSpec((1,) + a.shape[1:], lambda j: (j, 0, 0)) for a in more],
        pl.BlockSpec((1, height, n), lambda j: (j, 0, 0)),
        sds((nd, height, n), BF),
        flops=2 * groups * nt * rows * width * n * len(rhs),
        nbytes=2 * groups * nt * rows * (width + n * len(rhs)) + 2 * width * n * len(rhs),
    )(*[a for l in lhs for a in l], *[a for r in rhs for a in r], *more)


def wgrad_cols_kernel(groups, nd, *refs):
    lhs, rhs, out_ref = refs[:groups], refs[groups:-1], refs[-1]
    tile = lhs[0].shape[2]
    ds = out_ref.shape[2]
    left = [a[...].reshape(-1, tile).T for a in lhs]
    total = None
    for g in range(groups):
        term = dot(left[g], rhs[g][...].reshape(left[g].shape[1], -1))
        total = term if total is None else total + term
    for j in range(nd):
        out_ref[j] = total[:, j * ds : (j + 1) * ds].astype(BF)


def wgrad_cols(lhs, rhs, nd):
    groups = len(lhs)
    nt, rows, m = lhs[0].shape
    width = rhs[0].shape[2]
    tile = min(256, m)
    return call(
        functools.partial(wgrad_cols_kernel, groups, nd),
        (m // tile,),
        [pl.BlockSpec((nt, rows, tile), lambda i: (0, 0, i))] * groups
        + [whole_spec(a.shape) for a in rhs],
        pl.BlockSpec((nd, tile, width // nd), lambda i: (0, i, 0)),
        sds((nd, m, width // nd), BF),
        flops=2 * groups * nt * rows * width * m,
        nbytes=2 * groups * nt * rows * (width + m) + 2 * width * m,
    )(*lhs, *rhs)


def doc_starts(segments):
    row_len = segments.shape[-1]
    ids = jnp.arange(row_len, dtype=jnp.int32)
    change = jnp.concatenate(
        [jnp.ones_like(segments[:, :1], dtype=bool), segments[:, 1:] != segments[:, :-1]], axis=1
    )
    return lax.cummax(jnp.where(change, ids[None, :], 0), axis=1)


def tensor_sum(value, nt):
    if nt != 4:
        return lax.psum(value, "tensor")
    value = value + lax.ppermute(value, "tensor", swap_perm(4, 1))
    return value + lax.ppermute(value, "tensor", swap_perm(4, 2))


def slot_order(blocks, index, nt):
    if nt != 4:
        return blocks
    pairs = jnp.stack([blocks[:, 1], blocks[:, 0], blocks[:, 3], blocks[:, 2]], axis=1)
    blocks = jnp.where(index % 2 == 1, pairs, blocks)
    halves = jnp.stack([blocks[:, 2], blocks[:, 3], blocks[:, 0], blocks[:, 1]], axis=1)
    return jnp.where(index // 2 == 1, halves, blocks)


def per_device(nd, nt, groups, layer_input, segments, qkv_w, out_w, gain1, gateup_w, down_w, gain2, grad_out):
    seqs, local, width = layer_input.shape
    per = seqs // groups
    index = lax.axis_index("tensor").astype(jnp.int32)
    blocks = jnp.arange(nt, dtype=jnp.int32)
    slot_of = blocks ^ index if nt == 4 else blocks

    x = [layer_input[g * per : (g + 1) * per].reshape(per * local, width) for g in range(groups)]
    go = [grad_out[g * per : (g + 1) * per].reshape(per * local, width) for g in range(groups)]
    Order.last = None
    x_all = Gather(layer_input.reshape(seqs * local, width), nt)

    gains = lax.all_gather(jnp.stack([gain1, gain2]), "dp", axis=1, tiled=True).astype(F32)
    g1, g2 = gains[:1], gains[1:]
    qkvo_w = jnp.concatenate([qkv_w, out_w.T[None]])
    full_qkvo = lax.all_gather(qkvo_w, "dp", axis=0, tiled=False)
    full_gateup = lax.all_gather(gateup_w, "dp", axis=0, tiled=False)
    full_down = lax.all_gather(down_w, "dp", axis=0, tiled=False)

    start_abs = doc_starts(segments)
    pos_abs = jnp.arange(segments.shape[1], dtype=jnp.int32)[None, :] - start_abs
    start_slot = slot_order(start_abs.reshape(seqs, nt, local), index, nt)
    pos_slot = slot_order(pos_abs.reshape(seqs, nt, local), index, nt)
    inv_freq = ROPE_BASE ** (-jnp.arange(HALF, dtype=F32) * 2.0 / HEAD_DIM)
    angles = pos_slot.astype(F32)[..., None] * inv_freq
    cos, sin = jnp.cos(angles), jnp.sin(angles)
    cos = jnp.concatenate([cos] * 4, axis=-1)
    sin = jnp.concatenate([-sin, sin] * 2, axis=-1)

    def table(t, g):
        t = t[g * per : (g + 1) * per]
        return jnp.swapaxes(t, 0, 1).reshape(nt, per * local, PAIR)

    coss = [table(cos, g) for g in range(groups)]
    sins = [table(sin, g) for g in range(groups)]
    starts = [start_slot[g * per : (g + 1) * per] for g in range(groups)]

    both = range(groups)
    qkv, ctx, lse, mid, low2, g_mid, g_low = ({} for _ in range(7))
    attn_sum, a2_all, ga2, out_sum, ga1 = ({} for _ in range(5))
    sum1, sum2, gm_all, gmf, g_qkv, g_ctx = ({} for _ in range(6))

    def dp_sum(grad):
        return lax.psum_scatter(grad, "dp", scatter_dimension=0, tiled=False)

    def project(g):
        qkv[g] = project_qkv(a1[g], full_qkvo, coss[g], sins[g], nt)

    def attend(g):
        ctx[g], lse[g] = attention_forward(qkv[g], starts[g], slot_of, nt)
        attn_sum[g] = Scatter(mm_back([ctx[g]], full_qkvo, [3], nt, 4)[0], nt)

    def middle(g):
        mid[g], low2[g] = make_middle(x[g], g2, attn_sum[g].terms)
        a2_all[g] = Gather(low2[g], nt)

    def second_back(g):
        ga2[g] = Scatter(mm_back([gg[g], gu[g]], full_gateup, [0, 1], nt, 2)[0], nt)

    def project_out(g):
        out_sum[g] = Scatter(mm_cols(hid[g], full_down, nt, 2), nt)

    def residual_back(g):
        g_mid[g], g_low[g], sum2[g] = norm_back(go[g], mid[g], g2, ga2[g].terms)
        gm_all[g] = Gather(g_low[g], nt)

    def attention_back_start(g):
        gmf[g], g_ctx[g] = context_back(gm_all[g].pieces, full_qkvo, 3, nt)

    def attention_back(g):
        g_qkv[g] = attention_backward(
            qkv[g], g_ctx[g], starts[g], lse[g], coss[g], sins[g], slot_of, nt
        )

    def input_back(g):
        parts, (sum1[g],) = mm_back(g_qkv[g], full_qkvo, [0, 1, 2], nt, 4, a1[g])
        ga1[g] = Scatter(parts, nt)

    def up_projection(g):
        a2[g], silu[g], slope[g], hid[g] = gate_up(a2_all[g].pieces, full_gateup, nt)

    def hidden_back(g):
        gg[g], gu[g] = gate_back(gof[g], full_down, silu[g], slope[g], nt)

    def finish(g, grad_input):
        return norm_back_rows(g_mid[g], x[g], g1, ga1[g].terms, g, groups, grad_input)

    def by_group(held):
        return [held[g] for g in both]

    def gather_cotangent(g):
        go_all[g] = Gather(link(go[g], flat(x_all.pieces)[-1]), nt)

    a2, silu, slope, hid, gg, gu, go_all, gof = ({} for _ in range(8))
    x_all.second()
    gather_cotangent(0)
    gather_cotangent(1)
    a1 = [assemble(x_all.pieces, nt, 0, groups, g1, coss + sins)]
    project(0)
    attend(0)
    go_all[0].second()
    a1.append(assemble(x_all.pieces, nt, 1, groups, g1))
    project(1)
    attn_sum[0].second()
    attend(1)
    middle(0)
    gof[0] = assemble(go_all[0].pieces, nt, 0, 1)
    attn_sum[1].second()
    a2_all[0].second()
    middle(1)
    go_all[1].second()
    up_projection(0)
    a2_all[1].second()
    gof[1] = assemble(go_all[1].pieces, nt, 0, 1)
    up_projection(1)
    hidden_back(0)
    grad_down = dp_sum(wgrad_cols(by_group(hid), by_group(gof), nd))
    second_back(0)
    hidden_back(1)
    ga2[0].second()
    grad_gateup = wgrad_rows([by_group(a2)], [by_group(gg), by_group(gu)], [0, 0], nd)
    residual_back(0)
    grad_gateup = dp_sum(link(grad_gateup, grad_down))
    second_back(1)
    gm_all[0].second()
    project_out(0)
    attention_back_start(0)
    ga2[1].second()
    attention_back(0)
    residual_back(1)
    input_back(0)
    project_out(1)
    gm_all[1].second()
    out_sum[0].second()
    attention_back_start(1)
    attention_back(1)
    input_back(1)
    ds = gain1.shape[0]
    gains = tensor_sum(jnp.concatenate([(sum1[0] + sum1[1]) / g1, sum2[0] + sum2[1]]), nt)
    gains = jnp.swapaxes(gains.reshape(2, nd, ds), 0, 1).astype(BF)
    gains = jnp.pad(gains, ((0, 0), (0, 14), (0, qkv_w.shape[2] - ds)))
    out_sum[1].second()
    layer_out = layer_out_rows(mid[0], out_sum[0].terms, 0, groups, None)
    grad_qkvo = wgrad_rows(
        [a1, by_group(gmf)],
        [[g_qkv[g][c] for g in both] for c in range(3)] + [by_group(ctx)],
        [0, 0, 0, 1],
        nd,
        gains,
    )
    ga1[1].second()
    grad_qkvo = dp_sum(link(grad_qkvo, grad_gateup))
    layer_out = layer_out_rows(mid[1], out_sum[1].terms, 1, groups, layer_out)
    ga1[0].second()
    grad_input = finish(1, None)
    grad_input = finish(0, grad_input)
    return (
        layer_out.reshape(seqs, local, width),
        grad_input.reshape(seqs, local, width),
        grad_qkvo[: 3 * ds].astype(F32).reshape(3, ds, -1),
        grad_qkvo[3 * ds : 4 * ds].T.astype(F32),
        grad_qkvo[4 * ds, :ds].astype(F32),
        grad_gateup.astype(F32).reshape(2, ds, -1),
        grad_down.astype(F32),
        grad_qkvo[4 * ds + 1, :ds].astype(F32),
    )


def solution(mesh):
    nd, nt = mesh.shape["dp"], mesh.shape["tensor"]
    return jax.shard_map(
        functools.partial(per_device, nd, nt, 2),
        mesh=mesh,
        in_specs=(
            P("dp", "tensor", None),
            P("dp", None),
            P(None, "dp", "tensor"),
            P("tensor", "dp"),
            P("dp"),
            P(None, "dp", "tensor"),
            P("tensor", "dp"),
            P("dp"),
            P("dp", "tensor", None),
        ),
        out_specs=(
            P("dp", "tensor", None),
            P("dp", "tensor", None),
            P(None, "dp", "tensor"),
            P("tensor", "dp"),
            P("dp"),
            P(None, "dp", "tensor"),
            P("tensor", "dp"),
            P("dp"),
        ),
        check_vma=False,
    )
```

```python
import functools

import jax
import jax.numpy as jnp
import numpy as np
from jax import lax
from jax.experimental import pallas as pl
from jax.experimental.pallas import tpu as pltpu
from jax.sharding import PartitionSpec as P

HEAD_DIM = 64
HALF = HEAD_DIM // 2
PAIR = 2 * HEAD_DIM
NORM_EPS = 1e-05
ROPE_BASE = 130000.0
MASKED_SCORE = -1e30
BF = jnp.bfloat16
F32 = jnp.float32
VMEM_SLACK = 8 * 1024 * 1024
VMEM_SMALL = 24 * 1024 * 1024
VMEM_LARGE = 40 * 1024 * 1024
PIN_BYTES = 2 * 1024 * 1024
PIN_BYTES_LARGE = 1024 * 1024
SMALL = 3

NT = (((1,), (1,)), ((), ()))


def dot(a, b):
    return jnp.dot(a, b, preferred_element_type=F32)


def dot_nt(a, b):
    return lax.dot_general(a, b, NT, preferred_element_type=F32)


class Order:
    last = None


HBM = pl.BlockSpec(memory_space=pltpu.HBM)
ANY = pl.BlockSpec(memory_space=pl.ANY)


def is_large(array, least=None):
    return array.size * array.dtype.itemsize >= (least or PIN_BYTES)


def pin(array, least=None):
    return pltpu.with_memory_space_constraint(array, pltpu.HBM) if is_large(array, least) else array


def pinned(shape):
    return pltpu.HBM(shape.shape, shape.dtype) if is_large(shape) else shape


def block_bytes(spec, dtype):
    if spec.block_shape is None:
        return 0
    count = 2 if spec.pipeline_mode is None else spec.pipeline_mode.buffer_count
    return count * int(np.prod([d for d in spec.block_shape if d])) * np.dtype(dtype).itemsize


def call(body, grid, in_specs, out_specs, out_shape, scratch=(), flops=0, nbytes=0, aliases=None, prefetch=0):
    first_extra = prefetch + len(in_specs)
    many = isinstance(out_shape, (list, tuple))
    out_blocks = list(zip(out_specs, out_shape)) if many else [(out_specs, out_shape)]

    def run(*args):
        extra = [] if Order.last is None or any(a is Order.last for a in args) else [pin(Order.last)]

        blocks = list(zip(in_specs, args[prefetch:])) + out_blocks
        vmem = VMEM_SLACK + sum(block_bytes(spec, a.dtype) for spec, a in blocks)
        vmem += sum(int(np.prod(m.shape)) * np.dtype(m.dtype).itemsize for m in scratch)
        least = PIN_BYTES
        if vmem > VMEM_SMALL:
            vmem, least = VMEM_LARGE, PIN_BYTES_LARGE

        args = [pin(a, least) for a in args]

        def ordered_body(*refs):
            body(*refs[:first_extra], *refs[first_extra + len(extra) :])

        outs = pl.pallas_call(
            ordered_body,
            grid_spec=pltpu.PrefetchScalarGridSpec(
                num_scalar_prefetch=prefetch,
                grid=grid,
                in_specs=in_specs + [ANY] * len(extra),
                out_specs=out_specs,
                scratch_shapes=list(scratch),
            ),
            out_shape=[pinned(a) for a in out_shape] if many else pinned(out_shape),
            input_output_aliases=aliases or {},
            cost_estimate=pl.CostEstimate(flops=flops // SMALL, bytes_accessed=nbytes // SMALL, transcendentals=0),
            compiler_params=pltpu.CompilerParams(vmem_limit_bytes=vmem),
        )(*args, *extra)
        Order.last = outs[-1] if isinstance(outs, (list, tuple)) else outs
        return outs

    return run


def link_kernel(value_ref, done_ref, out_ref):
    pass


def link(value, done):
    return call(link_kernel, (1,), [HBM, HBM], HBM, sds(value.shape, value.dtype), aliases={0: 0})(value, done)


def whole_spec(shape, buffers=1):
    zeros = (0,) * len(shape)
    return pl.BlockSpec(shape, lambda *_: zeros, pipeline_mode=pl.Buffered(buffers))


def sds(shape, dtype):
    return jax.ShapeDtypeStruct(shape, dtype)


def swap_perm(count, bit):
    return [(i, i ^ bit) for i in range(count)]


def halves_kernel(y_ref, x_ref, left_ref, right_ref):
    left_ref[...] = y_ref[...]
    right_ref[...] = x_ref[...]


def halves(from_y, from_x):
    rows, width = from_y.shape
    half = width // 2
    tile = min(128, rows)

    def spec(which):
        return pl.BlockSpec((tile, half), lambda i: (i, which))

    return call(
        halves_kernel,
        (rows // tile,),
        [spec(0), spec(1)],
        [spec(0), spec(0)],
        [sds((rows, half), BF)] * 2,
        nbytes=rows * half * 8,
    )(from_y, from_x)


class Gather:
    def __init__(self, block, nt, direct=False):
        self.nt = nt
        if nt != 4:
            full = lax.all_gather(block, "tensor", axis=0, tiled=False)
            self.pieces = [(full[r],) for r in range(nt)]
            return
        self.block = block
        self.from_x = lax.ppermute(block, "tensor", swap_perm(4, 1))
        self.from_y = lax.ppermute(block, "tensor", swap_perm(4, 2))
        if direct:
            diag = lax.ppermute(block, "tensor", swap_perm(4, 3))
            self.pieces = [(block,), (self.from_x,), (self.from_y,), (diag,)]

    def second(self):
        if self.nt != 4:
            return
        left, right = halves(self.from_y, self.from_x)
        diag_x = lax.ppermute(left, "tensor", swap_perm(4, 1))
        diag_y = lax.ppermute(right, "tensor", swap_perm(4, 2))
        self.pieces = [(self.block,), (self.from_x,), (self.from_y,), (diag_x, diag_y)]


def add_halves_kernel(x_ref, for_x_ref, y_ref, for_y_ref, out_x_ref, out_y_ref):
    out_x_ref[...] = (x_ref[...].astype(F32) + for_x_ref[...].astype(F32)).astype(BF)
    out_y_ref[...] = (y_ref[...].astype(F32) + for_y_ref[...].astype(F32)).astype(BF)


def add_halves(to_x, for_x, to_y, for_y):
    rows, width = to_x.shape
    half = width // 2
    tile = min(128, rows)

    def spec(which):
        return pl.BlockSpec((tile, half), lambda i: (i, which))

    return call(
        add_halves_kernel,
        (rows // tile,),
        [spec(1), spec(0), spec(0), spec(0)],
        [spec(1), spec(0)],
        [sds(to_x.shape, BF)] * 2,
        nbytes=rows * half * 12,
        aliases={0: 0, 2: 1},
    )(to_x, for_x, to_y, for_y)


class Scatter:
    def __init__(self, parts, nt):
        self.nt = nt
        if nt != 4:
            full = jnp.stack([p[0] for p in parts])
            self.terms = [lax.psum_scatter(full, "tensor", scatter_dimension=0, tiled=False)]
            return
        (self.own,), (self.to_x,), (self.to_y,), (diag_x, diag_y) = parts
        self.for_y = lax.ppermute(diag_x, "tensor", swap_perm(4, 1))
        self.for_x = lax.ppermute(diag_y, "tensor", swap_perm(4, 2))

    def second(self):
        if self.nt != 4:
            return
        to_x, to_y = add_halves(self.to_x, self.for_x, self.to_y, self.for_y)
        self.terms = [
            self.own,
            lax.ppermute(to_x, "tensor", swap_perm(4, 1)),
            lax.ppermute(to_y, "tensor", swap_perm(4, 2)),
        ]


def piece_shapes(nt, rows, width):
    if nt != 4:
        return [((rows, width),)] * nt
    return [((rows, width),)] * 3 + [((rows, width // 2),) * 2]


def flat(pieces):
    return [a for p in pieces for a in p]


def regroup(items, nt):
    if len(items) == nt:
        return [(a,) for a in items]
    return [(items[0],), (items[1],), (items[2],), (items[3], items[4])]


def fill_from_pieces(refs, full_ref, nt):
    for slot, part in enumerate(regroup(refs, nt)):
        if len(part) == 1:
            full_ref[slot] = part[0][...]
        else:
            half = part[0].shape[1]
            full_ref[slot, :, :half] = part[0][...]
            full_ref[slot, :, half:] = part[1][...]


def out_piece_specs(nt, rows, width, step):
    specs = []
    half_steps = width // step // 2
    for part in piece_shapes(nt, rows, width):
        if len(part) == 1:
            specs.append(pl.BlockSpec((rows, step), lambda j: (0, j)))
        else:
            specs.append(pl.BlockSpec((rows, step), lambda j: (0, jnp.minimum(j, half_steps - 1))))
            specs.append(pl.BlockSpec((rows, step), lambda j: (0, jnp.maximum(j - half_steps, 0))))
    return specs


def store_piece(outs, nt, slot, steps, value):
    part = regroup(outs, nt)[slot]
    if len(part) == 1:
        part[0][...] = value.astype(BF)
    else:
        j = pl.program_id(0)

        @pl.when(j < steps // 2)
        def _():
            part[0][...] = value.astype(BF)

        @pl.when(j >= steps // 2)
        def _():
            part[1][...] = value.astype(BF)


def turn(v):
    lane = lax.broadcasted_iota(jnp.int32, v.shape, 1)
    return jnp.where(lane % HEAD_DIM < HALF, pltpu.roll(v, PAIR - HALF, 1), pltpu.roll(v, HALF, 1))


def rotate(v, cos, sin):
    return v * cos + turn(v) * sin


def unrotate(u, cos, sin):
    return u * cos + turn(u * sin)


def assemble_kernel(nt, count, normed, *refs):
    full_ref = refs[-1]
    fill_from_pieces(refs[:count], full_ref, nt)
    if normed:
        gain = refs[count][...]
        for slot in range(nt):
            x = full_ref[slot].astype(F32)
            scale = lax.rsqrt(jnp.mean(x * x, axis=-1, keepdims=True) + NORM_EPS)
            full_ref[slot] = (x * scale * gain).astype(BF)


def assemble(pieces, nt, group, groups, gain=None, ready=()):
    rows, width = pieces[0][0].shape
    rows //= groups
    tile = min(64, rows)
    first = group * (rows // tile)
    items = flat(pieces)
    extra = [] if gain is None else [gain]
    return call(
        functools.partial(assemble_kernel, nt, len(items), len(extra)),
        (rows // tile,),
        [pl.BlockSpec((tile, a.shape[1]), lambda i: (i + first, 0)) for a in items]
        + [whole_spec(a.shape) for a in extra]
        + [ANY] * len(ready),
        pl.BlockSpec((nt, tile, width), lambda i: (0, i, 0)),
        sds((nt, rows, width), BF),
        nbytes=4 * nt * rows * width,
    )(*items, *extra, *ready)


def qkv_kernel(nt, a1_ref, w_ref, cos_ref, sin_ref, out_ref):
    cols = out_ref.shape[3]
    weight = w_ref[:, 0].reshape(-1, cols)

    @pl.when(pl.program_id(0) < 2)
    def _():
        for slot in range(nt):
            raw = dot(a1_ref[slot], weight)
            cos, sin = cos_ref[slot], sin_ref[slot]
            for p in range(cols // PAIR):
                part = slice(p * PAIR, (p + 1) * PAIR)
                out_ref[0, slot, :, part] = rotate(raw[:, part], cos, sin).astype(BF)

    @pl.when(pl.program_id(0) == 2)
    def _():
        for slot in range(nt):
            out_ref[0, slot] = dot(a1_ref[slot], weight).astype(BF)


def project_qkv(a1, weight, cos, sin, nt):
    nd, _, ds, hc = weight.shape
    _, rows, width = a1.shape
    return call(
        functools.partial(qkv_kernel, nt),
        (3,),
        [
            whole_spec(a1.shape),
            pl.BlockSpec((nd, 1, ds, hc), lambda c: (0, c, 0, 0)),
            whole_spec(cos.shape),
            whole_spec(sin.shape),
        ],
        pl.BlockSpec((1, nt, rows, hc), lambda c: (c, 0, 0, 0)),
        sds((3, nt, rows, hc), BF),
        flops=2 * nt * rows * width * hc * 3,
        nbytes=2 * (nt * rows * width + 3 * width * hc + 3 * nt * rows * hc),
    )(a1, weight, cos, sin)


def allowed_block(start, key_block, query_block, size):
    key_id = lax.broadcasted_iota(jnp.int32, (size, size), 0) + key_block * size
    ok = key_id >= start
    if key_block == query_block:
        ok &= lax.broadcasted_iota(jnp.int32, (size, size), 1) + query_block * size >= key_id
    return ok


def attn_fwd_kernel(nt, slot_ref, q_ref, k_ref, v_ref, start_ref, ctx_ref, lse_ref, vt_ref):
    size = q_ref.shape[1]
    for b in range(nt):
        vt_ref[b] = v_ref[slot_ref[b]].T
    lane = lax.broadcasted_iota(jnp.int32, (size, PAIR), 1)
    for p in range(nt):
        slot = slot_ref[p]
        q = q_ref[slot] * BF(HEAD_DIM**-0.5)
        start = start_ref[0, pl.ds(slot, 1), :]
        outs = []
        for h in range(2):
            qh = jnp.where((lane >= HEAD_DIM) == (h == 1), q, BF(0))
            scores = []
            for b in range(p + 1):
                s = dot_nt(k_ref[slot_ref[b]], qh)
                scores.append(jnp.where(allowed_block(start, b, p, size), s, MASKED_SCORE))
            top = functools.reduce(
                jnp.maximum, [jnp.max(s, axis=0, keepdims=True) for s in scores]
            )
            total = jnp.zeros((1, size), F32)
            acc = jnp.zeros((HEAD_DIM, size), F32)
            for b, s in enumerate(scores):
                e = jnp.exp(s - top)
                total += jnp.sum(e, axis=0, keepdims=True)
                acc += dot(vt_ref[b, h * HEAD_DIM : (h + 1) * HEAD_DIM, :], e.astype(BF))
            outs.append(acc / total)
            lse_ref[0, 0, pl.ds(2 * p + h, 1), :] = top + jnp.log(total)
        ctx_ref[slot] = jnp.concatenate(outs, axis=0).T.astype(BF)


def qkv_specs(nt, size):
    def spec(c):
        return pl.BlockSpec((None, nt, size, PAIR), lambda s, g, _: (c, 0, s, g))

    return [spec(c) for c in range(3)]


def attention_forward(qkv, start, slot_of, nt):
    _, _, rows, hc = qkv.shape
    seqs = start.shape[0]
    size = rows // seqs
    pairs = hc // PAIR
    blk = pl.BlockSpec((nt, size, PAIR), lambda s, g, _: (0, s, g))
    return call(
        functools.partial(attn_fwd_kernel, nt),
        (seqs, pairs),
        qkv_specs(nt, size) + [pl.BlockSpec((1, nt, size), lambda s, g, _: (s, 0, 0))],
        [blk, pl.BlockSpec((1, 1, 2 * nt, size), lambda s, g, _: (s, g, 0, 0))],
        [sds((nt, rows, hc), BF), sds((seqs, pairs, 2 * nt, size), F32)],
        scratch=[pltpu.VMEM((nt, PAIR, size), BF)],
        flops=seqs * pairs * 2 * 4 * (nt * size) ** 2 * 128,
        nbytes=8 * nt * rows * hc,
        prefetch=1,
    )(slot_of, qkv, qkv, qkv, start)


def attn_bwd_kernel(
    nt, slot_ref, q_ref, k_ref, v_ref, go_ref, start_ref, lse_ref, cos_ref, sin_ref,
    gq_ref, gk_ref, gv_ref, kt_ref, dk_ref, dv_ref,
):
    size = q_ref.shape[1]
    scale = HEAD_DIM**-0.5
    for b in range(nt):
        kt_ref[b] = k_ref[slot_ref[b]].T
    dk_ref[...] = jnp.zeros_like(dk_ref)
    dv_ref[...] = jnp.zeros_like(dv_ref)
    lane = lax.broadcasted_iota(jnp.int32, (size, PAIR), 1)
    for p in range(nt):
        slot = slot_ref[p]
        q = q_ref[slot] * BF(scale)
        go = go_ref[slot]
        start = start_ref[0, pl.ds(slot, 1), :]
        outs = []
        for h in range(2):
            mine = (lane >= HEAD_DIM) == (h == 1)
            qh = jnp.where(mine, q, BF(0))
            goh = jnp.where(mine, go, BF(0))
            lse = lse_ref[0, 0, pl.ds(2 * p + h, 1), :]
            probs, grads = [], []
            inner = jnp.zeros((1, size), F32)
            for b in range(p + 1):
                key_slot = slot_ref[b]
                s = dot_nt(k_ref[key_slot], qh)
                s = jnp.where(allowed_block(start, b, p, size), s, MASKED_SCORE)
                e = jnp.exp(s - lse)
                g = dot_nt(v_ref[key_slot], goh)
                inner += jnp.sum(e * g, axis=0, keepdims=True)
                probs.append(e)
                grads.append(g)
            dqt = jnp.zeros((HEAD_DIM, size), F32)
            for b in range(p + 1):
                ds = (probs[b] * (grads[b] - inner)).astype(BF)
                dv_ref[b] += dot(probs[b].astype(BF), goh)
                dk_ref[b] += dot(ds, qh)
                dqt += dot(kt_ref[b, h * HEAD_DIM : (h + 1) * HEAD_DIM, :], ds)
            outs.append(dqt)
        dq = jnp.concatenate(outs, axis=0).T * scale
        gq_ref[slot] = unrotate(dq, cos_ref[slot], sin_ref[slot]).astype(BF)
    for b in range(nt):
        slot = slot_ref[b]
        gk_ref[slot] = unrotate(dk_ref[b], cos_ref[slot], sin_ref[slot]).astype(BF)
        gv_ref[slot] = dv_ref[b].astype(BF)


def attention_backward(qkv, go, start, lse, cos, sin, slot_of, nt):
    _, _, rows, hc = qkv.shape
    seqs = start.shape[0]
    size = rows // seqs
    pairs = hc // PAIR
    blk = pl.BlockSpec((nt, size, PAIR), lambda s, g, _: (0, s, g))
    table = pl.BlockSpec((nt, size, PAIR), lambda s, g, _: (0, s, 0))
    return call(
        functools.partial(attn_bwd_kernel, nt),
        (seqs, pairs),
        qkv_specs(nt, size)
        + [
            blk,
            pl.BlockSpec((1, nt, size), lambda s, g, _: (s, 0, 0)),
            pl.BlockSpec((1, 1, 2 * nt, size), lambda s, g, _: (s, g, 0, 0)),
            table, table,
        ],
        [blk, blk, blk],
        [sds((nt, rows, hc), BF)] * 3,
        scratch=[
            pltpu.VMEM((nt, PAIR, size), BF),
            pltpu.VMEM((nt, size, PAIR), F32),
            pltpu.VMEM((nt, size, PAIR), F32),
        ],
        flops=seqs * pairs * 2 * 10 * (nt * size) ** 2 * 128,
        nbytes=14 * nt * rows * hc,
        prefetch=1,
    )(slot_of, qkv, qkv, qkv, go, start, lse, cos, sin)


def shard_group(nd, count):
    while nd % count or nd // count % 2:
        count //= 2
    return max(count, 1)


def cols_out_kernel(nt, steps, lhs_ref, w_ref, *outs):
    for slot in range(nt):
        lhs = lhs_ref[slot]
        parts = [dot(lhs, w_ref[j]) for j in range(w_ref.shape[0])]
        store_piece(outs, nt, slot, steps, jnp.concatenate(parts, axis=1))


def mm_cols(lhs, weight, nt, group):
    nd, depth, ds = weight.shape
    group = shard_group(nd, group)
    rows = lhs.shape[1]
    width = nd * ds
    shapes = flat(piece_shapes(nt, rows, width))
    outs = call(
        functools.partial(cols_out_kernel, nt, nd // group),
        (nd // group,),
        [whole_spec(lhs.shape), pl.BlockSpec((group, depth, ds), lambda j: (j, 0, 0))],
        out_piece_specs(nt, rows, width, group * ds),
        [sds(s, BF) for s in shapes],
        flops=2 * nt * rows * depth * width,
        nbytes=2 * (nt * rows * (depth + width) + depth * width),
    )(lhs, weight)
    return regroup(outs, nt)


def cols_back_kernel(nt, steps, nlhs, nseen, *refs):
    lhs, w_refs, outs = refs[:nlhs], refs[nlhs : 2 * nlhs], refs[2 * nlhs + nseen :]
    depth = w_refs[0].shape[3]
    weights = [w[:, 0].reshape(-1, depth) for w in w_refs]
    sums = None
    for slot in range(nt):
        total = dot_nt(lhs[0][slot], weights[0])
        for c in range(1, nlhs):
            total += dot_nt(lhs[c][slot], weights[c])
        if nseen:
            part = jnp.sum(total * refs[2 * nlhs][slot].astype(F32), axis=0, keepdims=True)
            sums = part if sums is None else sums + part
        store_piece(outs[: len(outs) - nseen], nt, slot, steps, total)
    if nseen:
        outs[-1][...] = sums


def mm_back(lhs, weight, channels, nt, group, seen=None):
    nd, _, ds, depth = weight.shape
    count = len(lhs)
    group = shard_group(nd, group)
    rows = lhs[0].shape[1]
    width = nd * ds
    shapes = flat(piece_shapes(nt, rows, width))
    step = group * ds
    more = [] if seen is None else [seen]

    def spec(c):
        return pl.BlockSpec((group, 1, ds, depth), lambda j: (j, c, 0, 0))

    outs = call(
        functools.partial(cols_back_kernel, nt, nd // group, count, len(more)),
        (nd // group,),
        [whole_spec(a.shape) for a in lhs]
        + [spec(c) for c in channels]
        + [pl.BlockSpec((nt, rows, step), lambda j: (0, 0, j)) for _ in more],
        out_piece_specs(nt, rows, width, step) + [pl.BlockSpec((1, step), lambda j: (0, j)) for _ in more],
        [sds(s, BF) for s in shapes] + [sds((1, width), F32) for _ in more],
        flops=2 * nt * rows * depth * width * count,
        nbytes=2 * (nt * rows * (depth * count + width) + depth * width * count),
    )(*lhs, *[weight] * count, *more)
    return regroup(outs[: len(shapes)], nt), outs[len(shapes) :]


def gateup_kernel(nt, *refs):
    count = len(flat(piece_shapes(nt, 8, 8)))
    pieces, w_ref, (full_ref, silu_ref, slope_ref, hid_ref) = (
        refs[:count],
        refs[count],
        refs[count + 1 :],
    )

    @pl.when(pl.program_id(0) == 0)
    def _():
        fill_from_pieces(pieces, full_ref, nt)

    cols = hid_ref.shape[2]
    w_gate = w_ref[:, 0].reshape(-1, cols)
    w_up = w_ref[:, 1].reshape(-1, cols)
    for slot in range(nt):
        a2 = full_ref[slot]
        gate = dot(a2, w_gate)
        up = dot(a2, w_up)
        sig = 0.5 + 0.5 * jnp.tanh(0.5 * gate)
        silu = gate * sig
        silu_ref[slot] = silu.astype(BF)
        slope_ref[slot] = (up * (sig + silu - silu * sig)).astype(BF)
        hid_ref[slot] = (silu * up).astype(BF)


def gate_up(pieces, weight, nt):
    nd, _, ds, ff = weight.shape
    rows, width = pieces[0][0].shape
    step = min(512, ff)
    blk = pl.BlockSpec((nt, rows, step), lambda j: (0, 0, j))
    return call(
        functools.partial(gateup_kernel, nt),
        (ff // step,),
        [whole_spec(a.shape) for a in flat(pieces)]
        + [pl.BlockSpec((nd, 2, ds, step), lambda j: (0, 0, 0, j))],
        [whole_spec((nt, rows, width)), blk, blk, blk],
        [sds((nt, rows, width), BF)] + [sds((nt, rows, ff), BF)] * 3,
        flops=4 * nt * rows * width * ff,
        nbytes=2 * (2 * nt * rows * width + 2 * width * ff + 3 * nt * rows * ff),
    )(*flat(pieces), weight)


def gate_back_kernel(nt, full_ref, w_ref, silu_ref, slope_ref, gg_ref, gu_ref):
    weight = jnp.concatenate([w_ref[j] for j in range(w_ref.shape[0])], axis=1)
    for slot in range(nt):
        gh = dot_nt(full_ref[slot], weight)
        gg_ref[slot] = (gh * slope_ref[slot].astype(F32)).astype(BF)
        gu_ref[slot] = (gh * silu_ref[slot].astype(F32)).astype(BF)


def gate_back(full, weight, silu, slope, nt):
    nd, ff, ds = weight.shape
    _, rows, width = full.shape
    step = min(512, ff)
    blk = pl.BlockSpec((nt, rows, step), lambda j: (0, 0, j))
    return call(
        functools.partial(gate_back_kernel, nt),
        (ff // step,),
        [whole_spec(full.shape), pl.BlockSpec((nd, step, ds), lambda j: (0, j, 0)), blk, blk],
        [blk, blk],
        [sds((nt, rows, ff), BF)] * 2,
        flops=2 * nt * rows * width * ff,
        nbytes=2 * (nt * rows * width + width * ff + 4 * nt * rows * ff),
    )(full, weight, silu, slope)


def context_back_kernel(nt, *refs):
    pieces, w_ref, (full_ref, out_ref) = refs[:-3], refs[-3], refs[-2:]

    @pl.when(pl.program_id(0) == 0)
    def _():
        fill_from_pieces(pieces, full_ref, nt)

    weight = w_ref[:, 0].reshape(-1, w_ref.shape[3])
    for slot in range(nt):
        out_ref[slot] = dot(full_ref[slot], weight).astype(BF)


def context_back(pieces, weight, channel, nt):
    nd, _, ds, hc = weight.shape
    rows, width = pieces[0][0].shape
    step = min(256, hc)
    return call(
        functools.partial(context_back_kernel, nt),
        (hc // step,),
        [whole_spec(a.shape) for a in flat(pieces)]
        + [pl.BlockSpec((nd, 1, ds, step), lambda j: (0, channel, 0, j))],
        [whole_spec((nt, rows, width)), pl.BlockSpec((nt, rows, step), lambda j: (0, 0, j))],
        [sds((nt, rows, width), BF), sds((nt, rows, hc), BF)],
        flops=2 * nt * rows * width * hc,
        nbytes=2 * (2 * nt * rows * width + width * hc + nt * rows * hc),
    )(*flat(pieces), weight)


def middle_kernel(nterms, x_ref, gain_ref, *refs):
    terms, (mid_ref, low_ref) = refs[:nterms], refs[nterms:]
    mid = x_ref[...].astype(F32) + sum_terms(terms)
    mid_ref[...] = mid
    scale = lax.rsqrt(jnp.mean(mid * mid, axis=-1, keepdims=True) + NORM_EPS)
    low_ref[...] = (mid * scale * gain_ref[...]).astype(BF)


def make_middle(x, gain, terms):
    rows, width = x.shape
    tile = min(128, rows)
    blk = pl.BlockSpec((tile, width), lambda i: (i, 0))
    return call(
        functools.partial(middle_kernel, len(terms)),
        (rows // tile,),
        [blk, whole_spec(gain.shape)] + [blk] * len(terms),
        [blk, blk],
        [sds((rows, width), F32), sds((rows, width), BF)],
        nbytes=rows * width * (8 + 2 * len(terms)),
    )(x, gain, *terms)


def sum_terms(terms):
    total = terms[0][...].astype(F32)
    for t in terms[1:]:
        total += t[...].astype(F32)
    return total


def layer_out_kernel(nterms, mid_ref, *refs):
    refs[-1][...] = (mid_ref[...] + sum_terms(refs[:nterms])).astype(BF)


def place(group, groups, rows, tile, width, into):
    steps = rows // tile
    spec = pl.BlockSpec((tile, width), lambda i: (i + group * steps, 0))
    return spec, sds((groups * rows, width), BF), [] if into is None else [into]


def layer_out_rows(mid, terms, group, groups, into):
    rows, width = mid.shape
    tile = min(128, rows)
    blk = pl.BlockSpec((tile, width), lambda i: (i, 0))
    spec, shape, old = place(group, groups, rows, tile, width, into)
    return call(
        functools.partial(layer_out_kernel, len(terms)),
        (rows // tile,),
        [blk] * (1 + len(terms)) + [HBM] * len(old),
        spec,
        shape,
        nbytes=rows * width * (6 + 2 * len(terms)),
        aliases={1 + len(terms): 0} if old else None,
    )(mid, *terms, *old)


def norm_back_kernel(nterms, nouts, first_ref, v_ref, gain_ref, *refs):
    terms, outs, sums = refs[:nterms], refs[len(refs) - nouts :], []
    if nouts == 3:
        outs, sums = outs[:2], outs[2:]
    u = sum_terms(terms)
    v = v_ref[...].astype(F32)
    q = lax.rsqrt(jnp.mean(v * v, axis=-1, keepdims=True) + NORM_EPS)
    ug = u * gain_ref[...]
    inner = jnp.mean(ug * v, axis=-1, keepdims=True)
    grad = first_ref[...].astype(F32) + (q * ug - v * (q * q * q * inner))
    for out in outs:
        out[...] = grad.astype(out.dtype)
    for sum_ref in sums:

        @pl.when(pl.program_id(0) == 0)
        def _():
            sum_ref[...] = jnp.zeros_like(sum_ref)

        sum_ref[...] += jnp.sum(u * v * q, axis=0, keepdims=True)


def norm_back(first, v, gain, terms):
    rows, width = v.shape
    tile = min(128, rows)
    blk = pl.BlockSpec((tile, width), lambda i: (i, 0))
    return call(
        functools.partial(norm_back_kernel, len(terms), 3),
        (rows // tile,),
        [blk, blk, whole_spec(gain.shape)] + [blk] * len(terms),
        [blk, blk, pl.BlockSpec((1, width), lambda i: (0, 0))],
        [sds((rows, width), F32), sds((rows, width), BF), sds((1, width), F32)],
        nbytes=rows * width * (12 + 2 * len(terms)),
    )(first, v, gain, *terms)


def norm_back_rows(first, v, gain, terms, group, groups, into):
    rows, width = v.shape
    tile = min(128, rows)
    blk = pl.BlockSpec((tile, width), lambda i: (i, 0))
    spec, shape, old = place(group, groups, rows, tile, width, into)
    return call(
        functools.partial(norm_back_kernel, len(terms), 1),
        (rows // tile,),
        [blk, blk, whole_spec(gain.shape)] + [blk] * len(terms) + [HBM] * len(old),
        spec,
        shape,
        nbytes=rows * width * (12 + 2 * len(terms)),
        aliases={3 + len(terms): 0} if old else None,
    )(first, v, gain, *terms, *old)


def wgrad_rows_kernel(groups, which, nmore, *refs):
    nlhs = groups * (max(which) + 1)
    lhs, rhs, out_ref = refs[:nlhs], refs[nlhs : nlhs + groups * len(which)], refs[-1]
    tile = lhs[0].shape[2]
    left = [a[...].reshape(-1, tile).T for a in lhs]
    for c, w in enumerate(which):
        total = None
        for g in range(groups):
            a = left[w * groups + g]
            term = dot(a, rhs[c * groups + g][...].reshape(a.shape[1], -1))
            total = term if total is None else total + term
        out_ref[0, c * tile : (c + 1) * tile] = total.astype(BF)
    if nmore:
        out_ref[0, len(which) * tile :] = refs[-2][0]


def wgrad_rows(lhs, rhs, which, nd, more=None):
    groups = len(lhs[0])
    nt, rows, width = lhs[0][0].shape
    ds = width // nd
    n = rhs[0][0].shape[2]
    more = [] if more is None else [more]
    height = len(rhs) * ds + sum(a.shape[1] for a in more)
    return call(
        functools.partial(wgrad_rows_kernel, groups, which, len(more)),
        (nd,),
        [pl.BlockSpec((nt, rows, ds), lambda j: (0, 0, j))] * (groups * len(lhs))
        + [whole_spec(a.shape) for r in rhs for a in r]
        + [pl.BlockSpec((1,) + a.shape[1:], lambda j: (j, 0, 0)) for a in more],
        pl.BlockSpec((1, height, n), lambda j: (j, 0, 0)),
        sds((nd, height, n), BF),
        flops=2 * groups * nt * rows * width * n * len(rhs),
        nbytes=2 * groups * nt * rows * (width + n * len(rhs)) + 2 * width * n * len(rhs),
    )(*[a for l in lhs for a in l], *[a for r in rhs for a in r], *more)


def wgrad_cols_kernel(groups, nd, *refs):
    lhs, rhs, out_ref = refs[:groups], refs[groups:-1], refs[-1]
    tile = lhs[0].shape[2]
    ds = out_ref.shape[2]
    left = [a[...].reshape(-1, tile).T for a in lhs]
    total = None
    for g in range(groups):
        term = dot(left[g], rhs[g][...].reshape(left[g].shape[1], -1))
        total = term if total is None else total + term
    for j in range(nd):
        out_ref[j] = total[:, j * ds : (j + 1) * ds].astype(BF)


def wgrad_cols(lhs, rhs, nd):
    groups = len(lhs)
    nt, rows, m = lhs[0].shape
    width = rhs[0].shape[2]
    tile = min(256, m)
    return call(
        functools.partial(wgrad_cols_kernel, groups, nd),
        (m // tile,),
        [pl.BlockSpec((nt, rows, tile), lambda i: (0, 0, i))] * groups
        + [whole_spec(a.shape) for a in rhs],
        pl.BlockSpec((nd, tile, width // nd), lambda i: (0, i, 0)),
        sds((nd, m, width // nd), BF),
        flops=2 * groups * nt * rows * width * m,
        nbytes=2 * groups * nt * rows * (width + m) + 2 * width * m,
    )(*lhs, *rhs)


def doc_starts(segments):
    row_len = segments.shape[-1]
    ids = jnp.arange(row_len, dtype=jnp.int32)
    change = jnp.concatenate(
        [jnp.ones_like(segments[:, :1], dtype=bool), segments[:, 1:] != segments[:, :-1]], axis=1
    )
    return lax.cummax(jnp.where(change, ids[None, :], 0), axis=1)


def sum_all(value, axis, count):
    bit = 1
    while bit < count:
        value = value + lax.ppermute(value, axis, swap_perm(count, bit))
        bit *= 2
    return value


def tensor_sum(value, nt):
    if nt != 4:
        return lax.psum(value, "tensor")
    value = value + lax.ppermute(value, "tensor", swap_perm(4, 1))
    return value + lax.ppermute(value, "tensor", swap_perm(4, 2))


def slot_order(blocks, index, nt):
    if nt != 4:
        return blocks
    pairs = jnp.stack([blocks[:, 1], blocks[:, 0], blocks[:, 3], blocks[:, 2]], axis=1)
    blocks = jnp.where(index % 2 == 1, pairs, blocks)
    halves = jnp.stack([blocks[:, 2], blocks[:, 3], blocks[:, 0], blocks[:, 1]], axis=1)
    return jnp.where(index // 2 == 1, halves, blocks)


def per_device(nd, nt, groups, layer_input, segments, qkv_w, out_w, gain1, gateup_w, down_w, gain2, grad_out):
    seqs, local, width = layer_input.shape
    per = seqs // groups
    index = lax.axis_index("tensor").astype(jnp.int32)
    blocks = jnp.arange(nt, dtype=jnp.int32)
    slot_of = blocks ^ index if nt == 4 else blocks

    x = [layer_input[g * per : (g + 1) * per].reshape(per * local, width) for g in range(groups)]
    go = [grad_out[g * per : (g + 1) * per].reshape(per * local, width) for g in range(groups)]
    Order.last = None
    x_all = Gather(layer_input.reshape(seqs * local, width), nt)

    gains = lax.all_gather(jnp.stack([gain1, gain2]), "dp", axis=1, tiled=True).astype(F32)
    g1, g2 = gains[:1], gains[1:]
    qkvo_w = jnp.concatenate([qkv_w, out_w.T[None]])
    full_qkvo = lax.all_gather(qkvo_w, "dp", axis=0, tiled=False)
    full_gateup = lax.all_gather(gateup_w, "dp", axis=0, tiled=False)
    full_down = lax.all_gather(down_w, "dp", axis=0, tiled=False)

    start_abs = doc_starts(segments)
    pos_abs = jnp.arange(segments.shape[1], dtype=jnp.int32)[None, :] - start_abs
    start_slot = slot_order(start_abs.reshape(seqs, nt, local), index, nt)
    pos_slot = slot_order(pos_abs.reshape(seqs, nt, local), index, nt)
    inv_freq = ROPE_BASE ** (-jnp.arange(HALF, dtype=F32) * 2.0 / HEAD_DIM)
    angles = pos_slot.astype(F32)[..., None] * inv_freq
    cos, sin = jnp.cos(angles), jnp.sin(angles)
    cos = jnp.concatenate([cos] * 4, axis=-1)
    sin = jnp.concatenate([-sin, sin] * 2, axis=-1)

    def table(t, g):
        t = t[g * per : (g + 1) * per]
        return jnp.swapaxes(t, 0, 1).reshape(nt, per * local, PAIR)

    coss = [table(cos, g) for g in range(groups)]
    sins = [table(sin, g) for g in range(groups)]
    starts = [start_slot[g * per : (g + 1) * per] for g in range(groups)]

    both = range(groups)
    qkv, ctx, lse, mid, low2, g_mid, g_low = ({} for _ in range(7))
    attn_sum, a2_all, ga2, out_sum, ga1 = ({} for _ in range(5))
    sum1, sum2, gm_all, gmf, g_qkv, g_ctx = ({} for _ in range(6))

    def dp_sum(grad):
        return lax.psum_scatter(grad, "dp", scatter_dimension=0, tiled=False)

    def project(g):
        qkv[g] = project_qkv(a1[g], full_qkvo, coss[g], sins[g], nt)

    def attend(g):
        ctx[g], lse[g] = attention_forward(qkv[g], starts[g], slot_of, nt)
        attn_sum[g] = Scatter(mm_back([ctx[g]], full_qkvo, [3], nt, 4)[0], nt)

    def middle(g):
        mid[g], low2[g] = make_middle(x[g], g2, attn_sum[g].terms)
        a2_all[g] = Gather(low2[g], nt)

    def second_back(g):
        ga2[g] = Scatter(mm_back([gg[g], gu[g]], full_gateup, [0, 1], nt, 2)[0], nt)

    def project_out(g):
        out_sum[g] = Scatter(mm_cols(hid[g], full_down, nt, 2), nt)

    def residual_back(g):
        g_mid[g], g_low[g], sum2[g] = norm_back(go[g], mid[g], g2, ga2[g].terms)
        gm_all[g] = Gather(g_low[g], nt)

    def attention_back_start(g):
        gmf[g], g_ctx[g] = context_back(gm_all[g].pieces, full_qkvo, 3, nt)

    def attention_back(g):
        g_qkv[g] = attention_backward(
            qkv[g], g_ctx[g], starts[g], lse[g], coss[g], sins[g], slot_of, nt
        )

    def input_back(g):
        parts, (sum1[g],) = mm_back(g_qkv[g], full_qkvo, [0, 1, 2], nt, 4, a1[g])
        ga1[g] = Scatter(parts, nt)

    def up_projection(g):
        a2[g], silu[g], slope[g], hid[g] = gate_up(a2_all[g].pieces, full_gateup, nt)

    def hidden_back(g):
        gg[g], gu[g] = gate_back(gof[g], full_down, silu[g], slope[g], nt)

    def finish(g, grad_input):
        return norm_back_rows(g_mid[g], x[g], g1, ga1[g].terms, g, groups, grad_input)

    def by_group(held):
        return [held[g] for g in both]

    def gather_cotangent(g):
        go_all[g] = Gather(link(go[g], flat(x_all.pieces)[-1]), nt)

    a2, silu, slope, hid, gg, gu, go_all, gof = ({} for _ in range(8))
    x_all.second()
    gather_cotangent(0)
    gather_cotangent(1)
    a1 = [assemble(x_all.pieces, nt, 0, groups, g1, coss + sins)]
    project(0)
    attend(0)
    go_all[0].second()
    a1.append(assemble(x_all.pieces, nt, 1, groups, g1))
    project(1)
    attn_sum[0].second()
    attend(1)
    middle(0)
    gof[0] = assemble(go_all[0].pieces, nt, 0, 1)
    attn_sum[1].second()
    a2_all[0].second()
    middle(1)
    go_all[1].second()
    up_projection(0)
    a2_all[1].second()
    gof[1] = assemble(go_all[1].pieces, nt, 0, 1)
    up_projection(1)
    hidden_back(0)
    grad_down = dp_sum(wgrad_cols(by_group(hid), by_group(gof), nd))
    second_back(0)
    hidden_back(1)
    ga2[0].second()
    grad_gateup = wgrad_rows([by_group(a2)], [by_group(gg), by_group(gu)], [0, 0], nd)
    residual_back(0)
    grad_gateup = dp_sum(link(grad_gateup, grad_down))
    second_back(1)
    gm_all[0].second()
    project_out(0)
    attention_back_start(0)
    ga2[1].second()
    attention_back(0)
    residual_back(1)
    input_back(0)
    project_out(1)
    gm_all[1].second()
    out_sum[0].second()
    attention_back_start(1)
    attention_back(1)
    layer_out = layer_out_rows(mid[0], out_sum[0].terms, 0, groups, None)
    grad_qkvo = wgrad_rows(
        [a1, by_group(gmf)],
        [[g_qkv[g][c] for g in both] for c in range(3)] + [by_group(ctx)],
        [0, 0, 0, 1],
        nd,
    )
    grad_qkvo = dp_sum(link(grad_qkvo, grad_gateup))
    input_back(1)
    ga1[0].second()
    out_sum[1].second()
    ga1[1].second()
    grad_input = finish(0, None)
    layer_out = layer_out_rows(mid[1], out_sum[1].terms, 1, groups, layer_out)
    gains = jnp.concatenate([(sum1[0] + sum1[1]) / g1, sum2[0] + sum2[1]])
    gains = link(gains, Order.last)
    grad_input = finish(1, grad_input)
    ds = gain1.shape[0]
    gains = lax.psum(gains, "dp") if nd & (nd - 1) else sum_all(gains, "dp", nd)
    gains = tensor_sum(gains, nt)
    gains = lax.dynamic_slice_in_dim(gains, lax.axis_index("dp") * ds, ds, 1)
    return (
        layer_out.reshape(seqs, local, width),
        grad_input.reshape(seqs, local, width),
        grad_qkvo[: 3 * ds].astype(F32).reshape(3, ds, -1),
        grad_qkvo[3 * ds : 4 * ds].T.astype(F32),
        gains[0],
        grad_gateup.astype(F32).reshape(2, ds, -1),
        grad_down.astype(F32),
        gains[1],
    )


def solution(mesh):
    nd, nt = mesh.shape["dp"], mesh.shape["tensor"]
    return jax.shard_map(
        functools.partial(per_device, nd, nt, 2),
        mesh=mesh,
        in_specs=(
            P("dp", "tensor", None),
            P("dp", None),
            P(None, "dp", "tensor"),
            P("tensor", "dp"),
            P("dp"),
            P(None, "dp", "tensor"),
            P("tensor", "dp"),
            P("dp"),
            P("dp", "tensor", None),
        ),
        out_specs=(
            P("dp", "tensor", None),
            P("dp", "tensor", None),
            P(None, "dp", "tensor"),
            P("tensor", "dp"),
            P("dp"),
            P(None, "dp", "tensor"),
            P("tensor", "dp"),
            P("dp"),
        ),
        check_vma=False,
    )
```
